512 devices in a mesh: group: 8 (over x, core), leaf: 64 (over y, z).
Axes of the slice: x: 4, y: 8, z: 8, core: 2. Of those that a mesh axis runs over, the one named last changes fastest.
Arguments:
- points: float32 [4096, 3, 256], P(('group', 'leaf')), may hold values from 0 to 3
- charges: float32 [4096, 8, 256], P(('group', 'leaf')), may hold values from -0.4 to 0.4
- up_op: float32 [4096, 128, 256], P(('group', 'leaf')), may hold values from -0.375 to 0.375
- skel_pts: float32 [4096, 3, 128], P(('group', 'leaf')), may hold values from 0 to 3
- upward_transfer_matrix: float32 [4096, 128, 128], P(('group', 'leaf')), may hold values from -0.1875 to 0.1875
- cell_pts: float32 [512, 3, 128], P(('group', 'leaf')), may hold values from 0 to 3
- near_list: int32 [4096, 9], P(('group', 'leaf')), may hold values from -1 to 4095, as said below
- leaf_list: int32 [4096, 16], P(('group', 'leaf')), may hold values from 0 to 4095, as said below
- top_list: int32 [512, 16], P(('group', 'leaf')), may hold values from 0 to 511, as said below
Outputs:
- potential: float32 [4096, 8, 256], P(('group', 'leaf'))
The draws below stay inside these ranges and needn't reach their ends.
Inputs may be any that keep to these rules, and one draw needn't show every extreme that they name: `near_list`: row i starts with i itself; its other entries are distinct leaves i + o with 0 < |o| <= 4 inside 0 to 4095, or -1 for padding; the number of live entries varies by leaf, and the first leaf of each device lists every such neighbour that lies inside 0 to 4095. `leaf_list`: entries of a row are distinct leaves of the same subtree of 512 leaves, none within 4 of the row's leaf in the subtree's cyclic order. `top_list`: entries of a row are distinct cells of other subtrees.
All inputs are finite; a program needn't handle non-finite values.
Results may differ from the reference program's by a relative error of at most 0.0003.
Values sent between devices are 32-bit elements; how exact they have to be, the bound alone decides.
No kernel may reach another device: no remote copies, remote signals or barrier semaphores. Data moves between devices by JAX's collectives and lax.ppermute only.
A program may use at most 64 MiB of HBM per device.

```python
import jax
import jax.numpy as jnp
from jax import lax

LEAF_PTS = 256
RANK = 128
PROBES = 8
LEAVES_DEV = 8
WINDOW = 4
ILEAF = 16
ITOP = 16
NBR = 9
GROUP_LEAVES = 512
CELLS = 512
LEAVES = 4096
N_LEAF = 64


def draw_near_list(key, part):
    key = jax.random.fold_in(key, 11)
    pool = jnp.concatenate([jnp.arange(-WINDOW, 0), jnp.arange(1, WINDOW + 1)]).astype(jnp.int32)
    row_keys = jax.random.split(jax.random.fold_in(key, 1), LEAVES)
    orders = jax.vmap(lambda k: jax.random.permutation(k, 2 * WINDOW))(row_keys)
    counts = jax.random.randint(jax.random.fold_in(key, 2), (LEAVES,), 1, NBR + 1)
    index = jnp.arange(LEAVES, dtype=jnp.int32)
    counts = jnp.where(index % LEAVES_DEV == 0, NBR, counts)
    counts = jnp.where(index % LEAVES_DEV == 1, (NBR + 1) // 2, counts)
    offsets = jnp.concatenate([jnp.zeros((LEAVES, 1), jnp.int32), pool[orders].astype(jnp.int32)], axis=1)
    ids = index[:, None] + offsets
    live = (jnp.arange(NBR)[None, :] < counts[:, None]) & (ids >= 0) & (ids < LEAVES)
    return jnp.where(live, ids, -1).astype(jnp.int32)


def draw_leaf_list(key, part):
    key = jax.random.fold_in(key, 12)
    row_keys = jax.random.split(key, LEAVES)
    orders = jax.vmap(lambda k: jax.random.permutation(k, GROUP_LEAVES - NBR))(row_keys)[:, :ILEAF]
    index = jnp.arange(LEAVES, dtype=jnp.int32)
    inside = index % GROUP_LEAVES
    start = index - inside
    ids = start[:, None] + (inside[:, None] + WINDOW + 1 + orders) % GROUP_LEAVES
    return ids.astype(jnp.int32)


def draw_top_list(key, part):
    key = jax.random.fold_in(key, 13)
    row_keys = jax.random.split(key, CELLS)
    orders = jax.vmap(lambda k: jax.random.permutation(k, CELLS - N_LEAF))(row_keys)[:, :ITOP]
    index = jnp.arange(CELLS, dtype=jnp.int32)
    start = index // N_LEAF * N_LEAF
    ids = (start[:, None] + N_LEAF + orders) % CELLS
    return ids.astype(jnp.int32)


def block_scale(own_key, extent, shards, low, largest):
    factor_of = 1.0
    for dim, shards_of in shards:
        steps = jax.random.uniform(jax.random.fold_in(jax.random.fold_in(own_key, 6), dim), (shards_of,), jnp.float32, low / len(shards), largest / len(shards))
        factor_of = factor_of * jnp.repeat(jnp.exp(steps), extent[dim] // shards_of).reshape((-1,) + (1,) * (len(extent) - 1 - dim))
    return factor_of


def scatter_about(stream_key, shape, width, limit, cuts=(), kind=jnp.bfloat16):
    loudness = block_scale(stream_key, shape, cuts, -0.22, 0.18) if cuts else 1.0
    array = jax.random.normal(stream_key, shape, jnp.float32) * width * loudness
    return jnp.minimum(jnp.maximum(array, -limit), limit).astype(kind)


def setup_inputs(seed: int = 0) -> dict:
    key_list = jax.random.split(jax.random.key(seed), 10)
    points = jnp.clip(3.0 * jax.random.uniform(key_list[0], (LEAVES, 3, LEAF_PTS), jnp.float32) ** block_scale(key_list[0], (LEAVES, 3, LEAF_PTS), ((0, 512),), -0.2, 0.2), 0.0, 3.0)
    charges = scatter_about(key_list[1], (LEAVES, PROBES, LEAF_PTS), 0.05, 0.4, ((0, 512),), jnp.float32)
    up_op = scatter_about(key_list[2], (LEAVES, RANK, LEAF_PTS), LEAF_PTS ** -0.5, 0.375, ((0, 512),), jnp.float32)
    skel_pts = jnp.clip(3.0 * jax.random.uniform(key_list[3], (LEAVES, 3, RANK), jnp.float32) ** block_scale(key_list[3], (LEAVES, 3, RANK), ((0, 512),), -0.2, 0.2), 0.0, 3.0)
    upward_transfer_matrix = scatter_about(key_list[4], (LEAVES, RANK, RANK), (RANK * LEAVES_DEV) ** -0.5, 0.1875, ((0, 512),), jnp.float32)
    cell_pts = jnp.clip(3.0 * jax.random.uniform(key_list[5], (CELLS, 3, RANK), jnp.float32) ** block_scale(key_list[5], (CELLS, 3, RANK), ((0, 512),), -0.2, 0.2), 0.0, 3.0)
    near_list = draw_near_list(jax.random.fold_in(key_list[9], 71), 0)
    leaf_list = draw_leaf_list(jax.random.fold_in(key_list[9], 71), 0)
    top_list = draw_top_list(jax.random.fold_in(key_list[9], 71), 0)
    return {"points": points, "charges": charges, "up_op": up_op, "skel_pts": skel_pts, "upward_transfer_matrix": upward_transfer_matrix, "cell_pts": cell_pts, "near_list": near_list, "leaf_list": leaf_list, "top_list": top_list}


root_three = 1.7320508075688772
finest_level = lax.Precision.HIGHEST

def matern(left_pts, right_pts):
    square = None
    for comp in range(3):
        diff = left_pts[..., comp, :, None] - right_pts[..., comp, None, :]
        square = diff * diff if square is None else square + diff * diff
    scaled = root_three * jnp.sqrt(square)
    return (1.0 + scaled) * jnp.exp(-scaled)

def reference(points, charges, up_op, skel_pts, upward_transfer_matrix, cell_pts, near_list, leaf_list, top_list):
    total_leaves = points.shape[0]
    cells = cell_pts.shape[0]
    per_cell = total_leaves // cells
    source_weights = jnp.einsum('lrb,lpb->lpr', up_op, charges, precision=finest_level)

    def near_block(blocks):
        block_pts, block_list = blocks
        total = jnp.zeros((per_cell, charges.shape[1], points.shape[2]), jnp.float32)
        for slot in range(block_list.shape[1]):
            ids = block_list[:, slot]
            safe = jnp.maximum(ids, 0).astype(jnp.int32)
            kernel = matern(block_pts, points[safe])
            term = jnp.einsum('lab,lpb->lpa', kernel, charges[safe], precision=finest_level)
            total = total + jnp.where((ids >= 0)[:, None, None], term, 0.0)
        return total
    near = lax.map(near_block, (points.reshape(cells, per_cell, 3, -1), near_list.reshape(cells, per_cell, -1)))
    near = near.reshape(charges.shape)

    def leaf_block(blocks):
        block_skel, block_list = blocks
        total = jnp.zeros((per_cell, charges.shape[1], skel_pts.shape[2]), jnp.float32)
        for slot in range(block_list.shape[1]):
            ids = block_list[:, slot]
            kernel = matern(block_skel, skel_pts[ids])
            total = total + jnp.einsum('lab,lpb->lpa', kernel, source_weights[ids], precision=finest_level)
        return total
    leaf_distant_field = lax.map(leaf_block, (skel_pts.reshape(cells, per_cell, 3, -1), leaf_list.reshape(cells, per_cell, -1)))
    leaf_distant_field = leaf_distant_field.reshape(source_weights.shape)
    cell_skeleton_weights = jnp.einsum('kjo,keo->kej', upward_transfer_matrix, source_weights, precision=finest_level)
    cell_skeleton_weights = cell_skeleton_weights.reshape(cells, per_cell, source_weights.shape[1], -1).sum(1)

    def cell_block(blocks):
        own_pts, ids = blocks
        kernel = matern(own_pts, cell_pts[ids])
        return jnp.einsum('tab,tpb->pa', kernel, cell_skeleton_weights[ids], precision=finest_level)
    cell_distant_field = lax.map(cell_block, (cell_pts, top_list))
    parent_cell_index = jnp.repeat(cell_distant_field, per_cell, axis=0)
    received_field = leaf_distant_field + jnp.einsum('jdm,jud->jum', upward_transfer_matrix, parent_cell_index, precision=finest_level)
    return near + jnp.einsum('lrb,lpr->lpb', up_op, received_field, precision=finest_level)
```

```python
import functools
import math

import jax
import jax.numpy as jnp
from jax import lax
from jax.experimental import pallas as pl
from jax.experimental.pallas import tpu as pltpu
from jax.sharding import Mesh, PartitionSpec as P

F32 = jnp.float32
BF16 = jnp.bfloat16
KAPPA = math.sqrt(3.0) * math.log2(math.e)
LN2 = math.log(2.0)
CENTER = 1.5
FEAT = 32
REACH = 4
OWN = 8
NBR = 9
UNROLL = 8
EXACT = lax.Precision.HIGHEST

SMEM = pl.BlockSpec(memory_space=pltpu.SMEM)
VMEM = pl.BlockSpec(memory_space=pltpu.VMEM)


def split3(x):
    a = x.astype(BF16)
    r = x - a.astype(F32)
    b = r.astype(BF16)
    c = (r - b.astype(F32)).astype(BF16)
    return a.astype(F32), b.astype(F32), c.astype(F32)


def features(pts):
    x = (pts - CENTER) * KAPPA
    n = jnp.sum(x * x, axis=0, keepdims=True)
    x1, x2, x3 = split3(x)
    n1, n2, n3 = split3(n)
    one = jnp.ones_like(n)
    pad = jnp.zeros((FEAT - 24, pts.shape[1]), F32)
    src = jnp.concatenate([x1, x1, x2, x2, x1, x3, n1, n2, n3, one, one, one, pad], 0)
    tgt = jnp.concatenate([-2 * x1, -2 * x2, -2 * x1, -2 * x2, -2 * x3, -2 * x1, one, one, one, n1, n2, n3, pad], 0)
    return src, tgt


def two_halves(vals):
    v = vals * LN2
    high = v.astype(BF16).astype(F32)
    return jnp.concatenate([high, v - high], 0).astype(BF16)


def matern_over_ln2(t):
    m = jnp.maximum(t, 1e-12)
    s = m * lax.rsqrt(m)
    return (s + 1.0 / LN2) * jnp.exp2(-s)


def product(src_feat, tgt_feat, vals):
    t = jnp.dot(src_feat, tgt_feat, preferred_element_type=F32)
    k = matern_over_ln2(t)
    high = k.astype(BF16)
    low = (k - high.astype(F32)).astype(BF16)
    out = jnp.dot(vals, high, preferred_element_type=F32) + jnp.dot(vals, low, preferred_element_type=F32)
    return out


def nt(a, b):
    return lax.dot_general(a, b, (((1,), (1,)), ((), ())), precision=EXACT, preferred_element_type=F32)


def pack_kernel(pts, chg, up, skel, utm, cpts, llist, tlist, m1, m0, first, last):
    f32 = F32
    for l in range(OWN):
        w = nt(chg[l], up[l])
        cw = nt(w, utm[l])
        total = cw if l == 0 else total + cw
        for d in range(8):
            m1[d, 8 * l : 8 * l + 8, :] = w
            m1[d, 64 + 3 * l : 67 + 3 * l, :] = skel[l]
            m0[d, 3 * l : 3 * l + 3, :] = skel[l]
    for d in range(8):
        m1[d, 88:96, :] = total
        m1[d, 96:99, :] = cpts[0]
        m1[d, 99:104, :] = jnp.zeros((5, 128), f32)
        m0[d, 24:27, :] = cpts[0]
        m0[d, 29:32, :] = jnp.zeros((3, 128), f32)
    for slab, start in ((first, 0), (last, OWN - REACH)):
        for i in range(REACH):
            slab[8 * i : 8 * i + 8, :] = chg[start + i]
            slab[32 + 3 * i : 35 + 3 * i, :] = pts[start + i]
        slab[44:48, :] = jnp.zeros((4, 256), f32)
    lane = lax.broadcasted_iota(jnp.int32, (1, 128), 1)
    sub8 = lax.broadcasted_iota(jnp.int32, (8, 128), 0)
    row = lax.broadcasted_iota(jnp.int32, (128, 128), 0)
    col = lax.broadcasted_iota(jnp.int32, (128, 128), 1)
    before = (row < col).astype(f32).astype(BF16)
    ll = llist[...]
    tl = tlist[...]
    leaf_hit = ((ll >> 3) & 7) == sub8
    top_hit = ((tl & 7) == sub8) & (lane < 16)
    leaf_one = leaf_hit.astype(f32)
    top_one = top_hit.astype(f32)
    leaf_pos = jnp.dot(leaf_one.astype(BF16), before, preferred_element_type=f32)
    top_pos = jnp.dot(top_one.astype(BF16), before, preferred_element_type=f32) + 16.0
    leaf_n = jnp.sum(leaf_one, axis=1, keepdims=True)
    top_n = jnp.sum(top_one, axis=1, keepdims=True)
    leaf_pos = jnp.where(leaf_hit, leaf_pos, -1.0)
    top_pos = jnp.where(top_hit, top_pos, -1.0)
    local = (ll & 7) + ((ll >> 6) & 7) * 8
    codes = jnp.where(sub8 == 0, lane >> 4, jnp.where(sub8 == 1, local, 0)).astype(f32).astype(BF16)
    tcodes = jnp.where(sub8 == 0, tl >> 3, 0).astype(f32).astype(BF16)
    rowf = row.astype(f32)
    for d in range(8):
        oh = (leaf_pos[d : d + 1] == rowf).astype(f32).astype(BF16)
        got = lax.dot_general(codes, oh, (((1,), (1,)), ((), ())), preferred_element_type=f32)
        m0[d, 27:28, :] = got[0:1] * 64.0 + got[1:2]
        oh = (top_pos[d : d + 1] == rowf).astype(f32).astype(BF16)
        got = lax.dot_general(tcodes, oh, (((1,), (1,)), ((), ())), preferred_element_type=f32)[0:1]
        got = got + jnp.where(lane == 0, leaf_n[d : d + 1], 0.0) + jnp.where(lane == 1, top_n[d : d + 1], 0.0)
        m0[d, 28:29, :] = got


def pack(pts, chg, up, skel, utm, cpts, llist, tlist):
    sd = jax.ShapeDtypeStruct
    return pl.pallas_call(
        pack_kernel,
        in_specs=[VMEM] * 8,
        out_specs=[VMEM] * 4,
        out_shape=[sd((8, 104, 128), F32), sd((8, 32, 128), F32), sd((48, 256), F32), sd((48, 256), F32)],
        compiler_params=pltpu.CompilerParams(vmem_limit_bytes=32 << 20),
        name="pack",
    )(pts, chg, up, skel, utm, cpts, llist, tlist)


def near_kernel(lo, hi, ids, pts, chg, before, after, out, fs, ft, vals):
    me = (lax.axis_index("g") * lax.axis_size("y") + lax.axis_index("y")) * lax.axis_size("z") + lax.axis_index("z")
    base = me * OWN - REACH
    for e in range(lo, hi + 2 * REACH):
        if e < REACH:
            p, c = before[32 + 3 * e : 35 + 3 * e, :], before[8 * e : 8 * e + 8, :]
        elif e < REACH + OWN:
            p, c = pts[e - REACH], chg[e - REACH]
        else:
            i = e - REACH - OWN
            p, c = after[32 + 3 * i : 35 + 3 * i, :], after[8 * i : 8 * i + 8, :]
        src, tgt = features(p)
        fs[e - lo] = src.T.astype(BF16)
        if lo <= e - REACH < hi:
            ft[e - REACH - lo] = tgt.astype(BF16)
        vals[e - lo] = two_halves(c)
    dead = hi - lo + 2 * REACH
    vals[dead] = jnp.zeros((16, 256), BF16)

    def leaf(i, carry):
        tgt = ft[i]
        acc = jnp.zeros((16, 256), F32)
        for n in range(NBR):
            ident = ids[i + lo, n]
            live = ident >= 0
            e = jnp.where(live, ident - base - lo, 0)
            acc = acc + product(fs[e], tgt, vals[jnp.where(live, e, dead)])
        out[i] = acc[0:8] + acc[8:16]
        return carry

    lax.fori_loop(0, hi - lo, leaf, 0)


def near_part(lo, hi, ids, pts, chg, before, after):
    n = hi - lo
    return pl.pallas_call(
        functools.partial(near_kernel, lo, hi),
        in_specs=[SMEM] + [VMEM] * 4,
        out_specs=VMEM,
        out_shape=jax.ShapeDtypeStruct((n, 8, 256), F32),
        scratch_shapes=[
            pltpu.VMEM((n + 8, 256, FEAT), BF16),
            pltpu.VMEM((n, FEAT, 256), BF16),
            pltpu.VMEM((n + 9, 16, 256), BF16),
        ],
        cost_estimate=pl.CostEstimate(flops=n * 9 * 256 * 256 * 1000, bytes_accessed=300000, transcendentals=n * 9 * 65536 * 2),
        compiler_params=pltpu.CompilerParams(vmem_limit_bytes=32 << 20),
        name="near",
    )(ids, pts, chg, before, after)


def far_leaf_kernel(req, src, tgt, out, fs, ft, vals):
    for y in range(8):
        for l in range(OWN):
            i = 8 * y + l
            f, _ = features(src[y, 64 + 3 * l : 67 + 3 * l, :])
            fs[i] = f.T.astype(BF16)
            vals[i] = two_halves(src[y, 8 * l : 8 * l + 8, :])
            _, f = features(tgt[y, 3 * l : 3 * l + 3, :])
            ft[i] = f.astype(BF16)
    vals[64] = jnp.zeros((16, 128), BF16)
    out[...] = jnp.zeros_like(out)

    def of_device(d, carry):
        n = req[d, 1, 0]

        def chunk(i, c):
            for u in range(UNROLL):
                at = i * UNROLL + u
                code = req[d, 0, at]
                t = code >> 6
                s = code & 63
                r = product(fs[s], ft[d * 8 + t], vals[jnp.where(at < n, s, 64)])
                out[d, t] += r[0:8] + r[8:16]
            return c

        lax.fori_loop(0, (n + UNROLL - 1) // UNROLL, chunk, 0)
        return carry

    lax.fori_loop(0, 8, of_device, 0)


def far_leaf(req, src, tgt):
    return pl.pallas_call(
        far_leaf_kernel,
        in_specs=[SMEM, VMEM, VMEM],
        out_specs=VMEM,
        out_shape=jax.ShapeDtypeStruct((8, 9, 8, 128), F32),
        scratch_shapes=[
            pltpu.VMEM((64, 128, FEAT), BF16),
            pltpu.VMEM((64, FEAT, 128), BF16),
            pltpu.VMEM((65, 16, 128), BF16),
        ],
        cost_estimate=pl.CostEstimate(flops=128 * 128 * 128 * 1000, bytes_accessed=900000, transcendentals=128 * 16384 * 2),
        compiler_params=pltpu.CompilerParams(vmem_limit_bytes=32 << 20),
        name="far_leaf",
    )(req, src, tgt)


def far_top_kernel(req, src, tgt, part, out, fs, vals):
    for g in range(8):
        for y in range(8):
            i = 8 * g + y
            f, _ = features(src[g, 16 * y + 8 : 16 * y + 11, :])
            fs[i] = f.T.astype(BF16)
            vals[i] = two_halves(src[g, 16 * y : 16 * y + 8, :])
    out[...] = part[...]

    def of_device(d, carry):
        n = req[d, 1, 1]
        _, f = features(tgt[d, 24:27, :])
        ft = f.astype(BF16)

        def one(i, acc):
            s = req[d, 1, 16 + i]
            return acc + product(fs[s], ft, vals[s])

        acc = lax.fori_loop(0, n, one, jnp.zeros((16, 128), F32))
        out[d, 8] = acc[0:8] + acc[8:16]
        return carry

    lax.fori_loop(0, 8, of_device, 0)


def far_top(req, src, tgt, part):
    return pl.pallas_call(
        far_top_kernel,
        in_specs=[SMEM, VMEM, VMEM, VMEM],
        out_specs=VMEM,
        out_shape=jax.ShapeDtypeStruct((8, 9, 8, 128), F32),
        scratch_shapes=[pltpu.VMEM((64, 128, FEAT), BF16), pltpu.VMEM((64, 16, 128), BF16)],
        compiler_params=pltpu.CompilerParams(vmem_limit_bytes=32 << 20),
        name="far_top",
    )(req, src, tgt, part)


def final_kernel(got, utm, up, near1, near2, out):
    tot = got[0]
    for d in range(1, 8):
        tot = tot + got[d]
    cell = tot[8]
    for l in range(OWN):
        incoming = tot[l] + jnp.dot(cell, utm[l], precision=EXACT, preferred_element_type=F32)
        near = near1[l] if l < OWN // 2 else near2[l - OWN // 2]
        out[l] = near + jnp.dot(incoming, up[l], precision=EXACT, preferred_element_type=F32)


def final(got, utm, up, near1, near2):
    return pl.pallas_call(
        final_kernel,
        in_specs=[VMEM] * 5,
        out_specs=VMEM,
        out_shape=jax.ShapeDtypeStruct((8, 8, 256), F32),
        compiler_params=pltpu.CompilerParams(vmem_limit_bytes=32 << 20),
        name="final",
    )(got, utm, up, near1, near2)


def body(points, charges, up_op, skel_pts, utm, cell_pts, near_list, leaf_list, top_list):
    every = ("g", "y", "z")
    llist = leaf_list.reshape(1, 128)
    tlist = jnp.pad(top_list, ((0, 0), (0, 112)), constant_values=0)
    m1, m0, first, last = pack(points, charges, up_op, skel_pts, utm, cell_pts, llist, tlist)
    count = lax.axis_size("g") * lax.axis_size("y") * lax.axis_size("z")
    up = [(i, i + 1) for i in range(count - 1)]
    down = [(i + 1, i) for i in range(count - 1)]
    got1 = lax.all_to_all(m1, "y", 0, 0, tiled=True)
    got0 = lax.all_to_all(m0, "z", 0, 0, tiled=True)
    before = lax.ppermute(last, every, up)
    after = lax.ppermute(first, every, down)
    near1 = near_part(0, 4, near_list, points, charges, before, after)
    got1, near1 = lax.optimization_barrier((got1, near1))
    cells = jnp.broadcast_to(got1[:, 88:104, :].reshape(1, 128, 128), (8, 128, 128))
    gotg = lax.all_to_all(cells, "g", 0, 0, tiled=True)
    req = got0[:, 27:29, :].astype(jnp.int32)
    part = far_leaf(req, got1, got0)
    part = far_top(req, gotg, got0, part)
    part, charges2 = lax.optimization_barrier((part, charges))
    gotr = lax.all_to_all(part, "z", 0, 0, tiled=True)
    near2 = near_part(4, 8, near_list, points, charges2, before, after)
    return final(gotr, utm, up_op, near1, near2)


def solution(mesh):
    fine = Mesh(mesh.devices.reshape(mesh.shape["group"], 8, 8), ("g", "y", "z"))
    row = ("g", "y", "z")
    specs = tuple(P(row, *([None] * k)) for k in (2, 2, 2, 2, 2, 2, 1, 1, 1))
    return jax.shard_map(body, mesh=fine, in_specs=specs, out_specs=P(row, None, None), check_vma=False)
```

```python
import functools
import math

import jax
import jax.numpy as jnp
from jax import lax
from jax.experimental import pallas as pl
from jax.experimental.pallas import tpu as pltpu
from jax.sharding import Mesh, PartitionSpec as P

F32 = jnp.float32
BF16 = jnp.bfloat16
KAPPA = math.sqrt(3.0) * math.log2(math.e)
LN2 = math.log(2.0)
CENTER = 1.5
FEAT = 32
REACH = 4
OWN = 8
NBR = 9
PAIRS = 8
DUMMY = 64
EXACT = lax.Precision.HIGHEST

SMEM = pl.BlockSpec(memory_space=pltpu.SMEM)
VMEM = pl.BlockSpec(memory_space=pltpu.VMEM)
PARAMS = pltpu.CompilerParams(vmem_limit_bytes=40 << 20)


def split2(x):
    a = x.astype(BF16).astype(F32)
    return a, (x - a).astype(BF16).astype(F32)


def split3(x):
    a = x.astype(BF16).astype(F32)
    b, c = split2(x - a)
    return a, b, c


def dense_features(xyz):
    parts = [split2((x - CENTER) * KAPPA) for x in xyz]
    n = None
    for a, b in parts:
        r = a + b
        n = r * r if n is None else n + r * r
    n1, n2, n3 = split3(n)
    one = jnp.ones_like(n)
    zero = jnp.zeros_like(n)
    high = [a for a, _ in parts]
    low = [b for _, b in parts]
    high2 = [-2.0 * a for a in high]
    low2 = [-2.0 * b for b in low]
    s0 = high + [n1, n2, n3, one, one]
    s1 = low + [one, zero, zero, zero, zero]
    t0 = high2 + [one, one, one, n1, n2]
    t1 = low2 + [zero] * 5
    t2 = high2 + [n3] + [zero] * 4
    return s0, s1, t0, t1, t2


def spread(rows, tmp):
    n, width = rows[0].shape
    halves = width // 128
    for r, v in enumerate(rows):
        for h in range(halves):
            tmp[h, n * r : n * r + n, :] = v[:, 128 * h : 128 * h + 128]

    def load(leaf):
        return jnp.concatenate([tmp[h, pl.ds(leaf, 8, stride=n), :] for h in range(halves)], 1)

    return load


def two_halves(vals):
    v = vals * LN2
    high = v.astype(BF16).astype(F32)
    return jnp.concatenate([high, v - high], 0).astype(BF16)


def matern_over_ln2(t):
    m = jnp.maximum(t, 1e-12)
    s = m * lax.rsqrt(m)
    return (s + 1.0 / LN2) * jnp.exp2(-s)


def product(src_feat, tgt_feat, vals):
    t = jnp.dot(src_feat, tgt_feat, preferred_element_type=F32)
    k = matern_over_ln2(t)
    high = k.astype(BF16)
    low = (k - high.astype(F32)).astype(BF16)
    return jnp.dot(vals, high, preferred_element_type=F32) + jnp.dot(vals, low, preferred_element_type=F32)


def nt(a, b):
    return lax.dot_general(a, b, (((1,), (1,)), ((), ())), precision=EXACT, preferred_element_type=F32)


def request_kernel(pts, chg, skel, cpts, llist, tlist, m0, first, last, row16):
    lane = lax.broadcasted_iota(jnp.int32, (1, 128), 1)
    sub8 = lax.broadcasted_iota(jnp.int32, (8, 128), 0)
    lane8 = lax.broadcasted_iota(jnp.int32, (8, 128), 1)
    row = lax.broadcasted_iota(jnp.int32, (128, 128), 0)
    col = lax.broadcasted_iota(jnp.int32, (128, 128), 1)
    before = (row < col).astype(F32).astype(BF16)
    pick = (lax.broadcasted_iota(jnp.int32, (16, 128), 0) == (lax.broadcasted_iota(jnp.int32, (16, 128), 1) & 15))
    pick = pick.astype(F32).astype(BF16)
    ll = llist[...]
    mine = sub8 == (lane8 >> 4)

    def flat(v):
        w = jnp.dot(v.astype(F32).astype(BF16), pick, preferred_element_type=F32)
        return jnp.sum(jnp.where(mine, w, 0.0), axis=0, keepdims=True).astype(jnp.int32)

    upper = flat(ll >> 6)
    lower = flat(ll & 63)
    row16[...] = jnp.zeros((8, 128), jnp.int32)
    row16[0:1, 0:16] = tlist[...]
    tl = row16[0:1, :]
    leaf_hit = (lower >> 3) == sub8
    top_hit = ((tl & 7) == sub8) & (lane < 16)
    leaf_one = leaf_hit.astype(F32)
    top_one = top_hit.astype(F32)
    leaf_pos = jnp.dot(leaf_one.astype(BF16), before, preferred_element_type=F32)
    top_pos = jnp.dot(top_one.astype(BF16), before, preferred_element_type=F32) + 16.0
    leaf_n = jnp.sum(leaf_one, axis=1, keepdims=True)
    top_n = jnp.sum(top_one, axis=1, keepdims=True)
    leaf_pos = jnp.where(leaf_hit, leaf_pos, -1.0)
    top_pos = jnp.where(top_hit, top_pos, -1.0)
    local = (lower & 7) + (upper & 7) * 8
    codes = jnp.where(sub8 == 0, lane >> 4, jnp.where(sub8 == 1, local, 0)).astype(F32).astype(BF16)
    tcodes = jnp.where(sub8 == 0, tl >> 3, 0).astype(F32).astype(BF16)
    rowf = row.astype(F32)
    for d in range(8):
        for c in range(3):
            m0[d, 8 * c : 8 * c + 8, :] = skel[c]
            m0[d, 24 + c : 25 + c, :] = cpts[c]
        m0[d, 29:32, :] = jnp.zeros((3, 128), F32)
        oh = (leaf_pos[d : d + 1] == rowf).astype(F32).astype(BF16)
        got = lax.dot_general(codes, oh, (((1,), (1,)), ((), ())), preferred_element_type=F32)
        m0[d, 27:28, :] = got[0:1] * 128.0 + got[1:2]
        oh = (top_pos[d : d + 1] == rowf).astype(F32).astype(BF16)
        got = lax.dot_general(tcodes, oh, (((1,), (1,)), ((), ())), preferred_element_type=F32)[0:1]
        got = got + jnp.where(lane == 0, leaf_n[d : d + 1], 0.0) + jnp.where(lane == 1, top_n[d : d + 1], 0.0)
        m0[d, 28:29, :] = got
    for slab, start in ((first, 0), (last, OWN - REACH)):
        for i in range(REACH):
            slab[8 * i : 8 * i + 8, :] = chg[start + i]
        for c in range(3):
            slab[32 + 4 * c : 36 + 4 * c, :] = pts[c, start : start + REACH, :]
        slab[44:48, :] = jnp.zeros((4, 256), F32)


def request(pts, chg, skel, cpts, llist, tlist):
    sd = jax.ShapeDtypeStruct
    return pl.pallas_call(
        request_kernel,
        in_specs=[VMEM] * 6,
        out_specs=[VMEM] * 3,
        out_shape=[sd((8, 32, 128), F32), sd((48, 256), F32), sd((48, 256), F32)],
        scratch_shapes=[pltpu.VMEM((8, 128), jnp.int32)],
        compiler_params=PARAMS,
        name="request",
    )(pts, chg, skel, cpts, llist, tlist)


def weights_kernel(chg, up, skel, utm, cpts, m1):
    for l in range(OWN):
        w = nt(chg[l], up[l])
        cw = nt(w, utm[l])
        total = cw if l == 0 else total + cw
        for d in range(8):
            m1[d, 8 * l : 8 * l + 8, :] = w
    for d in range(8):
        m1[d, 88:96, :] = total
        for c in range(3):
            m1[d, 64 + 8 * c : 72 + 8 * c, :] = skel[c]
            m1[d, 96 + c : 97 + c, :] = cpts[c]
        m1[d, 99:104, :] = jnp.zeros((5, 128), F32)


def weights(chg, up, skel, utm, cpts):
    return pl.pallas_call(
        weights_kernel,
        in_specs=[VMEM] * 5,
        out_specs=VMEM,
        out_shape=jax.ShapeDtypeStruct((8, 104, 128), F32),
        compiler_params=PARAMS,
        name="weights",
    )(chg, up, skel, utm, cpts)


def near_kernel(lo, hi, ids, pts, chg, before, after, out, fs, ft, vals, xyz, ts, tl):
    me = (lax.axis_index("g") * lax.axis_size("y") + lax.axis_index("y")) * lax.axis_size("z") + lax.axis_index("z")
    base = me * OWN - REACH
    for c in range(3):
        xyz[c, 0:4, :] = before[32 + 4 * c : 36 + 4 * c, :]
        xyz[c, 4:12, :] = pts[c]
        xyz[c, 12:16, :] = after[32 + 4 * c : 36 + 4 * c, :]
    s0, s1, t0, t1, t2 = dense_features([xyz[0], xyz[1], xyz[2]])
    s0 = spread(s0, ts)
    s1 = spread(s1, tl)
    for e in range(lo, hi + 2 * REACH):
        a, b = s0(e), s1(e)
        fs[e - lo] = jnp.concatenate([a, b, a, b], 0).T.astype(BF16)
        if e < REACH:
            c = before[8 * e : 8 * e + 8, :]
        elif e < REACH + OWN:
            c = chg[e - REACH]
        else:
            c = after[8 * (e - REACH - OWN) : 8 * (e - REACH - OWN) + 8, :]
        vals[e - lo] = two_halves(c)
    for i, rows in enumerate((t0, t2, t1, t1)):
        load = spread(rows, ts)
        for e in range(lo + REACH, hi + REACH):
            ft[e - REACH - lo, 8 * i : 8 * i + 8, :] = load(e)
    dead = hi - lo + 2 * REACH
    vals[dead] = jnp.zeros((16, 256), BF16)

    def leaf(i, carry):
        tgt = ft[i].astype(BF16)
        acc = jnp.zeros((16, 256), F32)
        for n in range(NBR):
            ident = ids[i + lo, n]
            live = ident >= 0
            e = jnp.where(live, ident - base - lo, 0)
            acc = acc + product(fs[e], tgt, vals[jnp.where(live, e, dead)])
        out[i] = acc[0:8] + acc[8:16]
        return carry

    lax.fori_loop(0, hi - lo, leaf, 0)


def near_part(lo, hi, ids, pts, chg, before, after):
    n = hi - lo
    return pl.pallas_call(
        functools.partial(near_kernel, lo, hi),
        in_specs=[SMEM] + [VMEM] * 4,
        out_specs=VMEM,
        out_shape=jax.ShapeDtypeStruct((n, 8, 256), F32),
        scratch_shapes=[
            pltpu.VMEM((n + 8, 256, FEAT), BF16),
            pltpu.VMEM((n, FEAT, 256), F32),
            pltpu.VMEM((n + 9, 16, 256), BF16),
            pltpu.VMEM((3, 16, 256), F32),
            pltpu.VMEM((2, 128, 128), F32),
            pltpu.VMEM((2, 128, 128), F32),
        ],
        cost_estimate=pl.CostEstimate(flops=n * 9 * 65536000, bytes_accessed=300000, transcendentals=n * 9 * 131072),
        compiler_params=PARAMS,
        name="near",
    )(ids, pts, chg, before, after)


def prepare_sources(i, xyz, t0, t1, even, odd):
    s0, s1, _, _, _ = dense_features(xyz)
    s0 = spread(s0, t0)
    s1 = spread(s1, t1)
    rows = []
    for l in range(8):
        a, b = s0(l), s1(l)
        rows.append(jnp.concatenate([a, b, a, b], 0))
    zero = jnp.zeros((64, 128), F32)
    left = lax.broadcasted_iota(jnp.int32, (128, 128), 1) < FEAT
    for l in range(0, 8, 2):
        for a, b in ((l, l + 1), (l + 1, l)):
            both = jnp.concatenate([rows[a], rows[b], zero], 0).T
            even[8 * i + a] = jnp.where(left, both, 0.0).astype(BF16)[:, 0:64]
            odd[8 * i + b] = jnp.where(left, 0.0, both).astype(BF16)[:, 0:64]


def prepare_targets(i, xyz, tmp, ft):
    _, _, t0, t1, t2 = dense_features(xyz)
    for j, rows in enumerate((t0, t2, t1, t1)):
        load = spread(rows, tmp.at[j])
        for l in range(8):
            ft[8 * i + l, 8 * j : 8 * j + 8, :] = load(l)


def flatten(req, flat, row, start, slot):
    off = 0
    for d in range(8):
        n = req[d, 1, slot]

        def copy(j, carry, d=d, off=off):
            for u in range(8):
                flat[off + j * 8 + u] = req[d, row, start + j * 8 + u] + d * (1024 if row == 0 else 128)
            return carry

        lax.fori_loop(0, (n + 7) // 8, copy, 0)
        off = off + n
    for u in range(2 * PAIRS):
        flat[off + u] = DUMMY
    return off


def interact(total, flat, even, odd, ft, vals, add):
    zero = jnp.zeros((FEAT, 128), BF16)

    def chunk(i, carry):
        for u in range(PAIRS):
            ca = flat[i * (2 * PAIRS) + 2 * u]
            cb = flat[i * (2 * PAIRS) + 2 * u + 1]
            ta, sa = ca >> 7, ca & 127
            tb, sb = cb >> 7, cb & 127
            fa = ft[ta].astype(BF16)
            fb = ft[tb].astype(BF16)
            tgt = jnp.concatenate([jnp.concatenate([fa, zero], 1), jnp.concatenate([zero, fb], 1)], 0)
            r = product(even[sa] + odd[sb], tgt, jnp.concatenate([vals[sa], vals[sb]], 0))
            add(ta, r[0:8, 0:128] + r[8:16, 0:128])
            add(tb, r[16:24, 128:256] + r[24:32, 128:256])
        return carry

    lax.fori_loop(0, (total + 2 * PAIRS - 1) // (2 * PAIRS), chunk, 0)


def clear_dummy(even, odd, vals):
    even[DUMMY] = jnp.zeros((128, 64), BF16)
    odd[DUMMY] = jnp.zeros((128, 64), BF16)
    vals[DUMMY] = jnp.zeros((16, 128), BF16)


def far_leaf_kernel(req, src, tgt, out, flat, even, odd, ft, vals, t0, t1, t2):
    for y in range(8):
        prepare_sources(y, [src[y, 64 + 8 * c : 72 + 8 * c, :] for c in range(3)], t0.at[y], t1.at[y], even, odd)
        prepare_targets(y, [tgt[32 * y + 8 * c : 32 * y + 8 * c + 8, :] for c in range(3)], t2.at[y], ft)
        for l in range(OWN):
            vals[8 * y + l] = two_halves(src[y, 8 * l : 8 * l + 8, :])
    clear_dummy(even, odd, vals)
    out[...] = jnp.zeros_like(out)
    total = flatten(req, flat, 0, 0, 0)

    def add(t, v):
        out[t >> 3, t & 7] += v

    interact(total, flat, even, odd, ft, vals, add)


FAR_SCRATCH = [
    pltpu.SMEM((1024 + 64,), jnp.int32),
    pltpu.VMEM((65, 128, 64), BF16),
    pltpu.VMEM((65, 128, 64), BF16),
    pltpu.VMEM((64, FEAT, 128), F32),
    pltpu.VMEM((65, 16, 128), BF16),
    pltpu.VMEM((8, 1, 64, 128), F32),
    pltpu.VMEM((8, 1, 64, 128), F32),
    pltpu.VMEM((8, 4, 1, 64, 128), F32),
]


def far_leaf(req, src, tgt):
    return pl.pallas_call(
        far_leaf_kernel,
        in_specs=[SMEM, VMEM, VMEM],
        out_specs=VMEM,
        out_shape=jax.ShapeDtypeStruct((8, 9, 8, 128), F32),
        scratch_shapes=FAR_SCRATCH,
        cost_estimate=pl.CostEstimate(flops=2097152000, bytes_accessed=900000, transcendentals=4194304),
        compiler_params=PARAMS,
        name="far_leaf",
    )(req, src, tgt.reshape(256, 128))


def far_top_kernel(req, src, tgt, part, out, flat, even, odd, ft, vals, t0, t1, t2):
    for g in range(8):
        xyz = [src[pl.ds(128 * g + 8 + c, 8, stride=16), :] for c in range(3)]
        prepare_sources(g, xyz, t0.at[g], t1.at[g], even, odd)
        for y in range(8):
            vals[8 * g + y] = two_halves(src[128 * g + 16 * y : 128 * g + 16 * y + 8, :])
    prepare_targets(0, [tgt[pl.ds(24 + c, 8, stride=32), :] for c in range(3)], t2.at[0], ft)
    clear_dummy(even, odd, vals)
    out[...] = part[...]
    total = flatten(req, flat, 1, 16, 1)

    def add(t, v):
        out[t, 8] += v

    interact(total, flat, even, odd, ft, vals, add)


def far_top(req, src, tgt, part):
    return pl.pallas_call(
        far_top_kernel,
        in_specs=[SMEM, VMEM, VMEM, VMEM],
        out_specs=VMEM,
        out_shape=jax.ShapeDtypeStruct((8, 9, 8, 128), F32),
        scratch_shapes=FAR_SCRATCH,
        compiler_params=PARAMS,
        name="far_top",
    )(req, src.reshape(1024, 128), tgt.reshape(256, 128), part)


def final_kernel(got, utm, up, near1, near2, out):
    tot = got[0]
    for d in range(1, 8):
        tot = tot + got[d]
    cell = tot[8]
    half = near1.shape[0]
    for l in range(OWN):
        incoming = tot[l] + jnp.dot(cell, utm[l], precision=EXACT, preferred_element_type=F32)
        near = near1[l] if l < half else near2[l - half]
        out[l] = near + jnp.dot(incoming, up[l], precision=EXACT, preferred_element_type=F32)


def final(got, utm, up, near1, near2):
    return pl.pallas_call(
        final_kernel,
        in_specs=[VMEM] * 5,
        out_specs=VMEM,
        out_shape=jax.ShapeDtypeStruct((8, 8, 256), F32),
        compiler_params=PARAMS,
        name="final",
    )(got, utm, up, near1, near2)


def body(points, charges, up_op, skel_pts, utm, cell_pts, near_list, leaf_list, top_list):
    every = ("g", "y", "z")
    pts = jnp.transpose(points, (1, 0, 2))
    skel = jnp.transpose(skel_pts, (1, 0, 2))
    cpts = jnp.transpose(cell_pts, (1, 0, 2))
    count = lax.axis_size("g") * lax.axis_size("y") * lax.axis_size("z")
    up = [(i, i + 1) for i in range(count - 1)]
    down = [(i + 1, i) for i in range(count - 1)]
    m0, first, last = request(pts, charges, skel, cpts, leaf_list, top_list)
    got0 = lax.all_to_all(m0, "z", 0, 0, tiled=True)
    before = lax.ppermute(last, every, up)
    after = lax.ppermute(first, every, down)
    m1 = weights(charges, up_op, skel, utm, cpts)
    m1, got0 = lax.optimization_barrier((m1, got0))
    got1 = lax.all_to_all(m1, "y", 0, 0, tiled=True)
    req = got0[:, 27:29, :].astype(jnp.int32)
    near1 = near_part(0, 4, near_list, pts, charges, before, after)
    got1, near1 = lax.optimization_barrier((got1, near1))
    cells = jnp.broadcast_to(got1[:, 88:104, :].reshape(1, 128, 128), (8, 128, 128))
    gotg = lax.all_to_all(cells, "g", 0, 0, tiled=True)
    part = far_leaf(req, got1, got0)
    part = far_top(req, gotg, got0, part)
    part, charges2 = lax.optimization_barrier((part, charges))
    gotr = lax.all_to_all(part, "z", 0, 0, tiled=True)
    near2 = near_part(4, 8, near_list, pts, charges2, before, after)
    return final(gotr, utm, up_op, near1, near2)


def solution(mesh):
    fine = Mesh(mesh.devices.reshape(mesh.shape["group"], 8, 8), ("g", "y", "z"))
    row = ("g", "y", "z")
    specs = tuple(P(row, *([None] * k)) for k in (2, 2, 2, 2, 2, 2, 1, 1, 1))
    return jax.shard_map(body, mesh=fine, in_specs=specs, out_specs=P(row, None, None), check_vma=False)
```

```python
import functools
import math

import jax
import jax.numpy as jnp
from jax import lax
from jax.experimental import pallas as pl
from jax.experimental.pallas import tpu as pltpu
from jax.sharding import Mesh, PartitionSpec as P

F32 = jnp.float32
BF16 = jnp.bfloat16
KAPPA = math.sqrt(3.0) * math.log2(math.e)
LN2 = math.log(2.0)
CENTER = 1.5
FEAT = 32
REACH = 4
OWN = 8
NBR = 9
PAIRS = 8
DUMMY = 64

SMEM = pl.BlockSpec(memory_space=pltpu.SMEM)
HBM = pl.BlockSpec(memory_space=pltpu.HBM)
VMEM = pl.BlockSpec(memory_space=pltpu.VMEM)
PARAMS = pltpu.CompilerParams(vmem_limit_bytes=40 << 20)
WIDE = pltpu.CompilerParams(vmem_limit_bytes=60 << 20)


def split2(x):
    a = x.astype(BF16).astype(F32)
    return a, (x - a).astype(BF16).astype(F32)


def split3(x):
    a = x.astype(BF16).astype(F32)
    b, c = split2(x - a)
    return a, b, c


def dense_features(xyz):
    parts = [split2((x - CENTER) * KAPPA) for x in xyz]
    n = None
    for a, b in parts:
        r = a + b
        n = r * r if n is None else n + r * r
    n1, n2, n3 = split3(n)
    one = jnp.ones_like(n)
    zero = jnp.zeros_like(n)
    high = [a for a, _ in parts]
    low = [b for _, b in parts]
    high2 = [-2.0 * a for a in high]
    low2 = [-2.0 * b for b in low]
    s0 = high + [n1, n2, n3, one, one]
    s1 = low + [one, zero, zero, zero, zero]
    t0 = high2 + [one, one, one, n1, n2]
    t1 = low2 + [zero] * 5
    t2 = high2 + [n3] + [zero] * 4
    return s0, s1, t0, t1, t2


def spread(rows, tmp):
    n, width = rows[0].shape
    halves = width // 128
    for r, v in enumerate(rows):
        for h in range(halves):
            tmp[h, n * r : n * r + n, :] = v[:, 128 * h : 128 * h + 128]

    def load(leaf):
        return jnp.concatenate([tmp[h, pl.ds(leaf, 8, stride=n), :] for h in range(halves)], 1)

    return load


def two_halves(vals):
    v = vals * LN2
    high = v.astype(BF16).astype(F32)
    return jnp.concatenate([high, v - high], 0).astype(BF16)


def matern_over_ln2(t):
    m = jnp.maximum(t, 1e-12)
    s = m * lax.rsqrt(m)
    return (s + 1.0 / LN2) * jnp.exp2(-s)


def product(src_feat, tgt_feat, vals):
    t = jnp.dot(src_feat, tgt_feat, preferred_element_type=F32)
    k = matern_over_ln2(t)
    high = k.astype(BF16)
    low = (k - high.astype(F32)).astype(BF16)
    return jnp.dot(vals, high, preferred_element_type=F32) + jnp.dot(vals, low, preferred_element_type=F32)


def dot3(a, b, transposed=False):
    ah = a.astype(BF16).astype(F32)
    both = jnp.concatenate([ah, a - ah], 0).astype(BF16)
    bh = b.astype(BF16)
    bl = (b - bh.astype(F32)).astype(BF16)
    dims = (((1,), (1 if transposed else 0,)), ((), ()))
    r = lax.dot_general(both, bh, dims, preferred_element_type=F32)
    r = r + lax.dot_general(both, bl, dims, preferred_element_type=F32)
    return r[0:8] + r[8:16]


def fetch(pairs, sems):
    copies = [pltpu.make_async_copy(a, b, sems.at[i]) for i, (a, b) in enumerate(pairs)]
    for c in copies:
        c.start()
    return copies


def request_kernel(pts_h, chg_h, skel_h, cpts_h, llist_h, tlist_h, m0, first, last, row16, pts, chg, skel, cpts, llist, tlist, sems):
    ins = ((llist_h, llist), (tlist_h, tlist), (skel_h, skel), (cpts_h, cpts), (pts_h, pts), (chg_h, chg))
    copies = fetch(ins, sems)
    for c in copies[0:2]:
        c.wait()
    lane = lax.broadcasted_iota(jnp.int32, (1, 128), 1)
    sub8 = lax.broadcasted_iota(jnp.int32, (8, 128), 0)
    lane8 = lax.broadcasted_iota(jnp.int32, (8, 128), 1)
    row = lax.broadcasted_iota(jnp.int32, (128, 128), 0)
    col = lax.broadcasted_iota(jnp.int32, (128, 128), 1)
    before = (row < col).astype(F32).astype(BF16)
    pick = (lax.broadcasted_iota(jnp.int32, (16, 128), 0) == (lax.broadcasted_iota(jnp.int32, (16, 128), 1) & 15))
    pick = pick.astype(F32).astype(BF16)
    ll = llist[...]
    mine = sub8 == (lane8 >> 4)

    def flat(v):
        w = jnp.dot(v.astype(F32).astype(BF16), pick, preferred_element_type=F32)
        return jnp.sum(jnp.where(mine, w, 0.0), axis=0, keepdims=True).astype(jnp.int32)

    upper = flat(ll >> 6)
    lower = flat(ll & 63)
    row16[...] = jnp.zeros((8, 128), jnp.int32)
    row16[0:1, 0:16] = tlist[...]
    tl = row16[0:1, :]
    leaf_hit = (lower >> 3) == sub8
    top_hit = ((tl & 7) == sub8) & (lane < 16)
    leaf_one = leaf_hit.astype(F32)
    top_one = top_hit.astype(F32)
    leaf_pos = jnp.dot(leaf_one.astype(BF16), before, preferred_element_type=F32)
    top_pos = jnp.dot(top_one.astype(BF16), before, preferred_element_type=F32) + 16.0
    leaf_n = jnp.sum(leaf_one, axis=1, keepdims=True)
    top_n = jnp.sum(top_one, axis=1, keepdims=True)
    leaf_pos = jnp.where(leaf_hit, leaf_pos, -1.0)
    top_pos = jnp.where(top_hit, top_pos, -1.0)
    local = (lower & 7) + (upper & 7) * 8
    codes = jnp.where(sub8 == 0, lane >> 4, jnp.where(sub8 == 1, local, 0)).astype(F32).astype(BF16)
    tcodes = jnp.where(sub8 == 0, tl >> 3, 0).astype(F32).astype(BF16)
    rowf = row.astype(F32)
    for c in copies[2:6]:
        c.wait()
    for d in range(8):
        for c in range(3):
            m0[d, 8 * c : 8 * c + 8, :] = skel[c]
            m0[d, 24 + c : 25 + c, :] = cpts[c]
        m0[d, 29:32, :] = jnp.zeros((3, 128), F32)
        oh = (leaf_pos[d : d + 1] == rowf).astype(F32).astype(BF16)
        got = lax.dot_general(codes, oh, (((1,), (1,)), ((), ())), preferred_element_type=F32)
        m0[d, 27:28, :] = got[0:1] * 128.0 + got[1:2]
        oh = (top_pos[d : d + 1] == rowf).astype(F32).astype(BF16)
        got = lax.dot_general(tcodes, oh, (((1,), (1,)), ((), ())), preferred_element_type=F32)[0:1]
        got = got + jnp.where(lane == 0, leaf_n[d : d + 1], 0.0) + jnp.where(lane == 1, top_n[d : d + 1], 0.0)
        m0[d, 28:29, :] = got
    for slab, start in ((first, 0), (last, OWN - REACH)):
        for i in range(REACH):
            slab[8 * i : 8 * i + 8, :] = chg[start + i]
        for c in range(3):
            slab[32 + 4 * c : 36 + 4 * c, :] = pts[c, start : start + REACH, :]
        slab[44:48, :] = jnp.zeros((4, 256), F32)


def request(pts, chg, skel, cpts, llist, tlist):
    sd = jax.ShapeDtypeStruct
    return pl.pallas_call(
        request_kernel,
        in_specs=[HBM] * 6,
        out_specs=[VMEM] * 3,
        out_shape=[sd((8, 32, 128), F32), sd((48, 256), F32), sd((48, 256), F32)],
        scratch_shapes=[pltpu.VMEM((8, 128), jnp.int32)]
        + [pltpu.VMEM(a.shape, a.dtype) for a in (pts, chg, skel, cpts, llist, tlist)]
        + [pltpu.SemaphoreType.DMA((6,))],
        compiler_params=WIDE,
        name="request",
    )(pts, chg, skel, cpts, llist, tlist)


def weights_kernel(chg_h, up_h, skel_h, utm_h, cpts_h, m1, chg, up, skel, utm, cpts, sems):
    ins = [(chg_h, chg)]
    for l in range(OWN):
        ins += [(up_h.at[l], up.at[l]), (utm_h.at[l], utm.at[l])]
    ins += [(skel_h, skel), (cpts_h, cpts)]
    copies = fetch(ins, sems)
    copies[0].wait()
    for l in range(OWN):
        copies[1 + 2 * l].wait()
        w = dot3(chg[l], up[l], True)
        copies[2 + 2 * l].wait()
        cw = dot3(w, utm[l], True)
        total = cw if l == 0 else total + cw
        for d in range(8):
            m1[d, 8 * l : 8 * l + 8, :] = w
    copies[17].wait()
    copies[18].wait()
    for d in range(8):
        m1[d, 88:96, :] = total
        for c in range(3):
            m1[d, 64 + 8 * c : 72 + 8 * c, :] = skel[c]
            m1[d, 96 + c : 97 + c, :] = cpts[c]
        m1[d, 99:104, :] = jnp.zeros((5, 128), F32)


def weights(chg, up, skel, utm, cpts):
    return pl.pallas_call(
        weights_kernel,
        in_specs=[HBM] * 5,
        out_specs=VMEM,
        out_shape=jax.ShapeDtypeStruct((8, 104, 128), F32),
        scratch_shapes=[pltpu.VMEM(a.shape, a.dtype) for a in (chg, up, skel, utm, cpts)] + [pltpu.SemaphoreType.DMA((19,))],
        compiler_params=WIDE,
        name="weights",
    )(chg, up, skel, utm, cpts)


def near_kernel(lo, hi, ids, pts, chg, before, after, out, fs, ft, vals, xyz, ts, tl):
    me = (lax.axis_index("g") * lax.axis_size("y") + lax.axis_index("y")) * lax.axis_size("z") + lax.axis_index("z")
    base = me * OWN - REACH
    for c in range(3):
        xyz[c, 0:4, :] = before[32 + 4 * c : 36 + 4 * c, :]
        xyz[c, 4:12, :] = pts[c]
        xyz[c, 12:16, :] = after[32 + 4 * c : 36 + 4 * c, :]
    s0, s1, t0, t1, t2 = dense_features([xyz[0], xyz[1], xyz[2]])
    s0 = spread(s0, ts)
    s1 = spread(s1, tl)
    for e in range(lo, hi + 2 * REACH):
        a, b = s0(e), s1(e)
        fs[e - lo] = jnp.concatenate([a, b, a, b], 0).T.astype(BF16)
        if e < REACH:
            c = before[8 * e : 8 * e + 8, :]
        elif e < REACH + OWN:
            c = chg[e - REACH]
        else:
            c = after[8 * (e - REACH - OWN) : 8 * (e - REACH - OWN) + 8, :]
        vals[e - lo] = two_halves(c)
    for i, rows in enumerate((t0, t2, t1, t1)):
        load = spread(rows, ts)
        for e in range(lo + REACH, hi + REACH):
            ft[e - REACH - lo, 8 * i : 8 * i + 8, :] = load(e)
    dead = hi - lo + 2 * REACH
    vals[dead] = jnp.zeros((16, 256), BF16)

    def leaf(i, carry):
        tgt = ft[i].astype(BF16)
        acc = jnp.zeros((16, 256), F32)
        for n in range(NBR):
            ident = ids[i + lo, n]
            live = ident >= 0
            e = jnp.where(live, ident - base - lo, 0)
            acc = acc + product(fs[e], tgt, vals[jnp.where(live, e, dead)])
        out[i] = acc[0:8] + acc[8:16]
        return carry

    lax.fori_loop(0, hi - lo, leaf, 0)


def near_part(lo, hi, ids, pts, chg, before, after):
    n = hi - lo
    return pl.pallas_call(
        functools.partial(near_kernel, lo, hi),
        in_specs=[SMEM] + [VMEM] * 4,
        out_specs=VMEM,
        out_shape=jax.ShapeDtypeStruct((n, 8, 256), F32),
        scratch_shapes=[
            pltpu.VMEM((n + 8, 256, FEAT), BF16),
            pltpu.VMEM((n, FEAT, 256), F32),
            pltpu.VMEM((n + 9, 16, 256), BF16),
            pltpu.VMEM((3, 16, 256), F32),
            pltpu.VMEM((2, 128, 128), F32),
            pltpu.VMEM((2, 128, 128), F32),
        ],
        cost_estimate=pl.CostEstimate(flops=n * 9 * 65536000, bytes_accessed=300000, transcendentals=n * 9 * 131072),
        compiler_params=PARAMS,
        name="near",
    )(ids, pts, chg, before, after)


def prepare_sources(i, xyz, t0, t1, even, odd):
    s0, s1, _, _, _ = dense_features(xyz)
    s0 = spread(s0, t0)
    s1 = spread(s1, t1)
    rows = []
    for l in range(8):
        a, b = s0(l), s1(l)
        rows.append(jnp.concatenate([a, b, a, b], 0))
    zero = jnp.zeros((64, 128), F32)
    left = lax.broadcasted_iota(jnp.int32, (128, 128), 1) < FEAT
    for l in range(0, 8, 2):
        for a, b in ((l, l + 1), (l + 1, l)):
            both = jnp.concatenate([rows[a], rows[b], zero], 0).T
            even[8 * i + a] = jnp.where(left, both, 0.0).astype(BF16)[:, 0:64]
            odd[8 * i + b] = jnp.where(left, 0.0, both).astype(BF16)[:, 0:64]


def prepare_targets(i, xyz, tmp, ft):
    _, _, t0, t1, t2 = dense_features(xyz)
    for j, rows in enumerate((t0, t2, t1, t1)):
        load = spread(rows, tmp.at[j])
        for l in range(8):
            ft[8 * i + l, 8 * j : 8 * j + 8, :] = load(l)


def flatten(req, flat, row, start, slot):
    off = 0
    for d in range(8):
        n = req[d, 1, slot]

        def copy(j, carry, d=d, off=off):
            for u in range(8):
                flat[off + j * 8 + u] = req[d, row, start + j * 8 + u] + d * (1024 if row == 0 else 128)
            return carry

        lax.fori_loop(0, (n + 7) // 8, copy, 0)
        off = off + n
    for u in range(2 * PAIRS):
        flat[off + u] = DUMMY
    return off


def interact(total, flat, even, odd, ft, vals, add):
    zero = jnp.zeros((FEAT, 128), BF16)

    def chunk(i, carry):
        for u in range(PAIRS):
            ca = flat[i * (2 * PAIRS) + 2 * u]
            cb = flat[i * (2 * PAIRS) + 2 * u + 1]
            ta, sa = ca >> 7, ca & 127
            tb, sb = cb >> 7, cb & 127
            fa = ft[ta].astype(BF16)
            fb = ft[tb].astype(BF16)
            tgt = jnp.concatenate([jnp.concatenate([fa, zero], 1), jnp.concatenate([zero, fb], 1)], 0)
            r = product(even[sa] + odd[sb], tgt, jnp.concatenate([vals[sa], vals[sb]], 0))
            add(ta, r[0:8, 0:128] + r[8:16, 0:128])
            add(tb, r[16:24, 128:256] + r[24:32, 128:256])
        return carry

    lax.fori_loop(0, (total + 2 * PAIRS - 1) // (2 * PAIRS), chunk, 0)


def clear_dummy(even, odd, vals):
    even[DUMMY] = jnp.zeros((128, 64), BF16)
    odd[DUMMY] = jnp.zeros((128, 64), BF16)
    vals[DUMMY] = jnp.zeros((16, 128), BF16)


def far_leaf_kernel(req, src, tgt, out, flat, even, odd, ft, vals, t0, t1, t2):
    for y in range(8):
        prepare_sources(y, [src[y, 64 + 8 * c : 72 + 8 * c, :] for c in range(3)], t0.at[y], t1.at[y], even, odd)
        prepare_targets(y, [tgt[32 * y + 8 * c : 32 * y + 8 * c + 8, :] for c in range(3)], t2.at[y], ft)
        for l in range(OWN):
            vals[8 * y + l] = two_halves(src[y, 8 * l : 8 * l + 8, :])
    clear_dummy(even, odd, vals)
    out[...] = jnp.zeros_like(out)
    total = flatten(req, flat, 0, 0, 0)

    def add(t, v):
        out[t >> 3, t & 7] += v

    interact(total, flat, even, odd, ft, vals, add)


FAR_SCRATCH = [
    pltpu.SMEM((1024 + 64,), jnp.int32),
    pltpu.VMEM((65, 128, 64), BF16),
    pltpu.VMEM((65, 128, 64), BF16),
    pltpu.VMEM((64, FEAT, 128), F32),
    pltpu.VMEM((65, 16, 128), BF16),
    pltpu.VMEM((8, 1, 64, 128), F32),
    pltpu.VMEM((8, 1, 64, 128), F32),
    pltpu.VMEM((8, 4, 1, 64, 128), F32),
]


def far_leaf(req, src, tgt):
    return pl.pallas_call(
        far_leaf_kernel,
        in_specs=[SMEM, VMEM, VMEM],
        out_specs=VMEM,
        out_shape=jax.ShapeDtypeStruct((8, 9, 8, 128), F32),
        scratch_shapes=FAR_SCRATCH,
        cost_estimate=pl.CostEstimate(flops=2097152000, bytes_accessed=900000, transcendentals=4194304),
        compiler_params=PARAMS,
        name="far_leaf",
    )(req, src, tgt.reshape(256, 128))


def far_top_kernel(req, src, tgt, part, out, flat, even, odd, ft, vals, t0, t1, t2):
    for g in range(8):
        xyz = [src[pl.ds(128 * g + 8 + c, 8, stride=16), :] for c in range(3)]
        prepare_sources(g, xyz, t0.at[g], t1.at[g], even, odd)
        for y in range(8):
            vals[8 * g + y] = two_halves(src[128 * g + 16 * y : 128 * g + 16 * y + 8, :])
    prepare_targets(0, [tgt[pl.ds(24 + c, 8, stride=32), :] for c in range(3)], t2.at[0], ft)
    clear_dummy(even, odd, vals)
    out[...] = part[...]
    total = flatten(req, flat, 1, 16, 1)

    def add(t, v):
        out[t, 8] += v

    interact(total, flat, even, odd, ft, vals, add)


def far_top(req, src, tgt, part):
    return pl.pallas_call(
        far_top_kernel,
        in_specs=[SMEM, VMEM, VMEM, VMEM],
        out_specs=VMEM,
        out_shape=jax.ShapeDtypeStruct((8, 9, 8, 128), F32),
        scratch_shapes=FAR_SCRATCH,
        compiler_params=PARAMS,
        name="far_top",
    )(req, src.reshape(1024, 128), tgt.reshape(256, 128), part)


def final_kernel(got, utm, up, near1, near2, out):
    tot = got[0]
    for d in range(1, 8):
        tot = tot + got[d]
    cell = tot[8]
    half = near1.shape[0]
    for l in range(OWN):
        incoming = tot[l] + dot3(cell, utm[l])
        near = near1[l] if l < half else near2[l - half]
        out[l] = near + dot3(incoming, up[l])


def final(got, utm, up, near1, near2):
    return pl.pallas_call(
        final_kernel,
        in_specs=[VMEM] * 5,
        out_specs=VMEM,
        out_shape=jax.ShapeDtypeStruct((8, 8, 256), F32),
        compiler_params=PARAMS,
        name="final",
    )(got, utm, up, near1, near2)


def body(points, charges, up_op, skel_pts, utm, cell_pts, near_list, leaf_list, top_list):
    every = ("g", "y", "z")
    pts = jnp.transpose(points, (1, 0, 2))
    skel = jnp.transpose(skel_pts, (1, 0, 2))
    cpts = jnp.transpose(cell_pts, (1, 0, 2))
    count = lax.axis_size("g") * lax.axis_size("y") * lax.axis_size("z")
    up = [(i, i + 1) for i in range(count - 1)]
    down = [(i + 1, i) for i in range(count - 1)]
    m0, first, last = request(pts, charges, skel, cpts, leaf_list, top_list)
    got0 = lax.all_to_all(m0, "z", 0, 0, tiled=True)
    before = lax.ppermute(last, every, up)
    after = lax.ppermute(first, every, down)
    skel1, before, after = lax.optimization_barrier((skel, before, after))
    m1 = weights(charges, up_op, skel1, utm, cpts)
    m1, got0 = lax.optimization_barrier((m1, got0))
    got1 = lax.all_to_all(m1, "y", 0, 0, tiled=True)
    req = got0[:, 27:29, :].astype(jnp.int32)
    near1 = near_part(0, 4, near_list, pts, charges, before, after)
    got1, near1 = lax.optimization_barrier((got1, near1))
    cells = jnp.broadcast_to(got1[:, 88:104, :].reshape(1, 128, 128), (8, 128, 128))
    gotg = lax.all_to_all(cells, "g", 0, 0, tiled=True)
    part = far_leaf(req, got1, got0)
    part = far_top(req, gotg, got0, part)
    part, charges2 = lax.optimization_barrier((part, charges))
    gotr = lax.all_to_all(part, "z", 0, 0, tiled=True)
    near2 = near_part(4, 8, near_list, pts, charges2, before, after)
    return final(gotr, utm, up_op, near1, near2)


def solution(mesh):
    fine = Mesh(mesh.devices.reshape(mesh.shape["group"], 8, 8), ("g", "y", "z"))
    row = ("g", "y", "z")
    specs = tuple(P(row, *([None] * k)) for k in (2, 2, 2, 2, 2, 2, 1, 1, 1))
    return jax.shard_map(body, mesh=fine, in_specs=specs, out_specs=P(row, None, None), check_vma=False)
```

```python
import functools
import math

import jax
import jax.numpy as jnp
from jax import lax
from jax.experimental import pallas as pl
from jax.experimental.pallas import tpu as pltpu
from jax.sharding import Mesh, PartitionSpec as P

F32 = jnp.float32
BF16 = jnp.bfloat16
KAPPA = math.sqrt(3.0) * math.log2(math.e)
LN2 = math.log(2.0)
CENTER = 1.5
FEAT = 32
REACH = 4
OWN = 8
NBR = 9
PAIRS = 8
DUMMY = 64

SMEM = pl.BlockSpec(memory_space=pltpu.SMEM)
HBM = pl.BlockSpec(memory_space=pltpu.HBM)
VMEM = pl.BlockSpec(memory_space=pltpu.VMEM)
PARAMS = pltpu.CompilerParams(vmem_limit_bytes=40 << 20)
WIDE = pltpu.CompilerParams(vmem_limit_bytes=60 << 20)


def split2(x):
    a = x.astype(BF16).astype(F32)
    return a, (x - a).astype(BF16).astype(F32)


def split3(x):
    a = x.astype(BF16).astype(F32)
    b, c = split2(x - a)
    return a, b, c


def dense_features(xyz):
    parts = [split2((x - CENTER) * KAPPA) for x in xyz]
    n = None
    for a, b in parts:
        r = a + b
        n = r * r if n is None else n + r * r
    n1, n2, n3 = split3(n)
    one = jnp.ones_like(n)
    zero = jnp.zeros_like(n)
    high = [a for a, _ in parts]
    low = [b for _, b in parts]
    high2 = [-2.0 * a for a in high]
    low2 = [-2.0 * b for b in low]
    s0 = high + [n1, n2, n3, one, one]
    s1 = low + [one, zero, zero, zero, zero]
    t0 = high2 + [one, one, one, n1, n2]
    t1 = low2 + [zero] * 5
    t2 = high2 + [n3] + [zero] * 4
    return s0, s1, t0, t1, t2


def spread(rows, tmp):
    n, width = rows[0].shape
    halves = width // 128
    for r, v in enumerate(rows):
        for h in range(halves):
            tmp[h, n * r : n * r + n, :] = v[:, 128 * h : 128 * h + 128]

    def load(leaf):
        return jnp.concatenate([tmp[h, pl.ds(leaf, 8, stride=n), :] for h in range(halves)], 1)

    return load


def two_halves(vals):
    v = vals * LN2
    high = v.astype(BF16).astype(F32)
    return jnp.concatenate([high, v - high], 0).astype(BF16)


def matern_over_ln2(t):
    m = jnp.maximum(t, 1e-12)
    s = m * lax.rsqrt(m)
    return (s + 1.0 / LN2) * jnp.exp2(-s)


def product(src_feat, tgt_feat, vals):
    t = jnp.dot(src_feat, tgt_feat, preferred_element_type=F32)
    k = matern_over_ln2(t)
    high = k.astype(BF16)
    low = (k - high.astype(F32)).astype(BF16)
    return jnp.dot(vals, high, preferred_element_type=F32) + jnp.dot(vals, low, preferred_element_type=F32)


def dot3(a, b, transposed=False):
    ah = a.astype(BF16).astype(F32)
    both = jnp.concatenate([ah, a - ah], 0).astype(BF16)
    bh = b.astype(BF16)
    bl = (b - bh.astype(F32)).astype(BF16)
    dims = (((1,), (1 if transposed else 0,)), ((), ()))
    r = lax.dot_general(both, bh, dims, preferred_element_type=F32)
    r = r + lax.dot_general(both, bl, dims, preferred_element_type=F32)
    return r[0:8] + r[8:16]


def fetch(pairs, sems):
    copies = [pltpu.make_async_copy(a, b, sems.at[i]) for i, (a, b) in enumerate(pairs)]
    for c in copies:
        c.start()
    return copies


def request_kernel(pts_h, chg_h, skel_h, cpts_h, llist_h, tlist_h, m0, first, last, row16, pts, chg, skel, cpts, llist, tlist, sems):
    ins = ((llist_h, llist), (tlist_h, tlist), (skel_h, skel), (cpts_h, cpts), (pts_h, pts), (chg_h, chg))
    copies = fetch(ins, sems)
    for c in copies[0:2]:
        c.wait()
    lane = lax.broadcasted_iota(jnp.int32, (1, 128), 1)
    sub8 = lax.broadcasted_iota(jnp.int32, (8, 128), 0)
    lane8 = lax.broadcasted_iota(jnp.int32, (8, 128), 1)
    row = lax.broadcasted_iota(jnp.int32, (128, 128), 0)
    col = lax.broadcasted_iota(jnp.int32, (128, 128), 1)
    before = (row < col).astype(F32).astype(BF16)
    pick = (lax.broadcasted_iota(jnp.int32, (16, 128), 0) == (lax.broadcasted_iota(jnp.int32, (16, 128), 1) & 15))
    pick = pick.astype(F32).astype(BF16)
    ll = llist[...]
    mine = sub8 == (lane8 >> 4)

    def flat(v):
        w = jnp.dot(v.astype(F32).astype(BF16), pick, preferred_element_type=F32)
        return jnp.sum(jnp.where(mine, w, 0.0), axis=0, keepdims=True).astype(jnp.int32)

    upper = flat(ll >> 6)
    lower = flat(ll & 63)
    row16[...] = jnp.zeros((8, 128), jnp.int32)
    row16[0:1, 0:16] = tlist[...]
    tl = row16[0:1, :]
    leaf_hit = (lower >> 3) == sub8
    top_hit = ((tl & 7) == sub8) & (lane < 16)
    leaf_one = leaf_hit.astype(F32)
    top_one = top_hit.astype(F32)
    leaf_pos = jnp.dot(leaf_one.astype(BF16), before, preferred_element_type=F32)
    top_pos = jnp.dot(top_one.astype(BF16), before, preferred_element_type=F32) + 16.0
    leaf_n = jnp.sum(leaf_one, axis=1, keepdims=True)
    top_n = jnp.sum(top_one, axis=1, keepdims=True)
    leaf_pos = jnp.where(leaf_hit, leaf_pos, -1.0)
    top_pos = jnp.where(top_hit, top_pos, -1.0)
    local = (lower & 7) + (upper & 7) * 8
    codes = jnp.where(sub8 == 0, lane >> 4, jnp.where(sub8 == 1, local, 0)).astype(F32).astype(BF16)
    tcodes = jnp.where(sub8 == 0, tl >> 3, 0).astype(F32).astype(BF16)
    rowf = row.astype(F32)
    for c in copies[2:6]:
        c.wait()
    for d in range(8):
        for c in range(3):
            m0[d, 8 * c : 8 * c + 8, :] = skel[c]
            m0[d, 24 + c : 25 + c, :] = cpts[c]
        m0[d, 29:32, :] = jnp.zeros((3, 128), F32)
        oh = (leaf_pos[d : d + 1] == rowf).astype(F32).astype(BF16)
        got = lax.dot_general(codes, oh, (((1,), (1,)), ((), ())), preferred_element_type=F32)
        m0[d, 27:28, :] = got[0:1] * 128.0 + got[1:2]
        oh = (top_pos[d : d + 1] == rowf).astype(F32).astype(BF16)
        got = lax.dot_general(tcodes, oh, (((1,), (1,)), ((), ())), preferred_element_type=F32)[0:1]
        got = got + jnp.where(lane == 0, leaf_n[d : d + 1], 0.0) + jnp.where(lane == 1, top_n[d : d + 1], 0.0)
        m0[d, 28:29, :] = got
    for slab, start in ((first, 0), (last, OWN - REACH)):
        for i in range(REACH):
            slab[8 * i : 8 * i + 8, :] = chg[start + i]
        for c in range(3):
            slab[32 + 4 * c : 36 + 4 * c, :] = pts[c, start : start + REACH, :]
        slab[44:48, :] = jnp.zeros((4, 256), F32)


def request(pts, chg, skel, cpts, llist, tlist):
    sd = jax.ShapeDtypeStruct
    return pl.pallas_call(
        request_kernel,
        in_specs=[HBM] * 6,
        out_specs=[VMEM] * 3,
        out_shape=[sd((8, 32, 128), F32), sd((48, 256), F32), sd((48, 256), F32)],
        scratch_shapes=[pltpu.VMEM((8, 128), jnp.int32)]
        + [pltpu.VMEM(a.shape, a.dtype) for a in (pts, chg, skel, cpts, llist, tlist)]
        + [pltpu.SemaphoreType.DMA((6,))],
        compiler_params=WIDE,
        name="request",
    )(pts, chg, skel, cpts, llist, tlist)


def weights_kernel(chg_h, up_h, skel_h, utm_h, cpts_h, m1, chg, up, skel, utm, cpts, slab, sems):
    ins = ((chg_h, chg), (up_h, up), (utm_h, utm), (skel_h, skel), (cpts_h, cpts))
    copies = fetch(ins, sems)
    slab[96:104, :] = jnp.zeros((8, 128), F32)
    for c in copies[3:5]:
        c.wait()
    for c in range(3):
        slab[64 + 8 * c : 72 + 8 * c, :] = skel[c]
        slab[96 + c : 97 + c, :] = cpts[c]
    copies[0].wait()
    copies[1].wait()
    own = [dot3(chg[l], up[l], True) for l in range(OWN)]
    for l in range(OWN):
        slab[8 * l : 8 * l + 8, :] = own[l]
    copies[2].wait()
    total = dot3(own[0], utm[0], True)
    for l in range(1, OWN):
        total = total + dot3(own[l], utm[l], True)
    slab[88:96, :] = total
    for c in fetch([(slab, m1.at[d]) for d in range(8)], sems):
        c.wait()


def weights(chg, up, skel, utm, cpts):
    return pl.pallas_call(
        weights_kernel,
        in_specs=[HBM] * 5,
        out_specs=HBM,
        out_shape=jax.ShapeDtypeStruct((8, 104, 128), F32),
        scratch_shapes=[pltpu.VMEM(a.shape, a.dtype) for a in (chg, up, skel, utm, cpts)]
        + [pltpu.VMEM((104, 128), F32), pltpu.SemaphoreType.DMA((8,))],
        cost_estimate=pl.CostEstimate(flops=50000000, bytes_accessed=8000000, transcendentals=0),
        compiler_params=WIDE,
        name="weights",
    )(chg, up, skel, utm, cpts)


def near_kernel(lo, hi, ids, pts, chg, before, after, out, fs, ft, vals, xyz, ts, tl):
    me = (lax.axis_index("g") * lax.axis_size("y") + lax.axis_index("y")) * lax.axis_size("z") + lax.axis_index("z")
    base = me * OWN - REACH
    for c in range(3):
        xyz[c, 0:4, :] = before[32 + 4 * c : 36 + 4 * c, :]
        xyz[c, 4:12, :] = pts[c]
        xyz[c, 12:16, :] = after[32 + 4 * c : 36 + 4 * c, :]
    s0, s1, t0, t1, t2 = dense_features([xyz[0], xyz[1], xyz[2]])
    s0 = spread(s0, ts)
    s1 = spread(s1, tl)
    for e in range(lo, hi + 2 * REACH):
        a, b = s0(e), s1(e)
        fs[e - lo] = jnp.concatenate([a, b, a, b], 0).T.astype(BF16)
        if e < REACH:
            c = before[8 * e : 8 * e + 8, :]
        elif e < REACH + OWN:
            c = chg[e - REACH]
        else:
            c = after[8 * (e - REACH - OWN) : 8 * (e - REACH - OWN) + 8, :]
        vals[e - lo] = two_halves(c)
    for i, rows in enumerate((t0, t2, t1, t1)):
        load = spread(rows, ts)
        for e in range(lo + REACH, hi + REACH):
            ft[e - REACH - lo, 8 * i : 8 * i + 8, :] = load(e)
    dead = hi - lo + 2 * REACH
    vals[dead] = jnp.zeros((16, 256), BF16)

    def leaf(i, carry):
        tgt = ft[i].astype(BF16)
        acc = jnp.zeros((16, 256), F32)
        for n in range(NBR):
            ident = ids[i + lo, n]
            live = ident >= 0
            e = jnp.where(live, ident - base - lo, 0)
            acc = acc + product(fs[e], tgt, vals[jnp.where(live, e, dead)])
        out[i] = acc[0:8] + acc[8:16]
        return carry

    lax.fori_loop(0, hi - lo, leaf, 0)


def near_part(lo, hi, ids, pts, chg, before, after):
    n = hi - lo
    return pl.pallas_call(
        functools.partial(near_kernel, lo, hi),
        in_specs=[SMEM] + [VMEM] * 4,
        out_specs=VMEM,
        out_shape=jax.ShapeDtypeStruct((n, 8, 256), F32),
        scratch_shapes=[
            pltpu.VMEM((n + 8, 256, FEAT), BF16),
            pltpu.VMEM((n, FEAT, 256), F32),
            pltpu.VMEM((n + 9, 16, 256), BF16),
            pltpu.VMEM((3, 16, 256), F32),
            pltpu.VMEM((2, 128, 128), F32),
            pltpu.VMEM((2, 128, 128), F32),
        ],
        cost_estimate=pl.CostEstimate(flops=n * 9 * 65536000, bytes_accessed=300000, transcendentals=n * 9 * 131072),
        compiler_params=PARAMS,
        name="near",
    )(ids, pts, chg, before, after)


def prepare_sources(i, xyz, t0, t1, feat):
    s0, s1, _, _, _ = dense_features(xyz)
    s0 = spread(s0, t0)
    s1 = spread(s1, t1)
    for l in range(8):
        feat[8 * i + l, 0:8, :] = s0(l)
        feat[8 * i + l, 8:16, :] = s1(l)


def prepare_targets(i, xyz, tmp, ft):
    _, _, t0, t1, t2 = dense_features(xyz)
    for j, rows in enumerate((t0, t2, t1, t1)):
        load = spread(rows, tmp.at[j])
        for l in range(8):
            ft[8 * i + l, 8 * j : 8 * j + 8, :] = load(l)


def flatten(req, flat, row, start, slot):
    off = 0
    for d in range(8):
        n = req[d, 1, slot]

        def copy(j, carry, d=d, off=off):
            for u in range(8):
                flat[off + j * 8 + u] = req[d, row, start + j * 8 + u] + d * (1024 if row == 0 else 128)
            return carry

        lax.fori_loop(0, (n + 7) // 8, copy, 0)
        off = off + n
    for u in range(2 * PAIRS):
        flat[off + u] = DUMMY
    return off


def interact(total, flat, fs, ft, vals, add):
    zero = jnp.zeros((FEAT, 128), BF16)

    def chunk(i, carry):
        for u in range(PAIRS):
            ca = flat[i * (2 * PAIRS) + 2 * u]
            cb = flat[i * (2 * PAIRS) + 2 * u + 1]
            ta, sa = ca >> 7, ca & 127
            tb, sb = cb >> 7, cb & 127
            fa = ft[ta].astype(BF16)
            fb = ft[tb].astype(BF16)
            tgt = jnp.concatenate([jnp.concatenate([fa, zero], 1), jnp.concatenate([zero, fb], 1)], 0)
            ra, rb = fs[sa], fs[sb]
            src = jnp.concatenate([ra, ra, rb, rb], 0).T.astype(BF16)
            r = product(src, tgt, jnp.concatenate([vals[sa], vals[sb]], 0))
            add(ta, r[0:8, 0:128] + r[8:16, 0:128])
            add(tb, r[16:24, 128:256] + r[24:32, 128:256])
        return carry

    lax.fori_loop(0, (total + 2 * PAIRS - 1) // (2 * PAIRS), chunk, 0)


def clear_dummy(fs, vals):
    fs[DUMMY] = jnp.zeros((16, 128), F32)
    vals[DUMMY] = jnp.zeros((16, 128), BF16)


def far_leaf_kernel(req, src, tgt, out, flat, fs, ft, vals, t0, t1, t2):
    for y in range(8):
        prepare_sources(y, [src[y, 64 + 8 * c : 72 + 8 * c, :] for c in range(3)], t0.at[y], t1.at[y], fs)
        prepare_targets(y, [tgt[32 * y + 8 * c : 32 * y + 8 * c + 8, :] for c in range(3)], t2.at[y], ft)
        for l in range(OWN):
            vals[8 * y + l] = two_halves(src[y, 8 * l : 8 * l + 8, :])
    clear_dummy(fs, vals)
    out[...] = jnp.zeros_like(out)
    total = flatten(req, flat, 0, 0, 0)

    def add(t, v):
        out[t >> 3, t & 7] += v

    interact(total, flat, fs, ft, vals, add)


FAR_SCRATCH = [
    pltpu.SMEM((1024 + 64,), jnp.int32),
    pltpu.VMEM((65, 16, 128), F32),
    pltpu.VMEM((64, FEAT, 128), F32),
    pltpu.VMEM((65, 16, 128), BF16),
    pltpu.VMEM((8, 1, 64, 128), F32),
    pltpu.VMEM((8, 1, 64, 128), F32),
    pltpu.VMEM((8, 4, 1, 64, 128), F32),
]


def far_leaf(req, src, tgt):
    return pl.pallas_call(
        far_leaf_kernel,
        in_specs=[SMEM, VMEM, VMEM],
        out_specs=VMEM,
        out_shape=jax.ShapeDtypeStruct((8, 9, 8, 128), F32),
        scratch_shapes=FAR_SCRATCH,
        cost_estimate=pl.CostEstimate(flops=2097152000, bytes_accessed=900000, transcendentals=4194304),
        compiler_params=PARAMS,
        name="far_leaf",
    )(req, src, tgt.reshape(256, 128))


def far_top_kernel(req, src, tgt, part, out, flat, fs, ft, vals, t0, t1, t2):
    for g in range(8):
        xyz = [src[pl.ds(128 * g + 8 + c, 8, stride=16), :] for c in range(3)]
        prepare_sources(g, xyz, t0.at[g], t1.at[g], fs)
        for y in range(8):
            vals[8 * g + y] = two_halves(src[128 * g + 16 * y : 128 * g + 16 * y + 8, :])
    prepare_targets(0, [tgt[pl.ds(24 + c, 8, stride=32), :] for c in range(3)], t2.at[0], ft)
    clear_dummy(fs, vals)
    out[...] = part[...]
    total = flatten(req, flat, 1, 16, 1)

    def add(t, v):
        out[t, 8] += v

    interact(total, flat, fs, ft, vals, add)


def far_top(req, src, tgt, part):
    return pl.pallas_call(
        far_top_kernel,
        in_specs=[SMEM, VMEM, VMEM, VMEM],
        out_specs=VMEM,
        out_shape=jax.ShapeDtypeStruct((8, 9, 8, 128), F32),
        scratch_shapes=FAR_SCRATCH,
        compiler_params=PARAMS,
        name="far_top",
    )(req, src.reshape(1024, 128), tgt.reshape(256, 128), part)


def final_kernel(got, utm, up, near1, near2, out):
    tot = got[0]
    for d in range(1, 8):
        tot = tot + got[d]
    cell = tot[8]
    half = near1.shape[0]
    for l in range(OWN):
        incoming = tot[l] + dot3(cell, utm[l])
        near = near1[l] if l < half else near2[l - half]
        out[l] = near + dot3(incoming, up[l])


def final(got, utm, up, near1, near2):
    return pl.pallas_call(
        final_kernel,
        in_specs=[VMEM] * 5,
        out_specs=VMEM,
        out_shape=jax.ShapeDtypeStruct((8, 8, 256), F32),
        compiler_params=PARAMS,
        name="final",
    )(got, utm, up, near1, near2)


def body(points, charges, up_op, skel_pts, utm, cell_pts, near_list, leaf_list, top_list):
    every = ("g", "y", "z")
    pts = jnp.transpose(points, (1, 0, 2))
    skel = jnp.transpose(skel_pts, (1, 0, 2))
    cpts = jnp.transpose(cell_pts, (1, 0, 2))
    count = lax.axis_size("g") * lax.axis_size("y") * lax.axis_size("z")
    up = [(i, i + 1) for i in range(count - 1)]
    down = [(i + 1, i) for i in range(count - 1)]
    m0, first, last = request(pts, charges, skel, cpts, leaf_list, top_list)
    got0 = lax.all_to_all(m0, "z", 0, 0, tiled=True)
    before = lax.ppermute(last, every, up)
    after = lax.ppermute(first, every, down)
    m1 = weights(charges, up_op, skel, utm, cpts)
    m1, got0, before, after = lax.optimization_barrier((m1, got0, before, after))
    got1 = lax.all_to_all(m1, "y", 0, 0, tiled=True)
    req = got0[:, 27:29, :].astype(jnp.int32)
    near1 = near_part(0, 4, near_list, pts, charges, before, after)
    got1, near1 = lax.optimization_barrier((got1, near1))
    cells = jnp.broadcast_to(got1[:, 88:104, :].reshape(1, 128, 128), (8, 128, 128))
    gotg = lax.all_to_all(cells, "g", 0, 0, tiled=True)
    part = far_leaf(req, got1, got0)
    part = far_top(req, gotg, got0, part)
    part, charges2 = lax.optimization_barrier((part, charges))
    gotr = lax.all_to_all(part, "z", 0, 0, tiled=True)
    near2 = near_part(4, 8, near_list, pts, charges2, before, after)
    return final(gotr, utm, up_op, near1, near2)


def solution(mesh):
    fine = Mesh(mesh.devices.reshape(mesh.shape["group"], 8, 8), ("g", "y", "z"))
    row = ("g", "y", "z")
    specs = tuple(P(row, *([None] * k)) for k in (2, 2, 2, 2, 2, 2, 1, 1, 1))
    return jax.shard_map(body, mesh=fine, in_specs=specs, out_specs=P(row, None, None), check_vma=False)
```

```python
import functools
import math

import jax
import jax.numpy as jnp
from jax import lax
from jax.experimental import pallas as pl
from jax.experimental.pallas import tpu as pltpu
from jax.sharding import Mesh, PartitionSpec as P

F32 = jnp.float32
BF16 = jnp.bfloat16
KAPPA = math.sqrt(3.0) * math.log2(math.e)
LN2 = math.log(2.0)
CENTER = 1.5
FEAT = 32
REACH = 4
OWN = 8
NBR = 9
PAIRS = 8
DUMMY = 64
CHUNK = 8
EARLY = 32
NEAR_DUMMY = 16

SMEM = pl.BlockSpec(memory_space=pltpu.SMEM)
HBM = pl.BlockSpec(memory_space=pltpu.HBM)
VMEM = pl.BlockSpec(memory_space=pltpu.VMEM)
PARAMS = pltpu.CompilerParams(vmem_limit_bytes=40 << 20)
WIDE = pltpu.CompilerParams(vmem_limit_bytes=60 << 20)


def split2(x):
    a = x.astype(BF16).astype(F32)
    return a, (x - a).astype(BF16).astype(F32)


def split3(x):
    a = x.astype(BF16).astype(F32)
    b, c = split2(x - a)
    return a, b, c


def dense_features(xyz):
    parts = [split2((x - CENTER) * KAPPA) for x in xyz]
    n = None
    for a, b in parts:
        r = a + b
        n = r * r if n is None else n + r * r
    n1, n2, n3 = split3(n)
    one = jnp.ones_like(n)
    zero = jnp.zeros_like(n)
    high = [a for a, _ in parts]
    low = [b for _, b in parts]
    high2 = [-2.0 * a for a in high]
    low2 = [-2.0 * b for b in low]
    s0 = high + [n1, n2, n3, one, one]
    s1 = low + [one, zero, zero, zero, zero]
    t0 = high2 + [one, one, one, n1, n2]
    t1 = low2 + [zero] * 5
    t2 = high2 + [n3] + [zero] * 4
    return s0, s1, t0, t1, t2


def spread(rows, tmp):
    n, width = rows[0].shape
    halves = width // 128
    for r, v in enumerate(rows):
        for h in range(halves):
            tmp[h, n * r : n * r + n, :] = v[:, 128 * h : 128 * h + 128]

    def load(leaf):
        return jnp.concatenate([tmp[h, pl.ds(leaf, 8, stride=n), :] for h in range(halves)], 1)

    return load


def two_halves(vals):
    v = vals * LN2
    high = v.astype(BF16).astype(F32)
    return jnp.concatenate([high, v - high], 0).astype(BF16)


def matern_over_ln2(t):
    m = jnp.maximum(t, 1e-12)
    s = m * lax.rsqrt(m)
    return (s + 1.0 / LN2) * jnp.exp2(-s)


def product(src_feat, tgt_feat, vals):
    t = jnp.dot(src_feat, tgt_feat, preferred_element_type=F32)
    k = matern_over_ln2(t)
    high = k.astype(BF16)
    low = (k - high.astype(F32)).astype(BF16)
    return jnp.dot(vals, high, preferred_element_type=F32) + jnp.dot(vals, low, preferred_element_type=F32)


def dot3(a, b, transposed=False):
    ah = a.astype(BF16).astype(F32)
    both = jnp.concatenate([ah, a - ah], 0).astype(BF16)
    bh = b.astype(BF16)
    bl = (b - bh.astype(F32)).astype(BF16)
    dims = (((1,), (1 if transposed else 0,)), ((), ()))
    r = lax.dot_general(both, bh, dims, preferred_element_type=F32)
    r = r + lax.dot_general(both, bl, dims, preferred_element_type=F32)
    return r[0:8] + r[8:16]


def fetch(pairs, sems):
    copies = [pltpu.make_async_copy(a, b, sems.at[i]) for i, (a, b) in enumerate(pairs)]
    for c in copies:
        c.start()
    return copies


def request_kernel(pts_h, chg_h, skel_h, cpts_h, llist_h, tlist_h, m0, first, last, row16, pts, chg, skel, cpts, llist, tlist, sems):
    ins = ((llist_h, llist), (tlist_h, tlist), (skel_h, skel), (cpts_h, cpts), (pts_h, pts), (chg_h, chg))
    copies = fetch(ins, sems)
    for c in copies[0:2]:
        c.wait()
    lane = lax.broadcasted_iota(jnp.int32, (1, 128), 1)
    sub8 = lax.broadcasted_iota(jnp.int32, (8, 128), 0)
    lane8 = lax.broadcasted_iota(jnp.int32, (8, 128), 1)
    row = lax.broadcasted_iota(jnp.int32, (128, 128), 0)
    col = lax.broadcasted_iota(jnp.int32, (128, 128), 1)
    before = (row < col).astype(F32).astype(BF16)
    pick = (lax.broadcasted_iota(jnp.int32, (16, 128), 0) == (lax.broadcasted_iota(jnp.int32, (16, 128), 1) & 15))
    pick = pick.astype(F32).astype(BF16)
    ll = llist[...]
    mine = sub8 == (lane8 >> 4)

    def flat(v):
        w = jnp.dot(v.astype(F32).astype(BF16), pick, preferred_element_type=F32)
        return jnp.sum(jnp.where(mine, w, 0.0), axis=0, keepdims=True).astype(jnp.int32)

    upper = flat(ll >> 6)
    lower = flat(ll & 63)
    row16[...] = jnp.zeros((8, 128), jnp.int32)
    row16[0:1, 0:16] = tlist[...]
    tl = row16[0:1, :]
    leaf_hit = (lower >> 3) == sub8
    top_hit = ((tl & 7) == sub8) & (lane < 16)
    leaf_one = leaf_hit.astype(F32)
    top_one = top_hit.astype(F32)
    leaf_pos = jnp.dot(leaf_one.astype(BF16), before, preferred_element_type=F32)
    top_pos = jnp.dot(top_one.astype(BF16), before, preferred_element_type=F32) + 16.0
    leaf_n = jnp.sum(leaf_one, axis=1, keepdims=True)
    top_n = jnp.sum(top_one, axis=1, keepdims=True)
    leaf_pos = jnp.where(leaf_hit, leaf_pos, -1.0)
    top_pos = jnp.where(top_hit, top_pos, -1.0)
    local = (lower & 7) + (upper & 7) * 8
    codes = jnp.where(sub8 == 0, lane >> 4, jnp.where(sub8 == 1, local, 0)).astype(F32).astype(BF16)
    tcodes = jnp.where(sub8 == 0, tl >> 3, 0).astype(F32).astype(BF16)
    rowf = row.astype(F32)
    for c in copies[2:6]:
        c.wait()
    for d in range(8):
        for c in range(3):
            m0[d, 8 * c : 8 * c + 8, :] = skel[c]
            m0[d, 24 + c : 25 + c, :] = cpts[c]
        m0[d, 29:32, :] = jnp.zeros((3, 128), F32)
        oh = (leaf_pos[d : d + 1] == rowf).astype(F32).astype(BF16)
        got = lax.dot_general(codes, oh, (((1,), (1,)), ((), ())), preferred_element_type=F32)
        m0[d, 27:28, :] = got[0:1] * 128.0 + got[1:2]
        oh = (top_pos[d : d + 1] == rowf).astype(F32).astype(BF16)
        got = lax.dot_general(tcodes, oh, (((1,), (1,)), ((), ())), preferred_element_type=F32)[0:1]
        got = got + jnp.where(lane == 0, leaf_n[d : d + 1], 0.0) + jnp.where(lane == 1, top_n[d : d + 1], 0.0)
        m0[d, 28:29, :] = got
    for slab, start in ((first, 0), (last, OWN - REACH)):
        for i in range(REACH):
            slab[8 * i : 8 * i + 8, :] = chg[start + i]
        for c in range(3):
            slab[32 + 4 * c : 36 + 4 * c, :] = pts[c, start : start + REACH, :]
        slab[44:48, :] = jnp.zeros((4, 256), F32)


def request(pts, chg, skel, cpts, llist, tlist):
    sd = jax.ShapeDtypeStruct
    return pl.pallas_call(
        request_kernel,
        in_specs=[HBM] * 6,
        out_specs=[VMEM] * 3,
        out_shape=[sd((8, 32, 128), F32), sd((48, 256), F32), sd((48, 256), F32)],
        scratch_shapes=[pltpu.VMEM((8, 128), jnp.int32)]
        + [pltpu.VMEM(a.shape, a.dtype) for a in (pts, chg, skel, cpts, llist, tlist)]
        + [pltpu.SemaphoreType.DMA((6,))],
        compiler_params=WIDE,
        name="request",
    )(pts, chg, skel, cpts, llist, tlist)


def weights_kernel(chg_h, up_h, skel_h, utm_h, cpts_h, m1, chg, up, skel, utm, cpts, slab, sems):
    ins = ((chg_h, chg), (up_h, up), (utm_h, utm), (skel_h, skel), (cpts_h, cpts))
    copies = fetch(ins, sems)
    slab[96:104, :] = jnp.zeros((8, 128), F32)
    for c in copies[3:5]:
        c.wait()
    for c in range(3):
        slab[64 + 8 * c : 72 + 8 * c, :] = skel[c]
        slab[96 + c : 97 + c, :] = cpts[c]
    copies[0].wait()
    copies[1].wait()
    own = [dot3(chg[l], up[l], True) for l in range(OWN)]
    for l in range(OWN):
        slab[8 * l : 8 * l + 8, :] = own[l]
    copies[2].wait()
    total = dot3(own[0], utm[0], True)
    for l in range(1, OWN):
        total = total + dot3(own[l], utm[l], True)
    slab[88:96, :] = total
    for c in fetch([(slab, m1.at[d]) for d in range(8)], sems):
        c.wait()


def weights(chg, up, skel, utm, cpts):
    return pl.pallas_call(
        weights_kernel,
        in_specs=[HBM] * 5,
        out_specs=HBM,
        out_shape=jax.ShapeDtypeStruct((8, 104, 128), F32),
        scratch_shapes=[pltpu.VMEM(a.shape, a.dtype) for a in (chg, up, skel, utm, cpts)]
        + [pltpu.VMEM((104, 128), F32), pltpu.SemaphoreType.DMA((8,))],
        cost_estimate=pl.CostEstimate(flops=50000000, bytes_accessed=8000000, transcendentals=0),
        compiler_params=WIDE,
        name="weights",
    )(chg, up, skel, utm, cpts)


def near_blocks(ids, flat, base, early):
    pos = jnp.int32(0)
    seen = jnp.int32(0)
    for l in range(OWN):
        for n in range(NBR):
            ident = ids[l, n]
            e = ident - base
            own = (e >= REACH) & (e < REACH + OWN)
            first = own & (seen < EARLY)
            flat[pos] = l * 32 + e
            take = first if early else (ident >= 0) & jnp.logical_not(first)
            pos = pos + take.astype(jnp.int32)
            seen = seen + own.astype(jnp.int32)
    for u in range(CHUNK):
        flat[pos + u] = NEAR_DUMMY
    return pos


def near_setup(sources, xyz, vals_of, fs, ft, vals, ts, tl):
    s0, s1, t0, t1, t2 = dense_features(xyz)
    load0, load1 = spread(s0, ts.at[0]), spread(s1, tl)
    for e in sources:
        a, b = load0(e), load1(e)
        fs[e] = jnp.concatenate([a, b, a, b], 0).T.astype(BF16)
        vals[e] = two_halves(vals_of(e))
    vals[NEAR_DUMMY] = jnp.zeros((16, 256), BF16)
    fs[NEAR_DUMMY] = jnp.zeros((256, FEAT), BF16)
    load0, load1, load2 = spread(t0, ts.at[1]), spread(t1, ts.at[2]), spread(t2, ts.at[3])
    for l in range(OWN):
        e = l + REACH
        one = load1(e)
        ft[l, 0:16, :] = jnp.concatenate([load0(e), load2(e)], 0).astype(BF16)
        ft[l, 16:32, :] = jnp.concatenate([one, one], 0).astype(BF16)


def near_run(count, flat, out, fs, ft, vals):
    out[...] = jnp.zeros_like(out)

    def chunk(i, carry):
        for u in range(CHUNK):
            code = flat[i * CHUNK + u]
            l, e = code >> 5, code & 31
            r = product(fs[e], ft[l], vals[e])
            out[l] += r[0:8] + r[8:16]
        return carry

    lax.fori_loop(0, (count + CHUNK - 1) // CHUNK, chunk, 0)


def near_base():
    me = (lax.axis_index("g") * lax.axis_size("y") + lax.axis_index("y")) * lax.axis_size("z") + lax.axis_index("z")
    return me * OWN - REACH


def near_early_kernel(ids, pts, chg, out, flat, fs, ft, vals, xyz, ts, tl):
    count = near_blocks(ids, flat, near_base(), True)
    for c in range(3):
        xyz[c] = jnp.zeros((16, 256), F32)
        xyz[c, 4:12, :] = pts[c]
    own = range(REACH, REACH + OWN)
    near_setup(own, [xyz[0], xyz[1], xyz[2]], lambda e: chg[e - REACH], fs, ft, vals, ts, tl)
    near_run(count, flat, out, fs, ft, vals)


def near_late_kernel(ids, pts, chg, before, after, out, flat, fs, ft, vals, xyz, ts, tl):
    count = near_blocks(ids, flat, near_base(), False)
    for c in range(3):
        xyz[c, 0:4, :] = before[32 + 4 * c : 36 + 4 * c, :]
        xyz[c, 4:12, :] = pts[c]
        xyz[c, 12:16, :] = after[32 + 4 * c : 36 + 4 * c, :]

    def vals_of(e):
        if e < REACH:
            return before[8 * e : 8 * e + 8, :]
        if e < REACH + OWN:
            return chg[e - REACH]
        return after[8 * (e - REACH - OWN) : 8 * (e - REACH - OWN) + 8, :]

    near_setup(range(16), [xyz[0], xyz[1], xyz[2]], vals_of, fs, ft, vals, ts, tl)
    near_run(count, flat, out, fs, ft, vals)


def near_part(early, *args):
    return pl.pallas_call(
        near_early_kernel if early else near_late_kernel,
        in_specs=[SMEM] + [VMEM] * (len(args) - 1),
        out_specs=VMEM,
        out_shape=jax.ShapeDtypeStruct((OWN, 8, 256), F32),
        scratch_shapes=[
            pltpu.SMEM((OWN * NBR + CHUNK + 8,), jnp.int32),
            pltpu.VMEM((17, 256, FEAT), BF16),
            pltpu.VMEM((OWN, FEAT, 256), BF16),
            pltpu.VMEM((17, 16, 256), BF16),
            pltpu.VMEM((3, 16, 256), F32),
            pltpu.VMEM((4, 2, 128, 128), F32),
            pltpu.VMEM((2, 128, 128), F32),
        ],
        cost_estimate=pl.CostEstimate(flops=2000000000, bytes_accessed=300000, transcendentals=4194304),
        compiler_params=PARAMS,
        name="near",
    )(*args)


def prepare_sources(i, xyz, t0, t1, feat):
    s0, s1, _, _, _ = dense_features(xyz)
    s0 = spread(s0, t0)
    s1 = spread(s1, t1)
    for l in range(8):
        feat[8 * i + l, 0:8, :] = s0(l)
        feat[8 * i + l, 8:16, :] = s1(l)


def prepare_targets(i, xyz, tmp, ft):
    _, _, t0, t1, t2 = dense_features(xyz)
    load0, load1, load2 = spread(t0, tmp.at[0]), spread(t1, tmp.at[1]), spread(t2, tmp.at[2])
    for l in range(8):
        one = load1(l)
        ft[8 * i + l, 0:16, :] = jnp.concatenate([load0(l), load2(l)], 0).astype(BF16)
        ft[8 * i + l, 16:32, :] = jnp.concatenate([one, one], 0).astype(BF16)


def flatten(req, flat, row, start, slot):
    off = 0
    for d in range(8):
        n = req[d, 1, slot]

        def copy(j, carry, d=d, off=off):
            for u in range(8):
                flat[off + j * 8 + u] = req[d, row, start + j * 8 + u] + d * (1024 if row == 0 else 128)
            return carry

        lax.fori_loop(0, (n + 7) // 8, copy, 0)
        off = off + n
    for u in range(2 * PAIRS):
        flat[off + u] = DUMMY
    return off


def interact(total, flat, fs, ft, vals, add):
    zero = jnp.zeros((FEAT, 128), BF16)

    def chunk(i, carry):
        for u in range(PAIRS):
            ca = flat[i * (2 * PAIRS) + 2 * u]
            cb = flat[i * (2 * PAIRS) + 2 * u + 1]
            ta, sa = ca >> 7, ca & 127
            tb, sb = cb >> 7, cb & 127
            fa = ft[ta]
            fb = ft[tb]
            tgt = jnp.concatenate([jnp.concatenate([fa, zero], 1), jnp.concatenate([zero, fb], 1)], 0)
            ra, rb = fs[sa], fs[sb]
            src = jnp.concatenate([ra, ra, rb, rb], 0).T.astype(BF16)
            r = product(src, tgt, jnp.concatenate([vals[sa], vals[sb]], 0))
            add(ta, r[0:8, 0:128] + r[8:16, 0:128])
            add(tb, r[16:24, 128:256] + r[24:32, 128:256])
        return carry

    lax.fori_loop(0, (total + 2 * PAIRS - 1) // (2 * PAIRS), chunk, 0)


def clear_dummy(fs, vals):
    fs[DUMMY] = jnp.zeros((16, 128), F32)
    vals[DUMMY] = jnp.zeros((16, 128), BF16)


def far_leaf_kernel(req, src, tgt, out, flat, fs, ft, vals, t0, t1, t2):
    for y in range(8):
        prepare_sources(y, [src[y, 64 + 8 * c : 72 + 8 * c, :] for c in range(3)], t0.at[y], t1.at[y], fs)
        prepare_targets(y, [tgt[32 * y + 8 * c : 32 * y + 8 * c + 8, :] for c in range(3)], t2.at[y], ft)
        for l in range(OWN):
            vals[8 * y + l] = two_halves(src[y, 8 * l : 8 * l + 8, :])
    clear_dummy(fs, vals)
    out[...] = jnp.zeros_like(out)
    total = flatten(req, flat, 0, 0, 0)

    def add(t, v):
        out[t >> 3, t & 7] += v

    interact(total, flat, fs, ft, vals, add)


FAR_SCRATCH = [
    pltpu.SMEM((1024 + 64,), jnp.int32),
    pltpu.VMEM((65, 16, 128), F32),
    pltpu.VMEM((64, FEAT, 128), BF16),
    pltpu.VMEM((65, 16, 128), BF16),
    pltpu.VMEM((8, 1, 64, 128), F32),
    pltpu.VMEM((8, 1, 64, 128), F32),
    pltpu.VMEM((8, 3, 1, 64, 128), F32),
]


def far_leaf(req, src, tgt):
    return pl.pallas_call(
        far_leaf_kernel,
        in_specs=[SMEM, VMEM, VMEM],
        out_specs=VMEM,
        out_shape=jax.ShapeDtypeStruct((8, 9, 8, 128), F32),
        scratch_shapes=FAR_SCRATCH,
        cost_estimate=pl.CostEstimate(flops=2097152000, bytes_accessed=900000, transcendentals=4194304),
        compiler_params=PARAMS,
        name="far_leaf",
    )(req, src, tgt.reshape(256, 128))


def far_top_kernel(req, src, tgt, part, out, flat, fs, ft, vals, t0, t1, t2):
    for g in range(8):
        xyz = [src[pl.ds(128 * g + 8 + c, 8, stride=16), :] for c in range(3)]
        prepare_sources(g, xyz, t0.at[g], t1.at[g], fs)
        for y in range(8):
            vals[8 * g + y] = two_halves(src[128 * g + 16 * y : 128 * g + 16 * y + 8, :])
    prepare_targets(0, [tgt[pl.ds(24 + c, 8, stride=32), :] for c in range(3)], t2.at[0], ft)
    clear_dummy(fs, vals)
    out[...] = part[...]
    total = flatten(req, flat, 1, 16, 1)

    def add(t, v):
        out[t, 8] += v

    interact(total, flat, fs, ft, vals, add)


def far_top(req, src, tgt, part):
    return pl.pallas_call(
        far_top_kernel,
        in_specs=[SMEM, VMEM, VMEM, VMEM],
        out_specs=VMEM,
        out_shape=jax.ShapeDtypeStruct((8, 9, 8, 128), F32),
        scratch_shapes=FAR_SCRATCH,
        compiler_params=PARAMS,
        name="far_top",
    )(req, src.reshape(1024, 128), tgt.reshape(256, 128), part)


def final_kernel(got, utm, up, near1, near2, out):
    tot = got[0]
    for d in range(1, 8):
        tot = tot + got[d]
    cell = tot[8]
    for l in range(OWN):
        incoming = tot[l] + dot3(cell, utm[l])
        out[l] = near1[l] + near2[l] + dot3(incoming, up[l])


def final(got, utm, up, near1, near2):
    return pl.pallas_call(
        final_kernel,
        in_specs=[VMEM] * 5,
        out_specs=VMEM,
        out_shape=jax.ShapeDtypeStruct((8, 8, 256), F32),
        compiler_params=PARAMS,
        name="final",
    )(got, utm, up, near1, near2)


def body(points, charges, up_op, skel_pts, utm, cell_pts, near_list, leaf_list, top_list):
    every = ("g", "y", "z")
    pts = jnp.transpose(points, (1, 0, 2))
    skel = jnp.transpose(skel_pts, (1, 0, 2))
    cpts = jnp.transpose(cell_pts, (1, 0, 2))
    count = lax.axis_size("g") * lax.axis_size("y") * lax.axis_size("z")
    up = [(i, i + 1) for i in range(count - 1)]
    down = [(i + 1, i) for i in range(count - 1)]
    m0, first, last = request(pts, charges, skel, cpts, leaf_list, top_list)
    got0 = lax.all_to_all(m0, "z", 0, 0, tiled=True)
    m1 = weights(charges, up_op, skel, utm, cpts)
    m1, got0 = lax.optimization_barrier((m1, got0))
    got1 = lax.all_to_all(m1, "y", 0, 0, tiled=True)
    req = got0[:, 27:29, :].astype(jnp.int32)
    near1 = near_part(True, near_list, pts, charges)
    near1, first, last = lax.optimization_barrier((near1, first, last))
    before = lax.ppermute(last, every, up)
    after = lax.ppermute(first, every, down)
    got1, near1, before, after = lax.optimization_barrier((got1, near1, before, after))
    cells = jnp.broadcast_to(got1[:, 88:104, :].reshape(1, 128, 128), (8, 128, 128))
    gotg = lax.all_to_all(cells, "g", 0, 0, tiled=True)
    part = far_leaf(req, got1, got0)
    part = far_top(req, gotg, got0, part)
    part, charges2 = lax.optimization_barrier((part, charges))
    gotr = lax.all_to_all(part, "z", 0, 0, tiled=True)
    near2 = near_part(False, near_list, pts, charges2, before, after)
    return final(gotr, utm, up_op, near1, near2)


def solution(mesh):
    fine = Mesh(mesh.devices.reshape(mesh.shape["group"], 8, 8), ("g", "y", "z"))
    row = ("g", "y", "z")
    specs = tuple(P(row, *([None] * k)) for k in (2, 2, 2, 2, 2, 2, 1, 1, 1))
    return jax.shard_map(body, mesh=fine, in_specs=specs, out_specs=P(row, None, None), check_vma=False)
```

```python
import functools
import math

import jax
import jax.numpy as jnp
from jax import lax
from jax.experimental import pallas as pl
from jax.experimental.pallas import tpu as pltpu
from jax.sharding import Mesh, PartitionSpec as P

F32 = jnp.float32
BF16 = jnp.bfloat16
KAPPA = math.sqrt(3.0) * math.log2(math.e)
LN2 = math.log(2.0)
CENTER = 1.5
FEAT = 32
REACH = 4
OWN = 8
NBR = 9
PAIRS = 8
DUMMY = 64
CHUNK = 8
EARLY = 48
NEAR_DUMMY = 16

SMEM = pl.BlockSpec(memory_space=pltpu.SMEM)
HBM = pl.BlockSpec(memory_space=pltpu.HBM)
VMEM = pl.BlockSpec(memory_space=pltpu.VMEM)
PARAMS = pltpu.CompilerParams(vmem_limit_bytes=40 << 20)
WIDE = pltpu.CompilerParams(vmem_limit_bytes=60 << 20)


def split2(x):
    a = x.astype(BF16).astype(F32)
    return a, (x - a).astype(BF16).astype(F32)


def split3(x):
    a = x.astype(BF16).astype(F32)
    b, c = split2(x - a)
    return a, b, c


def dense_features(xyz):
    parts = [split2((x - CENTER) * KAPPA) for x in xyz]
    n = None
    for a, b in parts:
        r = a + b
        n = r * r if n is None else n + r * r
    n1, n2, n3 = split3(n)
    one = jnp.ones_like(n)
    zero = jnp.zeros_like(n)
    high = [a for a, _ in parts]
    low = [b for _, b in parts]
    high2 = [-2.0 * a for a in high]
    low2 = [-2.0 * b for b in low]
    s0 = high + [n1, n2, n3, one, one]
    s1 = low + [one, zero, zero, zero, zero]
    t0 = high2 + [one, one, one, n1, n2]
    t1 = low2 + [zero] * 5
    t2 = high2 + [n3] + [zero] * 4
    return s0, s1, t0, t1, t2


def spread(rows, tmp):
    n, width = rows[0].shape
    halves = width // 128
    for r, v in enumerate(rows):
        for h in range(halves):
            tmp[h, n * r : n * r + n, :] = v[:, 128 * h : 128 * h + 128]

    def load(leaf):
        return jnp.concatenate([tmp[h, pl.ds(leaf, 8, stride=n), :] for h in range(halves)], 1)

    return load


def two_halves(vals):
    v = vals * LN2
    high = v.astype(BF16).astype(F32)
    return jnp.concatenate([high, v - high], 0).astype(BF16)


def matern_over_ln2(t):
    m = jnp.maximum(t, 1e-12)
    s = m * lax.rsqrt(m)
    return (s + 1.0 / LN2) * jnp.exp2(-s)


def product(src_feat, tgt_feat, vals):
    t = jnp.dot(src_feat, tgt_feat, preferred_element_type=F32)
    k = matern_over_ln2(t)
    high = k.astype(BF16)
    low = (k - high.astype(F32)).astype(BF16)
    return jnp.dot(vals, high, preferred_element_type=F32) + jnp.dot(vals, low, preferred_element_type=F32)


def dot3(a, b, transposed=False):
    ah = a.astype(BF16).astype(F32)
    both = jnp.concatenate([ah, a - ah], 0).astype(BF16)
    bh = b.astype(BF16)
    bl = (b - bh.astype(F32)).astype(BF16)
    dims = (((1,), (1 if transposed else 0,)), ((), ()))
    r = lax.dot_general(both, bh, dims, preferred_element_type=F32)
    r = r + lax.dot_general(both, bl, dims, preferred_element_type=F32)
    return r[0:8] + r[8:16]


def fetch(pairs, sems):
    copies = [pltpu.make_async_copy(a, b, sems.at[i]) for i, (a, b) in enumerate(pairs)]
    for c in copies:
        c.start()
    return copies


def request_kernel(pts_h, chg_h, skel_h, cpts_h, llist_h, tlist_h, m0, first, last, row16, pts, chg, skel, cpts, llist, tlist, sems):
    ins = ((llist_h, llist), (tlist_h, tlist), (skel_h, skel), (cpts_h, cpts), (pts_h, pts), (chg_h, chg))
    copies = fetch(ins, sems)
    for c in copies[0:2]:
        c.wait()
    lane = lax.broadcasted_iota(jnp.int32, (1, 128), 1)
    sub8 = lax.broadcasted_iota(jnp.int32, (8, 128), 0)
    lane8 = lax.broadcasted_iota(jnp.int32, (8, 128), 1)
    row = lax.broadcasted_iota(jnp.int32, (128, 128), 0)
    col = lax.broadcasted_iota(jnp.int32, (128, 128), 1)
    before = (row < col).astype(F32).astype(BF16)
    pick = (lax.broadcasted_iota(jnp.int32, (16, 128), 0) == (lax.broadcasted_iota(jnp.int32, (16, 128), 1) & 15))
    pick = pick.astype(F32).astype(BF16)
    ll = llist[...]
    mine = sub8 == (lane8 >> 4)

    def flat(v):
        w = jnp.dot(v.astype(F32).astype(BF16), pick, preferred_element_type=F32)
        return jnp.sum(jnp.where(mine, w, 0.0), axis=0, keepdims=True).astype(jnp.int32)

    upper = flat(ll >> 6)
    lower = flat(ll & 63)
    row16[...] = jnp.zeros((8, 128), jnp.int32)
    row16[0:1, 0:16] = tlist[...]
    tl = row16[0:1, :]
    leaf_hit = (lower >> 3) == sub8
    top_hit = ((tl & 7) == sub8) & (lane < 16)
    leaf_one = leaf_hit.astype(F32)
    top_one = top_hit.astype(F32)
    leaf_pos = jnp.dot(leaf_one.astype(BF16), before, preferred_element_type=F32)
    top_pos = jnp.dot(top_one.astype(BF16), before, preferred_element_type=F32) + 16.0
    leaf_n = jnp.sum(leaf_one, axis=1, keepdims=True)
    top_n = jnp.sum(top_one, axis=1, keepdims=True)
    leaf_pos = jnp.where(leaf_hit, leaf_pos, -1.0)
    top_pos = jnp.where(top_hit, top_pos, -1.0)
    local = (lower & 7) + (upper & 7) * 8
    codes = jnp.where(sub8 == 0, lane >> 4, jnp.where(sub8 == 1, local, 0)).astype(F32).astype(BF16)
    tcodes = jnp.where(sub8 == 0, tl >> 3, 0).astype(F32).astype(BF16)
    rowf = row.astype(F32)
    for c in copies[2:6]:
        c.wait()
    for d in range(8):
        for c in range(3):
            m0[d, 8 * c : 8 * c + 8, :] = skel[c]
            m0[d, 24 + c : 25 + c, :] = cpts[c]
        m0[d, 29:32, :] = jnp.zeros((3, 128), F32)
        oh = (leaf_pos[d : d + 1] == rowf).astype(F32).astype(BF16)
        got = lax.dot_general(codes, oh, (((1,), (1,)), ((), ())), preferred_element_type=F32)
        m0[d, 27:28, :] = got[0:1] * 128.0 + got[1:2]
        oh = (top_pos[d : d + 1] == rowf).astype(F32).astype(BF16)
        got = lax.dot_general(tcodes, oh, (((1,), (1,)), ((), ())), preferred_element_type=F32)[0:1]
        got = got + jnp.where(lane == 0, leaf_n[d : d + 1], 0.0) + jnp.where(lane == 1, top_n[d : d + 1], 0.0)
        m0[d, 28:29, :] = got
    for slab, start in ((first, 0), (last, OWN - REACH)):
        for i in range(REACH):
            slab[8 * i : 8 * i + 8, :] = chg[start + i]
        for c in range(3):
            slab[32 + 4 * c : 36 + 4 * c, :] = pts[c, start : start + REACH, :]
        slab[44:48, :] = jnp.zeros((4, 256), F32)


def request(pts, chg, skel, cpts, llist, tlist):
    sd = jax.ShapeDtypeStruct
    return pl.pallas_call(
        request_kernel,
        in_specs=[HBM] * 6,
        out_specs=[VMEM] * 3,
        out_shape=[sd((8, 32, 128), F32), sd((48, 256), F32), sd((48, 256), F32)],
        scratch_shapes=[pltpu.VMEM((8, 128), jnp.int32)]
        + [pltpu.VMEM(a.shape, a.dtype) for a in (pts, chg, skel, cpts, llist, tlist)]
        + [pltpu.SemaphoreType.DMA((6,))],
        compiler_params=WIDE,
        name="request",
    )(pts, chg, skel, cpts, llist, tlist)


def weights_kernel(chg_h, up_h, skel_h, utm_h, cpts_h, m1, chg, up, skel, utm, cpts, slab, sems):
    ins = ((chg_h, chg), (up_h, up), (utm_h, utm), (skel_h, skel), (cpts_h, cpts))
    copies = fetch(ins, sems)
    slab[96:104, :] = jnp.zeros((8, 128), F32)
    for c in copies[3:5]:
        c.wait()
    for c in range(3):
        slab[64 + 8 * c : 72 + 8 * c, :] = skel[c]
        slab[96 + c : 97 + c, :] = cpts[c]
    copies[0].wait()
    copies[1].wait()
    own = [dot3(chg[l], up[l], True) for l in range(OWN)]
    for l in range(OWN):
        slab[8 * l : 8 * l + 8, :] = own[l]
    copies[2].wait()
    total = dot3(own[0], utm[0], True)
    for l in range(1, OWN):
        total = total + dot3(own[l], utm[l], True)
    slab[88:96, :] = total
    for c in fetch([(slab, m1.at[d]) for d in range(8)], sems):
        c.wait()


def weights(chg, up, skel, utm, cpts):
    return pl.pallas_call(
        weights_kernel,
        in_specs=[HBM] * 5,
        out_specs=HBM,
        out_shape=jax.ShapeDtypeStruct((8, 104, 128), F32),
        scratch_shapes=[pltpu.VMEM(a.shape, a.dtype) for a in (chg, up, skel, utm, cpts)]
        + [pltpu.VMEM((104, 128), F32), pltpu.SemaphoreType.DMA((8,))],
        cost_estimate=pl.CostEstimate(flops=50000000, bytes_accessed=8000000, transcendentals=0),
        compiler_params=WIDE,
        name="weights",
    )(chg, up, skel, utm, cpts)


def near_blocks(ids, flat, base, early):
    pos = jnp.int32(0)
    seen = jnp.int32(0)
    for l in range(OWN):
        for n in range(NBR):
            ident = ids[l, n]
            e = ident - base
            own = (e >= REACH) & (e < REACH + OWN)
            first = own & (seen < EARLY)
            flat[pos] = l * 32 + e
            take = first if early else (ident >= 0) & jnp.logical_not(first)
            pos = pos + take.astype(jnp.int32)
            seen = seen + own.astype(jnp.int32)
    for u in range(CHUNK):
        flat[pos + u] = NEAR_DUMMY
    return pos


def near_setup(sources, xyz, vals_of, fs, ft, vals, ts, tl):
    s0, s1, t0, t1, t2 = dense_features(xyz)
    load0, load1 = spread(s0, ts.at[0]), spread(s1, tl)
    for e in sources:
        a, b = load0(e), load1(e)
        fs[e] = jnp.concatenate([a, b, a, b], 0).T.astype(BF16)
        vals[e] = two_halves(vals_of(e))
    vals[NEAR_DUMMY] = jnp.zeros((16, 256), BF16)
    fs[NEAR_DUMMY] = jnp.zeros((256, FEAT), BF16)
    load0, load1, load2 = spread(t0, ts.at[1]), spread(t1, ts.at[2]), spread(t2, ts.at[3])
    for l in range(OWN):
        e = l + REACH
        one = load1(e)
        ft[l, 0:16, :] = jnp.concatenate([load0(e), load2(e)], 0).astype(BF16)
        ft[l, 16:32, :] = jnp.concatenate([one, one], 0).astype(BF16)


def near_run(count, flat, out, fs, ft, vals):
    out[...] = jnp.zeros_like(out)

    def chunk(i, carry):
        for u in range(CHUNK):
            code = flat[i * CHUNK + u]
            l, e = code >> 5, code & 31
            r = product(fs[e], ft[l], vals[e])
            out[l] += r[0:8] + r[8:16]
        return carry

    lax.fori_loop(0, (count + CHUNK - 1) // CHUNK, chunk, 0)


def near_base():
    me = (lax.axis_index("g") * lax.axis_size("y") + lax.axis_index("y")) * lax.axis_size("z") + lax.axis_index("z")
    return me * OWN - REACH


def near_early_kernel(ids, pts, chg, out, flat, fs, ft, vals, xyz, ts, tl):
    count = near_blocks(ids, flat, near_base(), True)
    for c in range(3):
        xyz[c] = jnp.zeros((16, 256), F32)
        xyz[c, 4:12, :] = pts[c]
    own = range(REACH, REACH + OWN)
    near_setup(own, [xyz[0], xyz[1], xyz[2]], lambda e: chg[e - REACH], fs, ft, vals, ts, tl)
    near_run(count, flat, out, fs, ft, vals)


def near_late_kernel(ids, pts, chg, before, after, out, flat, fs, ft, vals, xyz, ts, tl):
    count = near_blocks(ids, flat, near_base(), False)
    for c in range(3):
        xyz[c, 0:4, :] = before[32 + 4 * c : 36 + 4 * c, :]
        xyz[c, 4:12, :] = pts[c]
        xyz[c, 12:16, :] = after[32 + 4 * c : 36 + 4 * c, :]

    def vals_of(e):
        if e < REACH:
            return before[8 * e : 8 * e + 8, :]
        if e < REACH + OWN:
            return chg[e - REACH]
        return after[8 * (e - REACH - OWN) : 8 * (e - REACH - OWN) + 8, :]

    near_setup(range(16), [xyz[0], xyz[1], xyz[2]], vals_of, fs, ft, vals, ts, tl)
    near_run(count, flat, out, fs, ft, vals)


def near_part(early, *args):
    return pl.pallas_call(
        near_early_kernel if early else near_late_kernel,
        in_specs=[SMEM] + [VMEM] * (len(args) - 1),
        out_specs=VMEM,
        out_shape=jax.ShapeDtypeStruct((OWN, 8, 256), F32),
        scratch_shapes=[
            pltpu.SMEM((OWN * NBR + CHUNK + 8,), jnp.int32),
            pltpu.VMEM((17, 256, FEAT), BF16),
            pltpu.VMEM((OWN, FEAT, 256), BF16),
            pltpu.VMEM((17, 16, 256), BF16),
            pltpu.VMEM((3, 16, 256), F32),
            pltpu.VMEM((4, 2, 128, 128), F32),
            pltpu.VMEM((2, 128, 128), F32),
        ],
        cost_estimate=pl.CostEstimate(flops=2000000000, bytes_accessed=300000, transcendentals=4194304),
        compiler_params=PARAMS,
        name="near",
    )(*args)


def prepare_sources(i, xyz, t0, t1, feat):
    s0, s1, _, _, _ = dense_features(xyz)
    s0 = spread(s0, t0)
    s1 = spread(s1, t1)
    for l in range(8):
        feat[8 * i + l, 0:8, :] = s0(l)
        feat[8 * i + l, 8:16, :] = s1(l)


def prepare_targets(i, xyz, tmp, ft):
    _, _, t0, t1, t2 = dense_features(xyz)
    load0, load1, load2 = spread(t0, tmp.at[0]), spread(t1, tmp.at[1]), spread(t2, tmp.at[2])
    for l in range(8):
        one = load1(l)
        ft[8 * i + l, 0:16, :] = jnp.concatenate([load0(l), load2(l)], 0).astype(BF16)
        ft[8 * i + l, 16:32, :] = jnp.concatenate([one, one], 0).astype(BF16)


def flatten(req, flat, row, start, slot):
    off = 0
    for d in range(8):
        n = req[d, 1, slot]

        def copy(j, carry, d=d, off=off):
            for u in range(8):
                flat[off + j * 8 + u] = req[d, row, start + j * 8 + u] + d * (1024 if row == 0 else 128)
            return carry

        lax.fori_loop(0, (n + 7) // 8, copy, 0)
        off = off + n
    for u in range(2 * PAIRS):
        flat[off + u] = DUMMY
    return off


def interact(total, flat, fs, ft, vals, add):
    zero = jnp.zeros((FEAT, 128), BF16)

    def chunk(i, carry):
        for u in range(PAIRS):
            ca = flat[i * (2 * PAIRS) + 2 * u]
            cb = flat[i * (2 * PAIRS) + 2 * u + 1]
            ta, sa = ca >> 7, ca & 127
            tb, sb = cb >> 7, cb & 127
            fa = ft[ta]
            fb = ft[tb]
            tgt = jnp.concatenate([jnp.concatenate([fa, zero], 1), jnp.concatenate([zero, fb], 1)], 0)
            ra, rb = fs[sa], fs[sb]
            src = jnp.concatenate([ra, ra, rb, rb], 0).T.astype(BF16)
            r = product(src, tgt, jnp.concatenate([vals[sa], vals[sb]], 0))
            add(ta, r[0:8, 0:128] + r[8:16, 0:128])
            add(tb, r[16:24, 128:256] + r[24:32, 128:256])
        return carry

    lax.fori_loop(0, (total + 2 * PAIRS - 1) // (2 * PAIRS), chunk, 0)


def clear_dummy(fs, vals):
    fs[DUMMY] = jnp.zeros((16, 128), F32)
    vals[DUMMY] = jnp.zeros((16, 128), BF16)


def far_prep_kernel(req, tgt, ft, ftop, leaf_flat, top_flat, counts, tmp):
    for d in range(8):
        prepare_targets(d, [tgt[32 * d + 8 * c : 32 * d + 8 * c + 8, :] for c in range(3)], tmp.at[d], ft)
    prepare_targets(0, [tgt[pl.ds(24 + c, 8, stride=32), :] for c in range(3)], tmp.at[8], ftop)
    counts[0] = flatten(req, leaf_flat, 0, 0, 0)
    counts[1] = flatten(req, top_flat, 1, 16, 1)


def far_prep(req, tgt):
    sd = jax.ShapeDtypeStruct
    return pl.pallas_call(
        far_prep_kernel,
        in_specs=[SMEM, VMEM],
        out_specs=[VMEM, VMEM, SMEM, SMEM, SMEM],
        out_shape=[
            sd((64, FEAT, 128), BF16),
            sd((8, FEAT, 128), BF16),
            sd((1024 + 64,), jnp.int32),
            sd((256,), jnp.int32),
            sd((2,), jnp.int32),
        ],
        scratch_shapes=[pltpu.VMEM((9, 3, 1, 64, 128), F32)],
        cost_estimate=pl.CostEstimate(flops=100000000, bytes_accessed=900000, transcendentals=0),
        compiler_params=PARAMS,
        name="far_prep",
    )(req, tgt.reshape(256, 128))


def far_leaf_kernel(counts, flat, src, ft, out, fs, vals, t0, t1):
    for y in range(8):
        prepare_sources(y, [src[y, 64 + 8 * c : 72 + 8 * c, :] for c in range(3)], t0.at[y], t1.at[y], fs)
        for l in range(OWN):
            vals[8 * y + l] = two_halves(src[y, 8 * l : 8 * l + 8, :])
    clear_dummy(fs, vals)
    out[...] = jnp.zeros_like(out)

    def add(t, v):
        out[t >> 3, t & 7] += v

    interact(counts[0], flat, fs, ft, vals, add)


FAR_SCRATCH = [
    pltpu.VMEM((65, 16, 128), F32),
    pltpu.VMEM((65, 16, 128), BF16),
    pltpu.VMEM((8, 1, 64, 128), F32),
    pltpu.VMEM((8, 1, 64, 128), F32),
]


def far_leaf(counts, flat, src, ft):
    return pl.pallas_call(
        far_leaf_kernel,
        in_specs=[SMEM, SMEM, VMEM, VMEM],
        out_specs=VMEM,
        out_shape=jax.ShapeDtypeStruct((8, 9, 8, 128), F32),
        scratch_shapes=FAR_SCRATCH,
        cost_estimate=pl.CostEstimate(flops=2097152000, bytes_accessed=900000, transcendentals=4194304),
        compiler_params=PARAMS,
        name="far_leaf",
    )(counts, flat, src, ft)


def far_top_kernel(counts, flat, src, ft, part, out, fs, vals, t0, t1):
    for g in range(8):
        xyz = [src[pl.ds(128 * g + 8 + c, 8, stride=16), :] for c in range(3)]
        prepare_sources(g, xyz, t0.at[g], t1.at[g], fs)
        for y in range(8):
            vals[8 * g + y] = two_halves(src[128 * g + 16 * y : 128 * g + 16 * y + 8, :])
    clear_dummy(fs, vals)
    out[...] = part[...]

    def add(t, v):
        out[t, 8] += v

    interact(counts[1], flat, fs, ft, vals, add)


def far_top(counts, flat, src, ft, part):
    return pl.pallas_call(
        far_top_kernel,
        in_specs=[SMEM, SMEM, VMEM, VMEM, VMEM],
        out_specs=VMEM,
        out_shape=jax.ShapeDtypeStruct((8, 9, 8, 128), F32),
        scratch_shapes=FAR_SCRATCH,
        compiler_params=PARAMS,
        name="far_top",
    )(counts, flat, src.reshape(1024, 128), ft, part)


def final_kernel(got, utm, up, near1, near2, out):
    tot = got[0]
    for d in range(1, 8):
        tot = tot + got[d]
    cell = tot[8]
    for l in range(OWN):
        incoming = tot[l] + dot3(cell, utm[l])
        out[l] = near1[l] + near2[l] + dot3(incoming, up[l])


def final(got, utm, up, near1, near2):
    return pl.pallas_call(
        final_kernel,
        in_specs=[VMEM] * 5,
        out_specs=VMEM,
        out_shape=jax.ShapeDtypeStruct((8, 8, 256), F32),
        compiler_params=PARAMS,
        name="final",
    )(got, utm, up, near1, near2)


def body(points, charges, up_op, skel_pts, utm, cell_pts, near_list, leaf_list, top_list):
    every = ("g", "y", "z")
    pts = jnp.transpose(points, (1, 0, 2))
    skel = jnp.transpose(skel_pts, (1, 0, 2))
    cpts = jnp.transpose(cell_pts, (1, 0, 2))
    count = lax.axis_size("g") * lax.axis_size("y") * lax.axis_size("z")
    up = [(i, i + 1) for i in range(count - 1)]
    down = [(i + 1, i) for i in range(count - 1)]
    m0, first, last = request(pts, charges, skel, cpts, leaf_list, top_list)
    got0 = lax.all_to_all(m0, "z", 0, 0, tiled=True)
    m1 = weights(charges, up_op, skel, utm, cpts)
    m1, got0 = lax.optimization_barrier((m1, got0))
    got1 = lax.all_to_all(m1, "y", 0, 0, tiled=True)
    req = got0[:, 27:29, :].astype(jnp.int32)
    ft, ftop, leaf_flat, top_flat, counts = far_prep(req, got0)
    near1 = near_part(True, near_list, pts, charges)
    got1, near1, ft, counts = lax.optimization_barrier((got1, near1, ft, counts))
    cells = jnp.broadcast_to(got1[:, 88:104, :].reshape(1, 128, 128), (8, 128, 128))
    gotg = lax.all_to_all(cells, "g", 0, 0, tiled=True)
    part = far_leaf(counts, leaf_flat, got1, ft)
    part = far_top(counts, top_flat, gotg, ftop, part)
    part, first, last = lax.optimization_barrier((part, first, last))
    gotr = lax.all_to_all(part, "z", 0, 0, tiled=True)
    before = lax.ppermute(last, every, up)
    after = lax.ppermute(first, every, down)
    near2 = near_part(False, near_list, pts, charges, before, after)
    return final(gotr, utm, up_op, near1, near2)


def solution(mesh):
    fine = Mesh(mesh.devices.reshape(mesh.shape["group"], 8, 8), ("g", "y", "z"))
    row = ("g", "y", "z")
    specs = tuple(P(row, *([None] * k)) for k in (2, 2, 2, 2, 2, 2, 1, 1, 1))
    return jax.shard_map(body, mesh=fine, in_specs=specs, out_specs=P(row, None, None), check_vma=False)
```

```python
import functools
import math

import jax
import jax.numpy as jnp
from jax import lax
from jax.experimental import pallas as pl
from jax.experimental.pallas import tpu as pltpu
from jax.sharding import Mesh, PartitionSpec as P

F32 = jnp.float32
BF16 = jnp.bfloat16
KAPPA = math.sqrt(3.0) * math.log2(math.e)
LN2 = math.log(2.0)
CENTER = 1.5
FEAT = 32
REACH = 4
OWN = 8
NBR = 9
PAIRS = 8
DUMMY = 64
CHUNK = 8
NEAR_DUMMY = 16

SMEM = pl.BlockSpec(memory_space=pltpu.SMEM)
HBM = pl.BlockSpec(memory_space=pltpu.HBM)
VMEM = pl.BlockSpec(memory_space=pltpu.VMEM)
PARAMS = pltpu.CompilerParams(vmem_limit_bytes=40 << 20)
WIDE = pltpu.CompilerParams(vmem_limit_bytes=60 << 20)


def split2(x):
    a = x.astype(BF16).astype(F32)
    return a, (x - a).astype(BF16).astype(F32)


def split3(x):
    a = x.astype(BF16).astype(F32)
    b, c = split2(x - a)
    return a, b, c


def dense_features(xyz):
    parts = [split2((x - CENTER) * KAPPA) for x in xyz]
    n = None
    for a, b in parts:
        r = a + b
        n = r * r if n is None else n + r * r
    n1, n2, n3 = split3(n)
    one = jnp.ones_like(n)
    zero = jnp.zeros_like(n)
    high = [a for a, _ in parts]
    low = [b for _, b in parts]
    high2 = [-2.0 * a for a in high]
    low2 = [-2.0 * b for b in low]
    s0 = high + [n1, n2, n3, one, one]
    s1 = low + [one, zero, zero, zero, zero]
    t0 = high2 + [one, one, one, n1, n2]
    t1 = low2 + [zero] * 5
    t2 = high2 + [n3] + [zero] * 4
    return s0, s1, t0, t1, t2


def spread(rows, tmp):
    n, width = rows[0].shape
    halves = width // 128
    for r, v in enumerate(rows):
        for h in range(halves):
            tmp[h, n * r : n * r + n, :] = v[:, 128 * h : 128 * h + 128]

    def load(leaf):
        return jnp.concatenate([tmp[h, pl.ds(leaf, 8, stride=n), :] for h in range(halves)], 1)

    return load


def two_halves(vals):
    v = vals * LN2
    high = v.astype(BF16).astype(F32)
    return jnp.concatenate([high, v - high], 0).astype(BF16)


def matern_over_ln2(t):
    m = jnp.maximum(t, 1e-12)
    s = m * lax.rsqrt(m)
    return (s + 1.0 / LN2) * jnp.exp2(-s)


def product(src_feat, tgt_feat, vals):
    t = jnp.dot(src_feat, tgt_feat, preferred_element_type=F32)
    k = matern_over_ln2(t)
    high = k.astype(BF16)
    low = (k - high.astype(F32)).astype(BF16)
    return jnp.dot(vals, high, preferred_element_type=F32) + jnp.dot(vals, low, preferred_element_type=F32)


def dot3(a, b, transposed=False):
    ah = a.astype(BF16).astype(F32)
    both = jnp.concatenate([ah, a - ah], 0).astype(BF16)
    bh = b.astype(BF16)
    bl = (b - bh.astype(F32)).astype(BF16)
    dims = (((1,), (1 if transposed else 0,)), ((), ()))
    r = lax.dot_general(both, bh, dims, preferred_element_type=F32)
    r = r + lax.dot_general(both, bl, dims, preferred_element_type=F32)
    return r[0:8] + r[8:16]


def fetch(pairs, sems):
    copies = [pltpu.make_async_copy(a, b, sems.at[i]) for i, (a, b) in enumerate(pairs)]
    for c in copies:
        c.start()
    return copies


def request_kernel(pts_h, chg_h, skel_h, cpts_h, llist_h, tlist_h, m0, first, last, row16, pts, chg, skel, cpts, llist, tlist, sems):
    ins = ((llist_h, llist), (tlist_h, tlist), (skel_h, skel), (cpts_h, cpts), (pts_h, pts), (chg_h, chg))
    copies = fetch(ins, sems)
    for c in copies[0:2]:
        c.wait()
    lane = lax.broadcasted_iota(jnp.int32, (1, 128), 1)
    sub8 = lax.broadcasted_iota(jnp.int32, (8, 128), 0)
    lane8 = lax.broadcasted_iota(jnp.int32, (8, 128), 1)
    row = lax.broadcasted_iota(jnp.int32, (128, 128), 0)
    col = lax.broadcasted_iota(jnp.int32, (128, 128), 1)
    before = (row < col).astype(F32).astype(BF16)
    pick = (lax.broadcasted_iota(jnp.int32, (16, 128), 0) == (lax.broadcasted_iota(jnp.int32, (16, 128), 1) & 15))
    pick = pick.astype(F32).astype(BF16)
    ll = llist[...]
    mine = sub8 == (lane8 >> 4)

    def flat(v):
        w = jnp.dot(v.astype(F32).astype(BF16), pick, preferred_element_type=F32)
        return jnp.sum(jnp.where(mine, w, 0.0), axis=0, keepdims=True).astype(jnp.int32)

    upper = flat(ll >> 6)
    lower = flat(ll & 63)
    row16[...] = jnp.zeros((8, 128), jnp.int32)
    row16[0:1, 0:16] = tlist[...]
    tl = row16[0:1, :]
    leaf_hit = (lower >> 3) == sub8
    top_hit = ((tl & 7) == sub8) & (lane < 16)
    leaf_one = leaf_hit.astype(F32)
    top_one = top_hit.astype(F32)
    leaf_pos = jnp.dot(leaf_one.astype(BF16), before, preferred_element_type=F32)
    top_pos = jnp.dot(top_one.astype(BF16), before, preferred_element_type=F32) + 16.0
    leaf_n = jnp.sum(leaf_one, axis=1, keepdims=True)
    top_n = jnp.sum(top_one, axis=1, keepdims=True)
    leaf_pos = jnp.where(leaf_hit, leaf_pos, -1.0)
    top_pos = jnp.where(top_hit, top_pos, -1.0)
    local = (lower & 7) + (upper & 7) * 8
    codes = jnp.where(sub8 == 0, lane >> 4, jnp.where(sub8 == 1, local, 0)).astype(F32).astype(BF16)
    tcodes = jnp.where(sub8 == 0, tl >> 3, 0).astype(F32).astype(BF16)
    rowf = row.astype(F32)
    for c in copies[2:6]:
        c.wait()
    for d in range(8):
        for c in range(3):
            m0[d, 8 * c : 8 * c + 8, :] = skel[c]
            m0[d, 24 + c : 25 + c, :] = cpts[c]
        m0[d, 29:32, :] = jnp.zeros((3, 128), F32)
        oh = (leaf_pos[d : d + 1] == rowf).astype(F32).astype(BF16)
        got = lax.dot_general(codes, oh, (((1,), (1,)), ((), ())), preferred_element_type=F32)
        m0[d, 27:28, :] = got[0:1] * 128.0 + got[1:2]
        oh = (top_pos[d : d + 1] == rowf).astype(F32).astype(BF16)
        got = lax.dot_general(tcodes, oh, (((1,), (1,)), ((), ())), preferred_element_type=F32)[0:1]
        got = got + jnp.where(lane == 0, leaf_n[d : d + 1], 0.0) + jnp.where(lane == 1, top_n[d : d + 1], 0.0)
        m0[d, 28:29, :] = got
    for slab, start in ((first, 0), (last, OWN - REACH)):
        for i in range(REACH):
            slab[8 * i : 8 * i + 8, :] = chg[start + i]
        for c in range(3):
            slab[32 + 4 * c : 36 + 4 * c, :] = pts[c, start : start + REACH, :]
        slab[44:48, :] = jnp.zeros((4, 256), F32)


def request(pts, chg, skel, cpts, llist, tlist):
    sd = jax.ShapeDtypeStruct
    return pl.pallas_call(
        request_kernel,
        in_specs=[HBM] * 6,
        out_specs=[VMEM] * 3,
        out_shape=[sd((8, 32, 128), F32), sd((48, 256), F32), sd((48, 256), F32)],
        scratch_shapes=[pltpu.VMEM((8, 128), jnp.int32)]
        + [pltpu.VMEM(a.shape, a.dtype) for a in (pts, chg, skel, cpts, llist, tlist)]
        + [pltpu.SemaphoreType.DMA((6,))],
        compiler_params=WIDE,
        name="request",
    )(pts, chg, skel, cpts, llist, tlist)


def weights_kernel(chg_h, up_h, skel_h, utm_h, cpts_h, m1, chg, up, skel, utm, cpts, slab, sems):
    ins = ((chg_h, chg), (up_h, up), (utm_h, utm), (skel_h, skel), (cpts_h, cpts))
    copies = fetch(ins, sems)
    slab[96:104, :] = jnp.zeros((8, 128), F32)
    for c in copies[3:5]:
        c.wait()
    for c in range(3):
        slab[64 + 8 * c : 72 + 8 * c, :] = skel[c]
        slab[96 + c : 97 + c, :] = cpts[c]
    copies[0].wait()
    copies[1].wait()
    own = [dot3(chg[l], up[l], True) for l in range(OWN)]
    for l in range(OWN):
        slab[8 * l : 8 * l + 8, :] = own[l]
    copies[2].wait()
    total = dot3(own[0], utm[0], True)
    for l in range(1, OWN):
        total = total + dot3(own[l], utm[l], True)
    slab[88:96, :] = total
    for c in fetch([(slab, m1.at[d]) for d in range(8)], sems):
        c.wait()


def weights(chg, up, skel, utm, cpts):
    return pl.pallas_call(
        weights_kernel,
        in_specs=[HBM] * 5,
        out_specs=HBM,
        out_shape=jax.ShapeDtypeStruct((8, 104, 128), F32),
        scratch_shapes=[pltpu.VMEM(a.shape, a.dtype) for a in (chg, up, skel, utm, cpts)]
        + [pltpu.VMEM((104, 128), F32), pltpu.SemaphoreType.DMA((8,))],
        cost_estimate=pl.CostEstimate(flops=50000000, bytes_accessed=8000000, transcendentals=0),
        compiler_params=WIDE,
        name="weights",
    )(chg, up, skel, utm, cpts)


def near_blocks(ids, flat, base, first_leaf, early):
    pos = jnp.int32(0)
    for l in range(first_leaf, OWN):
        for n in range(NBR):
            ident = ids[l, n]
            e = ident - base
            flat[pos] = l * 32 + e
            take = (ident >= 0) & (e < REACH + OWN) if early else e >= REACH + OWN
            pos = pos + take.astype(jnp.int32)
    for u in range(CHUNK):
        flat[pos + u] = (OWN - 1) * 32 + NEAR_DUMMY
    return pos


def near_setup(sources, leaves, xyz, vals_of, fs, ft, vals, ts, tl):
    s0, s1, t0, t1, t2 = dense_features(xyz)
    load0, load1 = spread(s0, ts.at[0]), spread(s1, tl)
    for e in sources:
        a, b = load0(e), load1(e)
        fs[e] = jnp.concatenate([a, b, a, b], 0).T.astype(BF16)
        vals[e] = two_halves(vals_of(e))
    vals[NEAR_DUMMY] = jnp.zeros((16, 256), BF16)
    fs[NEAR_DUMMY] = jnp.zeros((256, FEAT), BF16)
    load0, load1, load2 = spread(t0, ts.at[1]), spread(t1, ts.at[2]), spread(t2, ts.at[3])
    for l in leaves:
        e = l + REACH
        one = load1(e)
        ft[l, 0:16, :] = jnp.concatenate([load0(e), load2(e)], 0).astype(BF16)
        ft[l, 16:32, :] = jnp.concatenate([one, one], 0).astype(BF16)


def near_run(count, flat, out, fs, ft, vals):
    out[...] = jnp.zeros_like(out)

    def chunk(i, carry):
        for u in range(CHUNK):
            code = flat[i * CHUNK + u]
            l, e = code >> 5, code & 31
            r = product(fs[e], ft[l], vals[e])
            out[l] += r[0:8] + r[8:16]
        return carry

    lax.fori_loop(0, (count + CHUNK - 1) // CHUNK, chunk, 0)


def near_base():
    me = (lax.axis_index("g") * lax.axis_size("y") + lax.axis_index("y")) * lax.axis_size("z") + lax.axis_index("z")
    return me * OWN - REACH


def near_early_kernel(ids, pts, chg, before, out, flat, fs, ft, vals, xyz, ts, tl):
    count = near_blocks(ids, flat, near_base(), 0, True)
    for c in range(3):
        xyz[c, 0:4, :] = before[32 + 4 * c : 36 + 4 * c, :]
        xyz[c, 4:12, :] = pts[c]
        xyz[c, 12:16, :] = jnp.zeros((4, 256), F32)

    def vals_of(e):
        return before[8 * e : 8 * e + 8, :] if e < REACH else chg[e - REACH]

    near_setup(range(REACH + OWN), range(OWN), [xyz[0], xyz[1], xyz[2]], vals_of, fs, ft, vals, ts, tl)
    near_run(count, flat, out, fs, ft, vals)


def near_late_kernel(ids, pts, after, out, flat, fs, ft, vals, xyz, ts, tl):
    count = near_blocks(ids, flat, near_base(), OWN - REACH, False)
    for c in range(3):
        xyz[c, 0:4, :] = jnp.zeros((4, 256), F32)
        xyz[c, 4:12, :] = pts[c]
        xyz[c, 12:16, :] = after[32 + 4 * c : 36 + 4 * c, :]

    def vals_of(e):
        return after[8 * (e - REACH - OWN) : 8 * (e - REACH - OWN) + 8, :]

    halo = range(REACH + OWN, 2 * REACH + OWN)
    near_setup(halo, range(OWN - REACH, OWN), [xyz[0], xyz[1], xyz[2]], vals_of, fs, ft, vals, ts, tl)
    near_run(count, flat, out, fs, ft, vals)


def near_part(early, *args):
    return pl.pallas_call(
        near_early_kernel if early else near_late_kernel,
        in_specs=[SMEM] + [VMEM] * (len(args) - 1),
        out_specs=VMEM,
        out_shape=jax.ShapeDtypeStruct((OWN, 8, 256), F32),
        scratch_shapes=[
            pltpu.SMEM((OWN * NBR + CHUNK + 8,), jnp.int32),
            pltpu.VMEM((17, 256, FEAT), BF16),
            pltpu.VMEM((OWN, FEAT, 256), BF16),
            pltpu.VMEM((17, 16, 256), BF16),
            pltpu.VMEM((3, 16, 256), F32),
            pltpu.VMEM((4, 2, 128, 128), F32),
            pltpu.VMEM((2, 128, 128), F32),
        ],
        cost_estimate=pl.CostEstimate(flops=2000000000, bytes_accessed=300000, transcendentals=4194304),
        compiler_params=PARAMS,
        name="near",
    )(*args)


def prepare_sources(i, xyz, t0, t1, feat):
    s0, s1, _, _, _ = dense_features(xyz)
    s0 = spread(s0, t0)
    s1 = spread(s1, t1)
    for l in range(8):
        feat[8 * i + l, 0:8, :] = s0(l)
        feat[8 * i + l, 8:16, :] = s1(l)


def prepare_targets(i, xyz, tmp, ft):
    _, _, t0, t1, t2 = dense_features(xyz)
    load0, load1, load2 = spread(t0, tmp.at[0]), spread(t1, tmp.at[1]), spread(t2, tmp.at[2])
    for l in range(8):
        one = load1(l)
        ft[8 * i + l, 0:16, :] = jnp.concatenate([load0(l), load2(l)], 0).astype(BF16)
        ft[8 * i + l, 16:32, :] = jnp.concatenate([one, one], 0).astype(BF16)


def flatten(req, flat, row, start, slot):
    off = 0
    for d in range(8):
        n = req[d, 1, slot]

        def copy(j, carry, d=d, off=off):
            for u in range(8):
                flat[off + j * 8 + u] = req[d, row, start + j * 8 + u] + d * (1024 if row == 0 else 128)
            return carry

        lax.fori_loop(0, (n + 7) // 8, copy, 0)
        off = off + n
    for u in range(2 * PAIRS):
        flat[off + u] = DUMMY
    return off


def interact(total, flat, fs, ft, vals, add):
    zero = jnp.zeros((FEAT, 128), BF16)

    def chunk(i, carry):
        for u in range(PAIRS):
            ca = flat[i * (2 * PAIRS) + 2 * u]
            cb = flat[i * (2 * PAIRS) + 2 * u + 1]
            ta, sa = ca >> 7, ca & 127
            tb, sb = cb >> 7, cb & 127
            fa = ft[ta]
            fb = ft[tb]
            tgt = jnp.concatenate([jnp.concatenate([fa, zero], 1), jnp.concatenate([zero, fb], 1)], 0)
            ra, rb = fs[sa], fs[sb]
            src = jnp.concatenate([ra, ra, rb, rb], 0).T.astype(BF16)
            r = product(src, tgt, jnp.concatenate([vals[sa], vals[sb]], 0))
            add(ta, r[0:8, 0:128] + r[8:16, 0:128])
            add(tb, r[16:24, 128:256] + r[24:32, 128:256])
        return carry

    lax.fori_loop(0, (total + 2 * PAIRS - 1) // (2 * PAIRS), chunk, 0)


def clear_dummy(fs, vals):
    fs[DUMMY] = jnp.zeros((16, 128), F32)
    vals[DUMMY] = jnp.zeros((16, 128), BF16)


def far_prep_kernel(req, tgt, ft, ftop, leaf_flat, top_flat, counts, tmp):
    for d in range(8):
        prepare_targets(d, [tgt[32 * d + 8 * c : 32 * d + 8 * c + 8, :] for c in range(3)], tmp.at[d], ft)
    prepare_targets(0, [tgt[pl.ds(24 + c, 8, stride=32), :] for c in range(3)], tmp.at[8], ftop)
    counts[0] = flatten(req, leaf_flat, 0, 0, 0)
    counts[1] = flatten(req, top_flat, 1, 16, 1)


def far_prep(req, tgt):
    sd = jax.ShapeDtypeStruct
    return pl.pallas_call(
        far_prep_kernel,
        in_specs=[SMEM, VMEM],
        out_specs=[VMEM, VMEM, SMEM, SMEM, SMEM],
        out_shape=[
            sd((64, FEAT, 128), BF16),
            sd((8, FEAT, 128), BF16),
            sd((1024 + 64,), jnp.int32),
            sd((256,), jnp.int32),
            sd((2,), jnp.int32),
        ],
        scratch_shapes=[pltpu.VMEM((9, 3, 1, 64, 128), F32)],
        cost_estimate=pl.CostEstimate(flops=100000000, bytes_accessed=900000, transcendentals=0),
        compiler_params=PARAMS,
        name="far_prep",
    )(req, tgt.reshape(256, 128))


def far_leaf_kernel(counts, flat, src, ft, out, fs, vals, t0, t1):
    for y in range(8):
        prepare_sources(y, [src[y, 64 + 8 * c : 72 + 8 * c, :] for c in range(3)], t0.at[y], t1.at[y], fs)
        for l in range(OWN):
            vals[8 * y + l] = two_halves(src[y, 8 * l : 8 * l + 8, :])
    clear_dummy(fs, vals)
    out[...] = jnp.zeros_like(out)

    def add(t, v):
        out[t >> 3, t & 7] += v

    interact(counts[0], flat, fs, ft, vals, add)


FAR_SCRATCH = [
    pltpu.VMEM((65, 16, 128), F32),
    pltpu.VMEM((65, 16, 128), BF16),
    pltpu.VMEM((8, 1, 64, 128), F32),
    pltpu.VMEM((8, 1, 64, 128), F32),
]


def far_leaf(counts, flat, src, ft):
    return pl.pallas_call(
        far_leaf_kernel,
        in_specs=[SMEM, SMEM, VMEM, VMEM],
        out_specs=VMEM,
        out_shape=jax.ShapeDtypeStruct((8, 9, 8, 128), F32),
        scratch_shapes=FAR_SCRATCH,
        cost_estimate=pl.CostEstimate(flops=2097152000, bytes_accessed=900000, transcendentals=4194304),
        compiler_params=PARAMS,
        name="far_leaf",
    )(counts, flat, src, ft)


def cells_kernel(src, out):
    for y in range(8):
        for d in range(8):
            out[d, 8 * y : 8 * y + 8, :] = src[y, 88:96, :]
            for c in range(3):
                out[d, 64 + 8 * c + y : 65 + 8 * c + y, :] = src[y, 96 + c : 97 + c, :]


def cells_message(src):
    return pl.pallas_call(
        cells_kernel,
        in_specs=[VMEM],
        out_specs=VMEM,
        out_shape=jax.ShapeDtypeStruct((8, 88, 128), F32),
        compiler_params=PARAMS,
        name="cells",
    )(src)


def far_top_kernel(counts, flat, src, ft, part, out, fs, vals, t0, t1):
    for g in range(8):
        xyz = [src[g, 64 + 8 * c : 72 + 8 * c, :] for c in range(3)]
        prepare_sources(g, xyz, t0.at[g], t1.at[g], fs)
        for y in range(8):
            vals[8 * g + y] = two_halves(src[g, 8 * y : 8 * y + 8, :])
    clear_dummy(fs, vals)
    out[...] = part[...]

    def add(t, v):
        out[t, 8] += v

    interact(counts[1], flat, fs, ft, vals, add)


def far_top(counts, flat, src, ft, part):
    return pl.pallas_call(
        far_top_kernel,
        in_specs=[SMEM, SMEM, VMEM, VMEM, VMEM],
        out_specs=VMEM,
        out_shape=jax.ShapeDtypeStruct((8, 9, 8, 128), F32),
        scratch_shapes=FAR_SCRATCH,
        compiler_params=PARAMS,
        name="far_top",
    )(counts, flat, src, ft, part)


def final_kernel(got, utm, up, near1, near2, out):
    tot = got[0]
    for d in range(1, 8):
        tot = tot + got[d]
    cell = tot[8]
    for l in range(OWN):
        incoming = tot[l] + dot3(cell, utm[l])
        out[l] = near1[l] + near2[l] + dot3(incoming, up[l])


def final(got, utm, up, near1, near2):
    return pl.pallas_call(
        final_kernel,
        in_specs=[VMEM] * 5,
        out_specs=VMEM,
        out_shape=jax.ShapeDtypeStruct((8, 8, 256), F32),
        compiler_params=PARAMS,
        name="final",
    )(got, utm, up, near1, near2)


def body(points, charges, up_op, skel_pts, utm, cell_pts, near_list, leaf_list, top_list):
    every = ("g", "y", "z")
    pts = jnp.transpose(points, (1, 0, 2))
    skel = jnp.transpose(skel_pts, (1, 0, 2))
    cpts = jnp.transpose(cell_pts, (1, 0, 2))
    count = lax.axis_size("g") * lax.axis_size("y") * lax.axis_size("z")
    up = [(i, i + 1) for i in range(count - 1)]
    down = [(i + 1, i) for i in range(count - 1)]
    m0, first, last = request(pts, charges, skel, cpts, leaf_list, top_list)
    got0 = lax.all_to_all(m0, "z", 0, 0, tiled=True)
    before = lax.ppermute(last, every, up)
    m1 = weights(charges, up_op, skel, utm, cpts)
    m1, got0, before = lax.optimization_barrier((m1, got0, before))
    got1 = lax.all_to_all(m1, "y", 0, 0, tiled=True)
    req = got0[:, 27:29, :].astype(jnp.int32)
    ft, ftop, leaf_flat, top_flat, counts = far_prep(req, got0)
    near1 = near_part(True, near_list, pts, charges, before)
    got1, near1, ft, counts = lax.optimization_barrier((got1, near1, ft, counts))
    gotg = lax.all_to_all(cells_message(got1), "g", 0, 0, tiled=True)
    part = far_leaf(counts, leaf_flat, got1, ft)
    part = far_top(counts, top_flat, gotg, ftop, part)
    part, first = lax.optimization_barrier((part, first))
    gotr = lax.all_to_all(part, "z", 0, 0, tiled=True)
    after = lax.ppermute(first, every, down)
    near2 = near_part(False, near_list, pts, after)
    return final(gotr, utm, up_op, near1, near2)


def solution(mesh):
    fine = Mesh(mesh.devices.reshape(mesh.shape["group"], 8, 8), ("g", "y", "z"))
    row = ("g", "y", "z")
    specs = tuple(P(row, *([None] * k)) for k in (2, 2, 2, 2, 2, 2, 1, 1, 1))
    return jax.shard_map(body, mesh=fine, in_specs=specs, out_specs=P(row, None, None), check_vma=False)
```

```python
import functools
import math

import jax
import jax.numpy as jnp
from jax import lax
from jax.experimental import pallas as pl
from jax.experimental.pallas import tpu as pltpu
from jax.sharding import Mesh, PartitionSpec as P

F32 = jnp.float32
BF16 = jnp.bfloat16
KAPPA = math.sqrt(3.0) * math.log2(math.e)
LN2 = math.log(2.0)
CENTER = 1.5
FEAT = 32
REACH = 4
OWN = 8
NBR = 9
PAIRS = 16
DUMMY = 64
CHUNK = 16
NEAR_DUMMY = 16

SMEM = pl.BlockSpec(memory_space=pltpu.SMEM)
HBM = pl.BlockSpec(memory_space=pltpu.HBM)
VMEM = pl.BlockSpec(memory_space=pltpu.VMEM)
PARAMS = pltpu.CompilerParams(vmem_limit_bytes=40 << 20)
WIDE = pltpu.CompilerParams(vmem_limit_bytes=60 << 20)


def split2(x):
    a = x.astype(BF16).astype(F32)
    return a, (x - a).astype(BF16).astype(F32)


def split3(x):
    a = x.astype(BF16).astype(F32)
    b, c = split2(x - a)
    return a, b, c


def dense_features(xyz):
    parts = [split2((x - CENTER) * KAPPA) for x in xyz]
    n = None
    for a, b in parts:
        r = a + b
        n = r * r if n is None else n + r * r
    n1, n2, n3 = split3(n)
    one = jnp.ones_like(n)
    zero = jnp.zeros_like(n)
    high = [a for a, _ in parts]
    low = [b for _, b in parts]
    high2 = [-2.0 * a for a in high]
    low2 = [-2.0 * b for b in low]
    s0 = high + [n1, n2, n3, one, one]
    s1 = low + [one, zero, zero, zero, zero]
    t0 = high2 + [one, one, one, n1, n2]
    t1 = low2 + [zero] * 5
    t2 = high2 + [n3] + [zero] * 4
    return s0, s1, t0, t1, t2


def spread(rows, tmp):
    n, width = rows[0].shape
    halves = width // 128
    for r, v in enumerate(rows):
        for h in range(halves):
            tmp[h, n * r : n * r + n, :] = v[:, 128 * h : 128 * h + 128]

    def load(leaf):
        return jnp.concatenate([tmp[h, pl.ds(leaf, 8, stride=n), :] for h in range(halves)], 1)

    return load


def two_halves(vals):
    v = vals * LN2
    high = v.astype(BF16).astype(F32)
    return jnp.concatenate([high, v - high], 0).astype(BF16)


def matern_over_ln2(t):
    m = jnp.maximum(t, 1e-12)
    s = m * lax.rsqrt(m)
    return (s + 1.0 / LN2) * jnp.exp2(-s)


def product(src_feat, tgt_feat, vals):
    t = jnp.dot(src_feat, tgt_feat, preferred_element_type=F32)
    k = matern_over_ln2(t)
    high = k.astype(BF16)
    low = (k - high.astype(F32)).astype(BF16)
    return jnp.dot(vals, high, preferred_element_type=F32) + jnp.dot(vals, low, preferred_element_type=F32)


def in_chunks(n, size, step):
    half = size // 2
    big = (n + half - 1) // size

    def full(i, carry):
        step(i * size, size)
        return carry

    def rest(i, carry):
        step(big * size, half)
        return carry

    lax.fori_loop(0, big, full, 0)
    lax.fori_loop(0, (n > big * size).astype(jnp.int32), rest, 0)


def dot3(a, b, transposed=False):
    ah = a.astype(BF16).astype(F32)
    both = jnp.concatenate([ah, a - ah], 0).astype(BF16)
    bh = b.astype(BF16)
    bl = (b - bh.astype(F32)).astype(BF16)
    dims = (((1,), (1 if transposed else 0,)), ((), ()))
    r = lax.dot_general(both, bh, dims, preferred_element_type=F32)
    r = r + lax.dot_general(both, bl, dims, preferred_element_type=F32)
    return r[0:8] + r[8:16]


def fetch(pairs, sems):
    copies = [pltpu.make_async_copy(a, b, sems.at[i]) for i, (a, b) in enumerate(pairs)]
    for c in copies:
        c.start()
    return copies


def request_kernel(pts_h, chg_h, skel_h, cpts_h, llist_h, tlist_h, m0, first, last, row16, pts, chg, skel, cpts, llist, tlist, sems):
    ins = ((llist_h, llist), (tlist_h, tlist), (skel_h, skel), (cpts_h, cpts), (pts_h, pts), (chg_h, chg))
    copies = fetch(ins, sems)
    for c in copies[0:2]:
        c.wait()
    lane = lax.broadcasted_iota(jnp.int32, (1, 128), 1)
    sub8 = lax.broadcasted_iota(jnp.int32, (8, 128), 0)
    lane8 = lax.broadcasted_iota(jnp.int32, (8, 128), 1)
    row = lax.broadcasted_iota(jnp.int32, (128, 128), 0)
    col = lax.broadcasted_iota(jnp.int32, (128, 128), 1)
    before = (row < col).astype(F32).astype(BF16)
    pick = (lax.broadcasted_iota(jnp.int32, (16, 128), 0) == (lax.broadcasted_iota(jnp.int32, (16, 128), 1) & 15))
    pick = pick.astype(F32).astype(BF16)
    ll = llist[...]
    mine = sub8 == (lane8 >> 4)

    def flat(v):
        w = jnp.dot(v.astype(F32).astype(BF16), pick, preferred_element_type=F32)
        return jnp.sum(jnp.where(mine, w, 0.0), axis=0, keepdims=True).astype(jnp.int32)

    upper = flat(ll >> 6)
    lower = flat(ll & 63)
    row16[...] = jnp.zeros((8, 128), jnp.int32)
    row16[0:1, 0:16] = tlist[...]
    tl = row16[0:1, :]
    leaf_hit = (lower >> 3) == sub8
    top_hit = ((tl & 7) == sub8) & (lane < 16)
    leaf_one = leaf_hit.astype(F32)
    top_one = top_hit.astype(F32)
    leaf_pos = jnp.dot(leaf_one.astype(BF16), before, preferred_element_type=F32)
    top_pos = jnp.dot(top_one.astype(BF16), before, preferred_element_type=F32) + 16.0
    leaf_n = jnp.sum(leaf_one, axis=1, keepdims=True)
    top_n = jnp.sum(top_one, axis=1, keepdims=True)
    leaf_pos = jnp.where(leaf_hit, leaf_pos, -1.0)
    top_pos = jnp.where(top_hit, top_pos, -1.0)
    local = (lower & 7) + (upper & 7) * 8
    codes = jnp.where(sub8 == 0, lane >> 4, jnp.where(sub8 == 1, local, 0)).astype(F32).astype(BF16)
    tcodes = jnp.where(sub8 == 0, tl >> 3, 0).astype(F32).astype(BF16)
    rowf = row.astype(F32)
    for c in copies[2:6]:
        c.wait()
    for d in range(8):
        for c in range(3):
            m0[d, 8 * c : 8 * c + 8, :] = skel[c]
            m0[d, 24 + c : 25 + c, :] = cpts[c]
        m0[d, 29:32, :] = jnp.zeros((3, 128), F32)
        oh = (leaf_pos[d : d + 1] == rowf).astype(F32).astype(BF16)
        got = lax.dot_general(codes, oh, (((1,), (1,)), ((), ())), preferred_element_type=F32)
        m0[d, 27:28, :] = got[0:1] * 128.0 + got[1:2]
        oh = (top_pos[d : d + 1] == rowf).astype(F32).astype(BF16)
        got = lax.dot_general(tcodes, oh, (((1,), (1,)), ((), ())), preferred_element_type=F32)[0:1]
        got = got + jnp.where(lane == 0, leaf_n[d : d + 1], 0.0) + jnp.where(lane == 1, top_n[d : d + 1], 0.0)
        m0[d, 28:29, :] = got
    for slab, start in ((first, 0), (last, OWN - REACH)):
        for i in range(REACH):
            slab[8 * i : 8 * i + 8, :] = chg[start + i]
        for c in range(3):
            slab[32 + 4 * c : 36 + 4 * c, :] = pts[c, start : start + REACH, :]
        slab[44:48, :] = jnp.zeros((4, 256), F32)


def request(pts, chg, skel, cpts, llist, tlist):
    sd = jax.ShapeDtypeStruct
    return pl.pallas_call(
        request_kernel,
        in_specs=[HBM] * 6,
        out_specs=[VMEM] * 3,
        out_shape=[sd((8, 32, 128), F32), sd((48, 256), F32), sd((48, 256), F32)],
        scratch_shapes=[pltpu.VMEM((8, 128), jnp.int32)]
        + [pltpu.VMEM(a.shape, a.dtype) for a in (pts, chg, skel, cpts, llist, tlist)]
        + [pltpu.SemaphoreType.DMA((6,))],
        compiler_params=WIDE,
        name="request",
    )(pts, chg, skel, cpts, llist, tlist)


def weights_kernel(chg_h, up_h, skel_h, utm_h, cpts_h, m1, chg, up, skel, utm, cpts, slab, sems):
    ins = ((chg_h, chg), (up_h, up), (utm_h, utm), (skel_h, skel), (cpts_h, cpts))
    copies = fetch(ins, sems)
    slab[96:104, :] = jnp.zeros((8, 128), F32)
    for c in copies[3:5]:
        c.wait()
    for c in range(3):
        slab[64 + 8 * c : 72 + 8 * c, :] = skel[c]
        slab[96 + c : 97 + c, :] = cpts[c]
    copies[0].wait()
    copies[1].wait()
    own = [dot3(chg[l], up[l], True) for l in range(OWN)]
    for l in range(OWN):
        slab[8 * l : 8 * l + 8, :] = own[l]
    copies[2].wait()
    total = dot3(own[0], utm[0], True)
    for l in range(1, OWN):
        total = total + dot3(own[l], utm[l], True)
    slab[88:96, :] = total
    for c in fetch([(slab, m1.at[d]) for d in range(8)], sems):
        c.wait()


def weights(chg, up, skel, utm, cpts):
    return pl.pallas_call(
        weights_kernel,
        in_specs=[HBM] * 5,
        out_specs=HBM,
        out_shape=jax.ShapeDtypeStruct((8, 104, 128), F32),
        scratch_shapes=[pltpu.VMEM(a.shape, a.dtype) for a in (chg, up, skel, utm, cpts)]
        + [pltpu.VMEM((104, 128), F32), pltpu.SemaphoreType.DMA((8,))],
        cost_estimate=pl.CostEstimate(flops=50000000, bytes_accessed=8000000, transcendentals=0),
        compiler_params=WIDE,
        name="weights",
    )(chg, up, skel, utm, cpts)


def near_blocks(ids, flat, base, first_leaf, early):
    pos = jnp.int32(0)
    for l in range(first_leaf, OWN):
        for n in range(NBR):
            ident = ids[l, n]
            e = ident - base
            flat[pos] = l * 32 + e
            take = (ident >= 0) & (e < REACH + OWN) if early else e >= REACH + OWN
            pos = pos + take.astype(jnp.int32)
    for u in range(CHUNK):
        flat[pos + u] = (OWN - 1) * 32 + NEAR_DUMMY
    return pos


def near_setup(sources, leaves, xyz, vals_of, fs, ft, vals, ts, tl):
    s0, s1, t0, t1, t2 = dense_features(xyz)
    load0, load1 = spread(s0, ts.at[0]), spread(s1, tl)
    for e in sources:
        a, b = load0(e), load1(e)
        fs[e] = jnp.concatenate([a, b, a, b], 0).T.astype(BF16)
        vals[e] = two_halves(vals_of(e))
    vals[NEAR_DUMMY] = jnp.zeros((16, 256), BF16)
    fs[NEAR_DUMMY] = jnp.zeros((256, FEAT), BF16)
    load0, load1, load2 = spread(t0, ts.at[1]), spread(t1, ts.at[2]), spread(t2, ts.at[3])
    for l in leaves:
        e = l + REACH
        one = load1(e)
        ft[l, 0:16, :] = jnp.concatenate([load0(e), load2(e)], 0).astype(BF16)
        ft[l, 16:32, :] = jnp.concatenate([one, one], 0).astype(BF16)


def near_run(count, flat, out, fs, ft, vals):
    out[...] = jnp.zeros_like(out)

    def step(start, size):
        for u in range(size):
            code = flat[start + u]
            l, e = code >> 5, code & 31
            r = product(fs[e], ft[l], vals[e])
            out[l] += r[0:8] + r[8:16]

    in_chunks(count, CHUNK, step)


def near_base():
    me = (lax.axis_index("g") * lax.axis_size("y") + lax.axis_index("y")) * lax.axis_size("z") + lax.axis_index("z")
    return me * OWN - REACH


def near_early_kernel(ids, pts, chg, before, out, flat, fs, ft, vals, xyz, ts, tl):
    count = near_blocks(ids, flat, near_base(), 0, True)
    for c in range(3):
        xyz[c, 0:4, :] = before[32 + 4 * c : 36 + 4 * c, :]
        xyz[c, 4:12, :] = pts[c]
        xyz[c, 12:16, :] = jnp.zeros((4, 256), F32)

    def vals_of(e):
        return before[8 * e : 8 * e + 8, :] if e < REACH else chg[e - REACH]

    near_setup(range(REACH + OWN), range(OWN), [xyz[0], xyz[1], xyz[2]], vals_of, fs, ft, vals, ts, tl)
    near_run(count, flat, out, fs, ft, vals)


def near_late_kernel(ids, pts, after, out, flat, fs, ft, vals, xyz, ts, tl):
    count = near_blocks(ids, flat, near_base(), OWN - REACH, False)
    for c in range(3):
        xyz[c, 0:4, :] = jnp.zeros((4, 256), F32)
        xyz[c, 4:12, :] = pts[c]
        xyz[c, 12:16, :] = after[32 + 4 * c : 36 + 4 * c, :]

    def vals_of(e):
        return after[8 * (e - REACH - OWN) : 8 * (e - REACH - OWN) + 8, :]

    halo = range(REACH + OWN, 2 * REACH + OWN)
    near_setup(halo, range(OWN - REACH, OWN), [xyz[0], xyz[1], xyz[2]], vals_of, fs, ft, vals, ts, tl)
    near_run(count, flat, out, fs, ft, vals)


def near_part(early, *args):
    return pl.pallas_call(
        near_early_kernel if early else near_late_kernel,
        in_specs=[SMEM] + [VMEM] * (len(args) - 1),
        out_specs=VMEM,
        out_shape=jax.ShapeDtypeStruct((OWN, 8, 256), F32),
        scratch_shapes=[
            pltpu.SMEM((OWN * NBR + CHUNK + 8,), jnp.int32),
            pltpu.VMEM((17, 256, FEAT), BF16),
            pltpu.VMEM((OWN, FEAT, 256), BF16),
            pltpu.VMEM((17, 16, 256), BF16),
            pltpu.VMEM((3, 16, 256), F32),
            pltpu.VMEM((4, 2, 128, 128), F32),
            pltpu.VMEM((2, 128, 128), F32),
        ],
        cost_estimate=pl.CostEstimate(flops=2000000000, bytes_accessed=300000, transcendentals=4194304),
        compiler_params=PARAMS,
        name="near",
    )(*args)


def prepare_sources(i, xyz, t0, t1, feat):
    s0, s1, _, _, _ = dense_features(xyz)
    s0 = spread(s0, t0)
    s1 = spread(s1, t1)
    for l in range(8):
        feat[8 * i + l, 0:8, :] = s0(l)
        feat[8 * i + l, 8:16, :] = s1(l)


def prepare_targets(i, xyz, tmp, ft):
    _, _, t0, t1, t2 = dense_features(xyz)
    load0, load1, load2 = spread(t0, tmp.at[0]), spread(t1, tmp.at[1]), spread(t2, tmp.at[2])
    for l in range(8):
        one = load1(l)
        ft[8 * i + l, 0:16, :] = jnp.concatenate([load0(l), load2(l)], 0).astype(BF16)
        ft[8 * i + l, 16:32, :] = jnp.concatenate([one, one], 0).astype(BF16)


def flatten(req, flat, row, start, slot):
    off = 0
    for d in range(8):
        n = req[d, 1, slot]

        def copy(j, carry, d=d, off=off):
            for u in range(8):
                flat[off + j * 8 + u] = req[d, row, start + j * 8 + u] + d * (1024 if row == 0 else 128)
            return carry

        lax.fori_loop(0, (n + 7) // 8, copy, 0)
        off = off + n
    for u in range(2 * PAIRS):
        flat[off + u] = DUMMY
    return off


def interact(total, flat, fs, ft, vals, add):
    zero = jnp.zeros((FEAT, 128), BF16)

    def step(start, size):
        for u in range(size // 2):
            ca = flat[start + 2 * u]
            cb = flat[start + 2 * u + 1]
            ta, sa = ca >> 7, ca & 127
            tb, sb = cb >> 7, cb & 127
            fa = ft[ta]
            fb = ft[tb]
            tgt = jnp.concatenate([jnp.concatenate([fa, zero], 1), jnp.concatenate([zero, fb], 1)], 0)
            ra, rb = fs[sa], fs[sb]
            src = jnp.concatenate([ra, ra, rb, rb], 0).T.astype(BF16)
            r = product(src, tgt, jnp.concatenate([vals[sa], vals[sb]], 0))
            add(ta, r[0:8, 0:128] + r[8:16, 0:128])
            add(tb, r[16:24, 128:256] + r[24:32, 128:256])

    in_chunks(total, 2 * PAIRS, step)


def clear_dummy(fs, vals):
    fs[DUMMY] = jnp.zeros((16, 128), F32)
    vals[DUMMY] = jnp.zeros((16, 128), BF16)


def far_prep_kernel(req, tgt, ft, ftop, leaf_flat, top_flat, counts, tmp):
    for d in range(8):
        prepare_targets(d, [tgt[32 * d + 8 * c : 32 * d + 8 * c + 8, :] for c in range(3)], tmp.at[d], ft)
    prepare_targets(0, [tgt[pl.ds(24 + c, 8, stride=32), :] for c in range(3)], tmp.at[8], ftop)
    counts[0] = flatten(req, leaf_flat, 0, 0, 0)
    counts[1] = flatten(req, top_flat, 1, 16, 1)


def far_prep(req, tgt):
    sd = jax.ShapeDtypeStruct
    return pl.pallas_call(
        far_prep_kernel,
        in_specs=[SMEM, VMEM],
        out_specs=[VMEM, VMEM, SMEM, SMEM, SMEM],
        out_shape=[
            sd((64, FEAT, 128), BF16),
            sd((8, FEAT, 128), BF16),
            sd((1024 + 64,), jnp.int32),
            sd((256,), jnp.int32),
            sd((2,), jnp.int32),
        ],
        scratch_shapes=[pltpu.VMEM((9, 3, 1, 64, 128), F32)],
        cost_estimate=pl.CostEstimate(flops=100000000, bytes_accessed=900000, transcendentals=0),
        compiler_params=PARAMS,
        name="far_prep",
    )(req, tgt.reshape(256, 128))


def far_leaf_kernel(counts, flat, src, ft, out, fs, vals, t0, t1):
    for y in range(8):
        prepare_sources(y, [src[y, 64 + 8 * c : 72 + 8 * c, :] for c in range(3)], t0.at[y], t1.at[y], fs)
        for l in range(OWN):
            vals[8 * y + l] = two_halves(src[y, 8 * l : 8 * l + 8, :])
    clear_dummy(fs, vals)
    out[...] = jnp.zeros_like(out)

    def add(t, v):
        out[t >> 3, t & 7] += v

    interact(counts[0], flat, fs, ft, vals, add)


FAR_SCRATCH = [
    pltpu.VMEM((65, 16, 128), F32),
    pltpu.VMEM((65, 16, 128), BF16),
    pltpu.VMEM((8, 1, 64, 128), F32),
    pltpu.VMEM((8, 1, 64, 128), F32),
]


def far_leaf(counts, flat, src, ft):
    return pl.pallas_call(
        far_leaf_kernel,
        in_specs=[SMEM, SMEM, VMEM, VMEM],
        out_specs=VMEM,
        out_shape=jax.ShapeDtypeStruct((8, 9, 8, 128), F32),
        scratch_shapes=FAR_SCRATCH,
        cost_estimate=pl.CostEstimate(flops=2097152000, bytes_accessed=900000, transcendentals=4194304),
        compiler_params=PARAMS,
        name="far_leaf",
    )(counts, flat, src, ft)


def cells_kernel(src, out, slab):
    for y in range(8):
        for c in range(3):
            slab[8 * c + y : 8 * c + y + 1, :] = src[y, 96 + c : 97 + c, :]
    for d in range(8):
        for y in range(8):
            out[d, 8 * y : 8 * y + 8, :] = src[y, 88:96, :]
        out[d, 64:88, :] = slab[...]


def cells_message(src):
    return pl.pallas_call(
        cells_kernel,
        in_specs=[VMEM],
        out_specs=VMEM,
        out_shape=jax.ShapeDtypeStruct((8, 88, 128), F32),
        scratch_shapes=[pltpu.VMEM((24, 128), F32)],
        compiler_params=PARAMS,
        name="cells",
    )(src)


def far_top_kernel(counts, flat, src, ft, part, out, fs, vals, t0, t1):
    for g in range(8):
        xyz = [src[g, 64 + 8 * c : 72 + 8 * c, :] for c in range(3)]
        prepare_sources(g, xyz, t0.at[g], t1.at[g], fs)
        for y in range(8):
            vals[8 * g + y] = two_halves(src[g, 8 * y : 8 * y + 8, :])
    clear_dummy(fs, vals)
    out[...] = part[...]

    def add(t, v):
        out[t, 8] += v

    interact(counts[1], flat, fs, ft, vals, add)


def far_top(counts, flat, src, ft, part):
    return pl.pallas_call(
        far_top_kernel,
        in_specs=[SMEM, SMEM, VMEM, VMEM, VMEM],
        out_specs=VMEM,
        out_shape=jax.ShapeDtypeStruct((8, 9, 8, 128), F32),
        scratch_shapes=FAR_SCRATCH,
        compiler_params=PARAMS,
        name="far_top",
    )(counts, flat, src, ft, part)


def final_kernel(got, utm, up, near1, near2, out):
    tot = got[0]
    for d in range(1, 8):
        tot = tot + got[d]
    cell = tot[8]
    for l in range(OWN):
        incoming = tot[l] + dot3(cell, utm[l])
        out[l] = near1[l] + near2[l] + dot3(incoming, up[l])


def final(got, utm, up, near1, near2):
    return pl.pallas_call(
        final_kernel,
        in_specs=[VMEM] * 5,
        out_specs=VMEM,
        out_shape=jax.ShapeDtypeStruct((8, 8, 256), F32),
        compiler_params=PARAMS,
        name="final",
    )(got, utm, up, near1, near2)


def body(points, charges, up_op, skel_pts, utm, cell_pts, near_list, leaf_list, top_list):
    every = ("g", "y", "z")
    pts = jnp.transpose(points, (1, 0, 2))
    skel = jnp.transpose(skel_pts, (1, 0, 2))
    cpts = jnp.transpose(cell_pts, (1, 0, 2))
    count = lax.axis_size("g") * lax.axis_size("y") * lax.axis_size("z")
    up = [(i, i + 1) for i in range(count - 1)]
    down = [(i + 1, i) for i in range(count - 1)]
    m0, first, last = request(pts, charges, skel, cpts, leaf_list, top_list)
    got0 = lax.all_to_all(m0, "z", 0, 0, tiled=True)
    before = lax.ppermute(last, every, up)
    m1 = weights(charges, up_op, skel, utm, cpts)
    m1, got0, before = lax.optimization_barrier((m1, got0, before))
    got1 = lax.all_to_all(m1, "y", 0, 0, tiled=True)
    req = got0[:, 27:29, :].astype(jnp.int32)
    ft, ftop, leaf_flat, top_flat, counts = far_prep(req, got0)
    near1 = near_part(True, near_list, pts, charges, before)
    got1, near1, ft, counts = lax.optimization_barrier((got1, near1, ft, counts))
    gotg = lax.all_to_all(cells_message(got1), "g", 0, 0, tiled=True)
    part = far_leaf(counts, leaf_flat, got1, ft)
    part = far_top(counts, top_flat, gotg, ftop, part)
    part, first = lax.optimization_barrier((part, first))
    gotr = lax.all_to_all(part, "z", 0, 0, tiled=True)
    after = lax.ppermute(first, every, down)
    near2 = near_part(False, near_list, pts, after)
    return final(gotr, utm, up_op, near1, near2)


def solution(mesh):
    fine = Mesh(mesh.devices.reshape(mesh.shape["group"], 8, 8), ("g", "y", "z"))
    row = ("g", "y", "z")
    specs = tuple(P(row, *([None] * k)) for k in (2, 2, 2, 2, 2, 2, 1, 1, 1))
    return jax.shard_map(body, mesh=fine, in_specs=specs, out_specs=P(row, None, None), check_vma=False)
```

```python
import functools
import math

import jax
import jax.numpy as jnp
from jax import lax
from jax.experimental import pallas as pl
from jax.experimental.pallas import tpu as pltpu
from jax.sharding import Mesh, PartitionSpec as P

F32 = jnp.float32
BF16 = jnp.bfloat16
KAPPA = math.sqrt(3.0) * math.log2(math.e)
LN2 = math.log(2.0)
CENTER = 1.5
FEAT = 32
REACH = 4
OWN = 8
NBR = 9
PAIRS = 16
DUMMY = 64
CHUNK = 16
NEAR_DUMMY = 16

SMEM = pl.BlockSpec(memory_space=pltpu.SMEM)
HBM = pl.BlockSpec(memory_space=pltpu.HBM)
VMEM = pl.BlockSpec(memory_space=pltpu.VMEM)
PARAMS = pltpu.CompilerParams(vmem_limit_bytes=40 << 20)
WIDE = pltpu.CompilerParams(vmem_limit_bytes=60 << 20)


def split2(x):
    a = x.astype(BF16).astype(F32)
    return a, (x - a).astype(BF16).astype(F32)


def split3(x):
    a = x.astype(BF16).astype(F32)
    b, c = split2(x - a)
    return a, b, c


def dense_features(xyz):
    parts = [split2((x - CENTER) * KAPPA) for x in xyz]
    n = None
    for a, b in parts:
        r = a + b
        n = r * r if n is None else n + r * r
    n1, n2, n3 = split3(n)
    one = jnp.ones_like(n)
    zero = jnp.zeros_like(n)
    high = [a for a, _ in parts]
    low = [b for _, b in parts]
    high2 = [-2.0 * a for a in high]
    low2 = [-2.0 * b for b in low]
    s0 = high + [n1, n2, n3, one, one]
    s1 = low + [one, zero, zero, zero, zero]
    t0 = high2 + [one, one, one, n1, n2]
    t1 = low2 + [zero] * 5
    t2 = high2 + [n3] + [zero] * 4
    return s0, s1, t0, t1, t2


def spread(rows, tmp):
    n, width = rows[0].shape
    halves = width // 128
    for r, v in enumerate(rows):
        for h in range(halves):
            tmp[h, n * r : n * r + n, :] = v[:, 128 * h : 128 * h + 128]

    def load(leaf):
        return jnp.concatenate([tmp[h, pl.ds(leaf, 8, stride=n), :] for h in range(halves)], 1)

    return load


def two_halves(vals):
    v = vals * LN2
    high = v.astype(BF16).astype(F32)
    return jnp.concatenate([high, v - high], 0).astype(BF16)


def matern_over_ln2(t):
    m = jnp.maximum(t, 1e-12)
    s = m * lax.rsqrt(m)
    return (s + 1.0 / LN2) * jnp.exp2(-s)


def product(src_feat, tgt_feat, vals):
    t = jnp.dot(src_feat, tgt_feat, preferred_element_type=F32)
    k = matern_over_ln2(t)
    high = k.astype(BF16)
    low = (k - high.astype(F32)).astype(BF16)
    return jnp.dot(vals, high, preferred_element_type=F32) + jnp.dot(vals, low, preferred_element_type=F32)


def in_chunks(n, size, step):
    half = size // 2
    big = (n + half - 1) // size

    def full(i, carry):
        step(i * size, size)
        return carry

    def rest(i, carry):
        step(big * size, half)
        return carry

    lax.fori_loop(0, big, full, 0)
    lax.fori_loop(0, (n > big * size).astype(jnp.int32), rest, 0)


def dot3(a, b, transposed=False):
    ah = a.astype(BF16).astype(F32)
    both = jnp.concatenate([ah, a - ah], 0).astype(BF16)
    bh = b.astype(BF16)
    bl = (b - bh.astype(F32)).astype(BF16)
    dims = (((1,), (1 if transposed else 0,)), ((), ()))
    r = lax.dot_general(both, bh, dims, preferred_element_type=F32)
    r = r + lax.dot_general(both, bl, dims, preferred_element_type=F32)
    return r[0:8] + r[8:16]


def fetch(pairs, sems):
    copies = [pltpu.make_async_copy(a, b, sems.at[i]) for i, (a, b) in enumerate(pairs)]
    for c in copies:
        c.start()
    return copies


def request_kernel(pts_h, chg_h, skel_h, cpts_h, llist_h, tlist_h, m0, first, last, row16, pts, chg, skel, cpts, llist, tlist, sems):
    ins = ((llist_h, llist), (tlist_h, tlist), (skel_h, skel), (cpts_h, cpts), (pts_h, pts), (chg_h, chg))
    copies = fetch(ins, sems)
    for c in copies[0:2]:
        c.wait()
    lane = lax.broadcasted_iota(jnp.int32, (1, 128), 1)
    sub8 = lax.broadcasted_iota(jnp.int32, (8, 128), 0)
    lane8 = lax.broadcasted_iota(jnp.int32, (8, 128), 1)
    row = lax.broadcasted_iota(jnp.int32, (128, 128), 0)
    col = lax.broadcasted_iota(jnp.int32, (128, 128), 1)
    before = (row < col).astype(F32).astype(BF16)
    pick = (lax.broadcasted_iota(jnp.int32, (16, 128), 0) == (lax.broadcasted_iota(jnp.int32, (16, 128), 1) & 15))
    pick = pick.astype(F32).astype(BF16)
    ll = llist[...]
    mine = sub8 == (lane8 >> 4)

    def flat(v):
        w = jnp.dot(v.astype(F32).astype(BF16), pick, preferred_element_type=F32)
        return jnp.sum(jnp.where(mine, w, 0.0), axis=0, keepdims=True).astype(jnp.int32)

    upper = flat(ll >> 6) & 7
    lower = flat(ll & 63)
    odd = ((lax.axis_index("d") >> 6) & 1) == 1
    leaf_u = jnp.where(odd, lower >> 3, upper)
    leaf_v = jnp.where(odd, upper, lower >> 3)
    row16[...] = jnp.zeros((8, 128), jnp.int32)
    row16[0:1, 0:16] = tlist[...]
    tl = row16[0:1, :]
    top_odd = ((tl >> 6) & 1) == 1
    top_u = jnp.where(top_odd, tl & 7, (tl >> 3) & 7)
    top_v = jnp.where(top_odd, (tl >> 3) & 7, tl & 7)
    leaf_hit = leaf_v == sub8
    top_hit = (top_v == sub8) & (lane < 16)
    leaf_one = leaf_hit.astype(F32)
    top_one = top_hit.astype(F32)
    leaf_pos = jnp.dot(leaf_one.astype(BF16), before, preferred_element_type=F32)
    top_pos = jnp.dot(top_one.astype(BF16), before, preferred_element_type=F32) + 16.0
    leaf_n = jnp.sum(leaf_one, axis=1, keepdims=True)
    top_n = jnp.sum(top_one, axis=1, keepdims=True)
    leaf_pos = jnp.where(leaf_hit, leaf_pos, -1.0)
    top_pos = jnp.where(top_hit, top_pos, -1.0)
    local = (lower & 7) + leaf_u * 8
    codes = jnp.where(sub8 == 0, lane >> 4, jnp.where(sub8 == 1, local, 0)).astype(F32).astype(BF16)
    tcodes = jnp.where(sub8 == 0, (tl >> 6) * 8 + top_u, 0).astype(F32).astype(BF16)
    rowf = row.astype(F32)
    for c in copies[2:6]:
        c.wait()
    for d in range(8):
        for c in range(3):
            m0[d, 8 * c : 8 * c + 8, :] = skel[c]
            m0[d, 24 + c : 25 + c, :] = cpts[c]
        m0[d, 29:32, :] = jnp.zeros((3, 128), F32)
        oh = (leaf_pos[d : d + 1] == rowf).astype(F32).astype(BF16)
        got = lax.dot_general(codes, oh, (((1,), (1,)), ((), ())), preferred_element_type=F32)
        m0[d, 27:28, :] = got[0:1] * 128.0 + got[1:2]
        oh = (top_pos[d : d + 1] == rowf).astype(F32).astype(BF16)
        got = lax.dot_general(tcodes, oh, (((1,), (1,)), ((), ())), preferred_element_type=F32)[0:1]
        got = got + jnp.where(lane == 0, leaf_n[d : d + 1], 0.0) + jnp.where(lane == 1, top_n[d : d + 1], 0.0)
        m0[d, 28:29, :] = got
    for slab, start in ((first, 0), (last, OWN - REACH)):
        for i in range(REACH):
            slab[8 * i : 8 * i + 8, :] = chg[start + i]
        for c in range(3):
            slab[32 + 4 * c : 36 + 4 * c, :] = pts[c, start : start + REACH, :]
        slab[44:48, :] = jnp.zeros((4, 256), F32)


def request(pts, chg, skel, cpts, llist, tlist):
    sd = jax.ShapeDtypeStruct
    return pl.pallas_call(
        request_kernel,
        in_specs=[HBM] * 6,
        out_specs=[VMEM] * 3,
        out_shape=[sd((8, 32, 128), F32), sd((48, 256), F32), sd((48, 256), F32)],
        scratch_shapes=[pltpu.VMEM((8, 128), jnp.int32)]
        + [pltpu.VMEM(a.shape, a.dtype) for a in (pts, chg, skel, cpts, llist, tlist)]
        + [pltpu.SemaphoreType.DMA((6,))],
        compiler_params=WIDE,
        name="request",
    )(pts, chg, skel, cpts, llist, tlist)


def weights_kernel(chg_h, up_h, skel_h, utm_h, cpts_h, m1, chg, up, skel, utm, cpts, slab, sems):
    ins = ((chg_h, chg), (up_h, up), (utm_h, utm), (skel_h, skel), (cpts_h, cpts))
    copies = fetch(ins, sems)
    slab[96:104, :] = jnp.zeros((8, 128), F32)
    for c in copies[3:5]:
        c.wait()
    for c in range(3):
        slab[64 + 8 * c : 72 + 8 * c, :] = skel[c]
        slab[96 + c : 97 + c, :] = cpts[c]
    copies[0].wait()
    copies[1].wait()
    own = [dot3(chg[l], up[l], True) for l in range(OWN)]
    for l in range(OWN):
        slab[8 * l : 8 * l + 8, :] = own[l]
    copies[2].wait()
    total = dot3(own[0], utm[0], True)
    for l in range(1, OWN):
        total = total + dot3(own[l], utm[l], True)
    slab[88:96, :] = total
    for c in fetch([(slab, m1.at[d]) for d in range(8)], sems):
        c.wait()


def weights(chg, up, skel, utm, cpts):
    return pl.pallas_call(
        weights_kernel,
        in_specs=[HBM] * 5,
        out_specs=HBM,
        out_shape=jax.ShapeDtypeStruct((8, 104, 128), F32),
        scratch_shapes=[pltpu.VMEM(a.shape, a.dtype) for a in (chg, up, skel, utm, cpts)]
        + [pltpu.VMEM((104, 128), F32), pltpu.SemaphoreType.DMA((8,))],
        cost_estimate=pl.CostEstimate(flops=50000000, bytes_accessed=8000000, transcendentals=0),
        compiler_params=WIDE,
        name="weights",
    )(chg, up, skel, utm, cpts)


def near_blocks(ids, flat, base, first_leaf, early):
    pos = jnp.int32(0)
    for l in range(first_leaf, OWN):
        for n in range(NBR):
            ident = ids[l, n]
            e = ident - base
            flat[pos] = l * 32 + e
            take = (ident >= 0) & (e < REACH + OWN) if early else e >= REACH + OWN
            pos = pos + take.astype(jnp.int32)
    for u in range(CHUNK):
        flat[pos + u] = (OWN - 1) * 32 + NEAR_DUMMY
    return pos


def near_setup(sources, leaves, xyz, vals_of, fs, ft, vals, ts, tl):
    s0, s1, t0, t1, t2 = dense_features(xyz)
    load0, load1 = spread(s0, ts.at[0]), spread(s1, tl)
    for e in sources:
        a, b = load0(e), load1(e)
        fs[e] = jnp.concatenate([a, b, a, b], 0).T.astype(BF16)
        vals[e] = two_halves(vals_of(e))
    vals[NEAR_DUMMY] = jnp.zeros((16, 256), BF16)
    fs[NEAR_DUMMY] = jnp.zeros((256, FEAT), BF16)
    load0, load1, load2 = spread(t0, ts.at[1]), spread(t1, ts.at[2]), spread(t2, ts.at[3])
    for l in leaves:
        e = l + REACH
        one = load1(e)
        ft[l, 0:16, :] = jnp.concatenate([load0(e), load2(e)], 0).astype(BF16)
        ft[l, 16:32, :] = jnp.concatenate([one, one], 0).astype(BF16)


def near_run(count, flat, out, fs, ft, vals):
    out[...] = jnp.zeros_like(out)

    def step(start, size):
        for u in range(size):
            code = flat[start + u]
            l, e = code >> 5, code & 31
            r = product(fs[e], ft[l], vals[e])
            out[l] += r[0:8] + r[8:16]

    in_chunks(count, CHUNK, step)


def near_base():
    return lax.axis_index("d") * OWN - REACH


def near_early_kernel(ids, pts, chg, before, out, flat, fs, ft, vals, xyz, ts, tl):
    count = near_blocks(ids, flat, near_base(), 0, True)
    for c in range(3):
        xyz[c, 0:4, :] = before[32 + 4 * c : 36 + 4 * c, :]
        xyz[c, 4:12, :] = pts[c]
        xyz[c, 12:16, :] = jnp.zeros((4, 256), F32)

    def vals_of(e):
        return before[8 * e : 8 * e + 8, :] if e < REACH else chg[e - REACH]

    near_setup(range(REACH + OWN), range(OWN), [xyz[0], xyz[1], xyz[2]], vals_of, fs, ft, vals, ts, tl)
    near_run(count, flat, out, fs, ft, vals)


def near_late_kernel(ids, pts, after, out, flat, fs, ft, vals, xyz, ts, tl):
    count = near_blocks(ids, flat, near_base(), OWN - REACH, False)
    for c in range(3):
        xyz[c, 0:4, :] = jnp.zeros((4, 256), F32)
        xyz[c, 4:12, :] = pts[c]
        xyz[c, 12:16, :] = after[32 + 4 * c : 36 + 4 * c, :]

    def vals_of(e):
        return after[8 * (e - REACH - OWN) : 8 * (e - REACH - OWN) + 8, :]

    halo = range(REACH + OWN, 2 * REACH + OWN)
    near_setup(halo, range(OWN - REACH, OWN), [xyz[0], xyz[1], xyz[2]], vals_of, fs, ft, vals, ts, tl)
    near_run(count, flat, out, fs, ft, vals)


def near_part(early, *args):
    return pl.pallas_call(
        near_early_kernel if early else near_late_kernel,
        in_specs=[SMEM] + [VMEM] * (len(args) - 1),
        out_specs=VMEM,
        out_shape=jax.ShapeDtypeStruct((OWN, 8, 256), F32),
        scratch_shapes=[
            pltpu.SMEM((OWN * NBR + CHUNK + 8,), jnp.int32),
            pltpu.VMEM((17, 256, FEAT), BF16),
            pltpu.VMEM((OWN, FEAT, 256), BF16),
            pltpu.VMEM((17, 16, 256), BF16),
            pltpu.VMEM((3, 16, 256), F32),
            pltpu.VMEM((4, 2, 128, 128), F32),
            pltpu.VMEM((2, 128, 128), F32),
        ],
        cost_estimate=pl.CostEstimate(flops=2000000000, bytes_accessed=300000, transcendentals=4194304),
        compiler_params=PARAMS,
        name="near",
    )(*args)


def prepare_sources(i, xyz, t0, t1, feat):
    s0, s1, _, _, _ = dense_features(xyz)
    s0 = spread(s0, t0)
    s1 = spread(s1, t1)
    for l in range(8):
        feat[8 * i + l, 0:8, :] = s0(l)
        feat[8 * i + l, 8:16, :] = s1(l)


def prepare_targets(i, xyz, tmp, ft):
    _, _, t0, t1, t2 = dense_features(xyz)
    load0, load1, load2 = spread(t0, tmp.at[0]), spread(t1, tmp.at[1]), spread(t2, tmp.at[2])
    for l in range(8):
        one = load1(l)
        ft[8 * i + l, 0:16, :] = jnp.concatenate([load0(l), load2(l)], 0).astype(BF16)
        ft[8 * i + l, 16:32, :] = jnp.concatenate([one, one], 0).astype(BF16)


def flatten(req, flat, row, start, slot):
    off = 0
    for d in range(8):
        n = req[d, 1, slot]

        def copy(j, carry, d=d, off=off):
            for u in range(8):
                flat[off + j * 8 + u] = req[d, row, start + j * 8 + u] + d * (1024 if row == 0 else 128)
            return carry

        lax.fori_loop(0, (n + 7) // 8, copy, 0)
        off = off + n
    for u in range(2 * PAIRS):
        flat[off + u] = DUMMY
    return off


def interact(total, flat, fs, ft, vals, add):
    zero = jnp.zeros((FEAT, 128), BF16)

    def step(start, size):
        for u in range(size // 2):
            ca = flat[start + 2 * u]
            cb = flat[start + 2 * u + 1]
            ta, sa = ca >> 7, ca & 127
            tb, sb = cb >> 7, cb & 127
            fa = ft[ta]
            fb = ft[tb]
            tgt = jnp.concatenate([jnp.concatenate([fa, zero], 1), jnp.concatenate([zero, fb], 1)], 0)
            ra, rb = fs[sa], fs[sb]
            src = jnp.concatenate([ra, ra, rb, rb], 0).T.astype(BF16)
            r = product(src, tgt, jnp.concatenate([vals[sa], vals[sb]], 0))
            add(ta, r[0:8, 0:128] + r[8:16, 0:128])
            add(tb, r[16:24, 128:256] + r[24:32, 128:256])

    in_chunks(total, 2 * PAIRS, step)


def clear_dummy(fs, vals):
    fs[DUMMY] = jnp.zeros((16, 128), F32)
    vals[DUMMY] = jnp.zeros((16, 128), BF16)


def far_prep_kernel(req, tgt, ft, ftop, leaf_flat, top_flat, counts, tmp):
    for d in range(8):
        prepare_targets(d, [tgt[32 * d + 8 * c : 32 * d + 8 * c + 8, :] for c in range(3)], tmp.at[d], ft)
    prepare_targets(0, [tgt[pl.ds(24 + c, 8, stride=32), :] for c in range(3)], tmp.at[8], ftop)
    counts[0] = flatten(req, leaf_flat, 0, 0, 0)
    counts[1] = flatten(req, top_flat, 1, 16, 1)


def far_prep(req, tgt):
    sd = jax.ShapeDtypeStruct
    return pl.pallas_call(
        far_prep_kernel,
        in_specs=[SMEM, VMEM],
        out_specs=[VMEM, VMEM, SMEM, SMEM, SMEM],
        out_shape=[
            sd((64, FEAT, 128), BF16),
            sd((8, FEAT, 128), BF16),
            sd((1024 + 64,), jnp.int32),
            sd((256,), jnp.int32),
            sd((2,), jnp.int32),
        ],
        scratch_shapes=[pltpu.VMEM((9, 3, 1, 64, 128), F32)],
        cost_estimate=pl.CostEstimate(flops=100000000, bytes_accessed=900000, transcendentals=0),
        compiler_params=PARAMS,
        name="far_prep",
    )(req, tgt.reshape(256, 128))


def far_leaf_kernel(counts, flat, src, ft, out, fs, vals, t0, t1):
    for y in range(8):
        prepare_sources(y, [src[y, 64 + 8 * c : 72 + 8 * c, :] for c in range(3)], t0.at[y], t1.at[y], fs)
        for l in range(OWN):
            vals[8 * y + l] = two_halves(src[y, 8 * l : 8 * l + 8, :])
    clear_dummy(fs, vals)
    out[...] = jnp.zeros_like(out)

    def add(t, v):
        out[t >> 3, t & 7] += v

    interact(counts[0], flat, fs, ft, vals, add)


FAR_SCRATCH = [
    pltpu.VMEM((65, 16, 128), F32),
    pltpu.VMEM((65, 16, 128), BF16),
    pltpu.VMEM((8, 1, 64, 128), F32),
    pltpu.VMEM((8, 1, 64, 128), F32),
]


def far_leaf(counts, flat, src, ft):
    return pl.pallas_call(
        far_leaf_kernel,
        in_specs=[SMEM, SMEM, VMEM, VMEM],
        out_specs=VMEM,
        out_shape=jax.ShapeDtypeStruct((8, 9, 8, 128), F32),
        scratch_shapes=FAR_SCRATCH,
        cost_estimate=pl.CostEstimate(flops=2097152000, bytes_accessed=900000, transcendentals=4194304),
        compiler_params=PARAMS,
        name="far_leaf",
    )(counts, flat, src, ft)


def cells_kernel(src, out, slab):
    for y in range(8):
        for c in range(3):
            slab[8 * c + y : 8 * c + y + 1, :] = src[y, 96 + c : 97 + c, :]
    for d in range(8):
        for y in range(8):
            out[d, 8 * y : 8 * y + 8, :] = src[y, 88:96, :]
        out[d, 64:88, :] = slab[...]


def cells_message(src):
    return pl.pallas_call(
        cells_kernel,
        in_specs=[VMEM],
        out_specs=VMEM,
        out_shape=jax.ShapeDtypeStruct((8, 88, 128), F32),
        scratch_shapes=[pltpu.VMEM((24, 128), F32)],
        compiler_params=PARAMS,
        name="cells",
    )(src)


def far_top_kernel(counts, flat, src, ft, part, out, fs, vals, t0, t1):
    for g in range(8):
        xyz = [src[g, 64 + 8 * c : 72 + 8 * c, :] for c in range(3)]
        prepare_sources(g, xyz, t0.at[g], t1.at[g], fs)
        for y in range(8):
            vals[8 * g + y] = two_halves(src[g, 8 * y : 8 * y + 8, :])
    clear_dummy(fs, vals)
    out[...] = part[...]

    def add(t, v):
        out[t, 8] += v

    interact(counts[1], flat, fs, ft, vals, add)


def far_top(counts, flat, src, ft, part):
    return pl.pallas_call(
        far_top_kernel,
        in_specs=[SMEM, SMEM, VMEM, VMEM, VMEM],
        out_specs=VMEM,
        out_shape=jax.ShapeDtypeStruct((8, 9, 8, 128), F32),
        scratch_shapes=FAR_SCRATCH,
        compiler_params=PARAMS,
        name="far_top",
    )(counts, flat, src, ft, part)


def final_kernel(got, utm, up, near1, near2, out):
    tot = got[0]
    for d in range(1, 8):
        tot = tot + got[d]
    cell = tot[8]
    for l in range(OWN):
        incoming = tot[l] + dot3(cell, utm[l])
        out[l] = near1[l] + near2[l] + dot3(incoming, up[l])


def final(got, utm, up, near1, near2):
    return pl.pallas_call(
        final_kernel,
        in_specs=[VMEM] * 5,
        out_specs=VMEM,
        out_shape=jax.ShapeDtypeStruct((8, 8, 256), F32),
        compiler_params=PARAMS,
        name="final",
    )(got, utm, up, near1, near2)


def device(g, u, v):
    return g * 64 + (v * 8 + u if g % 2 else u * 8 + v)


def body(points, charges, up_op, skel_pts, utm, cell_pts, near_list, leaf_list, top_list):
    r = range(8)
    along_u = [[device(g, u, v) for u in r] for g in r for v in r]
    along_v = [[device(g, u, v) for v in r] for g in r for u in r]
    along_g = [[device(g, u, v) for g in r] for u in r for v in r]

    def exchange(x, groups):
        return lax.all_to_all(x, "d", 0, 0, axis_index_groups=groups, tiled=True)

    pts = jnp.transpose(points, (1, 0, 2))
    skel = jnp.transpose(skel_pts, (1, 0, 2))
    cpts = jnp.transpose(cell_pts, (1, 0, 2))
    count = lax.axis_size("d")
    up = [(i, i + 1) for i in range(count - 1)]
    down = [(i + 1, i) for i in range(count - 1)]
    m0, first, last = request(pts, charges, skel, cpts, leaf_list, top_list)
    got0 = exchange(m0, along_v)
    before = lax.ppermute(last, "d", up)
    m1 = weights(charges, up_op, skel, utm, cpts)
    m1, got0, before = lax.optimization_barrier((m1, got0, before))
    got1 = exchange(m1, along_u)
    req = got0[:, 27:29, :].astype(jnp.int32)
    ft, ftop, leaf_flat, top_flat, counts = far_prep(req, got0)
    near1 = near_part(True, near_list, pts, charges, before)
    got1, near1, ft, counts = lax.optimization_barrier((got1, near1, ft, counts))
    gotg = exchange(cells_message(got1), along_g)
    part = far_leaf(counts, leaf_flat, got1, ft)
    part = far_top(counts, top_flat, gotg, ftop, part)
    part, first = lax.optimization_barrier((part, first))
    gotr = exchange(part, along_v)
    after = lax.ppermute(first, "d", down)
    near2 = near_part(False, near_list, pts, after)
    return final(gotr, utm, up_op, near1, near2)


def solution(mesh):
    line = Mesh(mesh.devices.reshape(-1), ("d",))
    specs = tuple(P("d", *([None] * k)) for k in (2, 2, 2, 2, 2, 2, 1, 1, 1))
    return jax.shard_map(body, mesh=line, in_specs=specs, out_specs=P("d", None, None), check_vma=False)
```

```python
import functools
import math

import jax
import jax.numpy as jnp
from jax import lax
from jax.experimental import pallas as pl
from jax.experimental.pallas import tpu as pltpu
from jax.sharding import Mesh, PartitionSpec as P

F32 = jnp.float32
BF16 = jnp.bfloat16
KAPPA = math.sqrt(3.0) * math.log2(math.e)
LN2 = math.log(2.0)
CENTER = 1.5
FEAT = 32
REACH = 4
OWN = 8
NBR = 9
PAIRS = 16
DUMMY = 64
CHUNK = 16
NEAR_DUMMY = 16

SMEM = pl.BlockSpec(memory_space=pltpu.SMEM)
HBM = pl.BlockSpec(memory_space=pltpu.HBM)
VMEM = pl.BlockSpec(memory_space=pltpu.VMEM)
PARAMS = pltpu.CompilerParams(vmem_limit_bytes=40 << 20)
WIDE = pltpu.CompilerParams(vmem_limit_bytes=60 << 20)


def split2(x):
    a = x.astype(BF16).astype(F32)
    return a, (x - a).astype(BF16).astype(F32)


def split3(x):
    a = x.astype(BF16).astype(F32)
    b, c = split2(x - a)
    return a, b, c


def dense_features(xyz):
    parts = [split2((x - CENTER) * KAPPA) for x in xyz]
    n = None
    for a, b in parts:
        r = a + b
        n = r * r if n is None else n + r * r
    n1, n2, n3 = split3(n)
    one = jnp.ones_like(n)
    zero = jnp.zeros_like(n)
    high = [a for a, _ in parts]
    low = [b for _, b in parts]
    high2 = [-2.0 * a for a in high]
    low2 = [-2.0 * b for b in low]
    s0 = high + [n1, n2, n3, one, one]
    s1 = low + [one, zero, zero, zero, zero]
    t0 = high2 + [one, one, one, n1, n2]
    t1 = low2 + [zero] * 5
    t2 = high2 + [n3] + [zero] * 4
    return s0, s1, t0, t1, t2


def spread(rows, tmp):
    n, width = rows[0].shape
    halves = width // 128
    for r, v in enumerate(rows):
        for h in range(halves):
            tmp[h, n * r : n * r + n, :] = v[:, 128 * h : 128 * h + 128]

    def load(leaf):
        return jnp.concatenate([tmp[h, pl.ds(leaf, 8, stride=n), :] for h in range(halves)], 1)

    return load


def two_halves(vals):
    v = vals * LN2
    high = v.astype(BF16).astype(F32)
    return jnp.concatenate([high, v - high], 0).astype(BF16)


def matern_over_ln2(t):
    m = jnp.maximum(t, 1e-12)
    s = m * lax.rsqrt(m)
    return (s + 1.0 / LN2) * jnp.exp2(-s)


def product(src_feat, tgt_feat, vals):
    t = jnp.dot(src_feat, tgt_feat, preferred_element_type=F32)
    k = matern_over_ln2(t)
    high = k.astype(BF16)
    low = (k - high.astype(F32)).astype(BF16)
    return jnp.dot(vals, high, preferred_element_type=F32) + jnp.dot(vals, low, preferred_element_type=F32)


def in_chunks(n, size, step):
    half = size // 2
    big = (n + half - 1) // size

    def full(i, carry):
        step(i * size, size)
        return carry

    def rest(i, carry):
        step(big * size, half)
        return carry

    lax.fori_loop(0, big, full, 0)
    lax.fori_loop(0, (n > big * size).astype(jnp.int32), rest, 0)


def dot3(a, b, transposed=False):
    ah = a.astype(BF16).astype(F32)
    both = jnp.concatenate([ah, a - ah], 0).astype(BF16)
    bh = b.astype(BF16)
    bl = (b - bh.astype(F32)).astype(BF16)
    dims = (((1,), (1 if transposed else 0,)), ((), ()))
    r = lax.dot_general(both, bh, dims, preferred_element_type=F32)
    r = r + lax.dot_general(both, bl, dims, preferred_element_type=F32)
    return r[0:8] + r[8:16]


def odd_group():
    return (lax.axis_index("d") >> 6) & 1


def fetch(pairs, sems, at):
    copies = [pltpu.make_async_copy(a, b, sems.at[at + i]) for i, (a, b) in enumerate(pairs)]
    for c in copies:
        c.start()
    return copies


def pack_kernel(
    pts_h, chg_h, skel_h, cpts_h, llist_h, tlist_h, up_h, utm_h,
    m0_h, m1_h, first_h, last_h,
    pts, chg, skel, cpts, llist, tlist, up, utm, m0, m1, first, last, row16, sems,
):
    ins = ((llist_h, llist), (tlist_h, tlist), (skel_h, skel), (cpts_h, cpts), (chg_h, chg), (pts_h, pts), (up_h, up), (utm_h, utm))
    copies = fetch(ins, sems, 0)
    for c in copies[0:2]:
        c.wait()
    lane = lax.broadcasted_iota(jnp.int32, (1, 128), 1)
    sub8 = lax.broadcasted_iota(jnp.int32, (8, 128), 0)
    lane8 = lax.broadcasted_iota(jnp.int32, (8, 128), 1)
    row = lax.broadcasted_iota(jnp.int32, (128, 128), 0)
    col = lax.broadcasted_iota(jnp.int32, (128, 128), 1)
    before = (row < col).astype(F32).astype(BF16)
    pick = (lax.broadcasted_iota(jnp.int32, (16, 128), 0) == (lax.broadcasted_iota(jnp.int32, (16, 128), 1) & 15))
    pick = pick.astype(F32).astype(BF16)
    ll = llist[...]
    mine = sub8 == (lane8 >> 4)

    def flat(v):
        w = jnp.dot(v.astype(F32).astype(BF16), pick, preferred_element_type=F32)
        return jnp.sum(jnp.where(mine, w, 0.0), axis=0, keepdims=True).astype(jnp.int32)

    upper = flat(ll >> 6) & 7
    lower = flat(ll & 63)
    row16[...] = jnp.zeros((8, 128), jnp.int32)
    row16[0:1, 0:16] = tlist[...]
    tl = row16[0:1, :]
    odd = odd_group() == 1
    leaf_u = jnp.where(odd, lower >> 3, upper)
    leaf_v = jnp.where(odd, upper, lower >> 3)
    top_u = jnp.where(odd, tl & 7, (tl >> 3) & 7)
    top_v = jnp.where(odd, (tl >> 3) & 7, tl & 7)
    leaf_hit = leaf_v == sub8
    top_hit = (top_v == sub8) & (lane < 16)
    leaf_one = leaf_hit.astype(F32)
    top_one = top_hit.astype(F32)
    leaf_pos = jnp.dot(leaf_one.astype(BF16), before, preferred_element_type=F32)
    top_pos = jnp.dot(top_one.astype(BF16), before, preferred_element_type=F32) + 16.0
    leaf_n = jnp.sum(leaf_one, axis=1, keepdims=True)
    top_n = jnp.sum(top_one, axis=1, keepdims=True)
    leaf_pos = jnp.where(leaf_hit, leaf_pos, -1.0)
    top_pos = jnp.where(top_hit, top_pos, -1.0)
    local = (lower & 7) + leaf_u * 8
    codes = jnp.where(sub8 == 0, lane >> 4, jnp.where(sub8 == 1, local, 0)).astype(F32).astype(BF16)
    tcodes = jnp.where(sub8 == 0, (tl >> 6) * 8 + top_u, 0).astype(F32).astype(BF16)
    rowf = row.astype(F32)
    for c in copies[2:6]:
        c.wait()
    for d in range(8):
        for c in range(3):
            m0[d, 8 * c : 8 * c + 8, :] = skel[c]
            m0[d, 24 + c : 25 + c, :] = cpts[c]
        m0[d, 29:32, :] = jnp.zeros((3, 128), F32)
        oh = (leaf_pos[d : d + 1] == rowf).astype(F32).astype(BF16)
        got = lax.dot_general(codes, oh, (((1,), (1,)), ((), ())), preferred_element_type=F32)
        m0[d, 27:28, :] = got[0:1] * 128.0 + got[1:2]
        oh = (top_pos[d : d + 1] == rowf).astype(F32).astype(BF16)
        got = lax.dot_general(tcodes, oh, (((1,), (1,)), ((), ())), preferred_element_type=F32)[0:1]
        got = got + jnp.where(lane == 0, leaf_n[d : d + 1], 0.0) + jnp.where(lane == 1, top_n[d : d + 1], 0.0)
        m0[d, 28:29, :] = got
    for slab, start in ((first, 0), (last, OWN - REACH)):
        for i in range(REACH):
            slab[8 * i : 8 * i + 8, :] = chg[start + i]
        for c in range(3):
            slab[32 + 4 * c : 36 + 4 * c, :] = pts[c, start : start + REACH, :]
        slab[44:48, :] = jnp.zeros((4, 256), F32)
    outs = fetch(((first, first_h), (last, last_h)), sems, 8)
    m1[96:104, :] = jnp.zeros((8, 128), F32)
    for c in range(3):
        m1[64 + 8 * c : 72 + 8 * c, :] = skel[c]
        m1[96 + c : 97 + c, :] = cpts[c]
    copies[6].wait()
    own = [dot3(chg[l], up[l], True) for l in range(OWN)]
    for l in range(OWN):
        m1[8 * l : 8 * l + 8, :] = own[l]
    copies[7].wait()
    total = dot3(own[0], utm[0], True)
    for l in range(1, OWN):
        total = total + dot3(own[l], utm[l], True)
    m1[88:96, :] = total
    for d in range(8):
        m0[d, 32:40, :] = total
    outs += fetch([(m0, m0_h)] + [(m1, m1_h.at[d]) for d in range(8)], sems, 10)
    for c in outs:
        c.wait()


def pack(*args):
    sd = jax.ShapeDtypeStruct
    shapes = [(8, 40, 128), (104, 128), (48, 256), (48, 256)]
    return pl.pallas_call(
        pack_kernel,
        in_specs=[HBM] * 8,
        out_specs=[HBM] * 4,
        out_shape=[sd((8, 40, 128), F32), sd((8, 104, 128), F32), sd((48, 256), F32), sd((48, 256), F32)],
        scratch_shapes=[pltpu.VMEM(a.shape, a.dtype) for a in args]
        + [pltpu.VMEM(s, F32) for s in shapes]
        + [pltpu.VMEM((8, 128), jnp.int32), pltpu.SemaphoreType.DMA((19,))],
        compiler_params=WIDE,
        name="pack",
    )(*args)


def near_blocks(ids, flat, base, first_leaf, early):
    pos = jnp.int32(0)
    for l in range(first_leaf, OWN):
        for n in range(NBR):
            ident = ids[l, n]
            e = ident - base
            flat[pos] = l * 32 + e
            take = (ident >= 0) & (e < REACH + OWN) if early else e >= REACH + OWN
            pos = pos + take.astype(jnp.int32)
    for u in range(CHUNK):
        flat[pos + u] = (OWN - 1) * 32 + NEAR_DUMMY
    return pos


def near_setup(sources, leaves, xyz, vals_of, fs, ft, vals, ts, tl):
    s0, s1, t0, t1, t2 = dense_features(xyz)
    load0, load1 = spread(s0, ts.at[0]), spread(s1, tl)
    for e in sources:
        a, b = load0(e), load1(e)
        fs[e] = jnp.concatenate([a, b, a, b], 0).T.astype(BF16)
        vals[e] = two_halves(vals_of(e))
    vals[NEAR_DUMMY] = jnp.zeros((16, 256), BF16)
    fs[NEAR_DUMMY] = jnp.zeros((256, FEAT), BF16)
    load0, load1, load2 = spread(t0, ts.at[1]), spread(t1, ts.at[2]), spread(t2, ts.at[3])
    for l in leaves:
        e = l + REACH
        one = load1(e)
        ft[l, 0:16, :] = jnp.concatenate([load0(e), load2(e)], 0).astype(BF16)
        ft[l, 16:32, :] = jnp.concatenate([one, one], 0).astype(BF16)


def near_run(count, flat, out, fs, ft, vals):
    out[...] = jnp.zeros_like(out)

    def step(start, size):
        for u in range(size):
            code = flat[start + u]
            l, e = code >> 5, code & 31
            r = product(fs[e], ft[l], vals[e])
            out[l] += r[0:8] + r[8:16]

    in_chunks(count, CHUNK, step)


def near_base():
    return lax.axis_index("d") * OWN - REACH


def near_early_kernel(ids, pts, chg, before, out, flat, fs, ft, vals, xyz, ts, tl):
    count = near_blocks(ids, flat, near_base(), 0, True)
    for c in range(3):
        xyz[c, 0:4, :] = before[32 + 4 * c : 36 + 4 * c, :]
        xyz[c, 4:12, :] = pts[c]
        xyz[c, 12:16, :] = jnp.zeros((4, 256), F32)

    def vals_of(e):
        return before[8 * e : 8 * e + 8, :] if e < REACH else chg[e - REACH]

    near_setup(range(REACH + OWN), range(OWN), [xyz[0], xyz[1], xyz[2]], vals_of, fs, ft, vals, ts, tl)
    near_run(count, flat, out, fs, ft, vals)


def near_late_kernel(ids, pts, after, out, flat, fs, ft, vals, xyz, ts, tl):
    count = near_blocks(ids, flat, near_base(), OWN - REACH, False)
    for c in range(3):
        xyz[c, 0:4, :] = jnp.zeros((4, 256), F32)
        xyz[c, 4:12, :] = pts[c]
        xyz[c, 12:16, :] = after[32 + 4 * c : 36 + 4 * c, :]

    def vals_of(e):
        return after[8 * (e - REACH - OWN) : 8 * (e - REACH - OWN) + 8, :]

    halo = range(REACH + OWN, 2 * REACH + OWN)
    near_setup(halo, range(OWN - REACH, OWN), [xyz[0], xyz[1], xyz[2]], vals_of, fs, ft, vals, ts, tl)
    near_run(count, flat, out, fs, ft, vals)


def near_part(early, *args):
    return pl.pallas_call(
        near_early_kernel if early else near_late_kernel,
        in_specs=[SMEM] + [VMEM] * (len(args) - 1),
        out_specs=VMEM,
        out_shape=jax.ShapeDtypeStruct((OWN, 8, 256), F32),
        scratch_shapes=[
            pltpu.SMEM((OWN * NBR + CHUNK + 8,), jnp.int32),
            pltpu.VMEM((17, 256, FEAT), BF16),
            pltpu.VMEM((OWN, FEAT, 256), BF16),
            pltpu.VMEM((17, 16, 256), BF16),
            pltpu.VMEM((3, 16, 256), F32),
            pltpu.VMEM((4, 2, 128, 128), F32),
            pltpu.VMEM((2, 128, 128), F32),
        ],
        cost_estimate=pl.CostEstimate(flops=2000000000, bytes_accessed=300000, transcendentals=4194304),
        compiler_params=PARAMS,
        name="near",
    )(*args)


def prepare_sources(i, xyz, t0, t1, feat):
    s0, s1, _, _, _ = dense_features(xyz)
    s0 = spread(s0, t0)
    s1 = spread(s1, t1)
    for l in range(8):
        feat[8 * i + l, 0:8, :] = s0(l)
        feat[8 * i + l, 8:16, :] = s1(l)


def prepare_targets(i, xyz, tmp, ft):
    _, _, t0, t1, t2 = dense_features(xyz)
    load0, load1, load2 = spread(t0, tmp.at[0]), spread(t1, tmp.at[1]), spread(t2, tmp.at[2])
    for l in range(8):
        one = load1(l)
        ft[8 * i + l, 0:16, :] = jnp.concatenate([load0(l), load2(l)], 0).astype(BF16)
        ft[8 * i + l, 16:32, :] = jnp.concatenate([one, one], 0).astype(BF16)


def flatten(req, flat, row, start, slot):
    off = 0
    for d in range(8):
        n = req[d, 1, slot]

        def copy(j, carry, d=d, off=off):
            for u in range(8):
                flat[off + j * 8 + u] = req[d, row, start + j * 8 + u] + d * (1024 if row == 0 else 128)
            return carry

        lax.fori_loop(0, (n + 7) // 8, copy, 0)
        off = off + n
    for u in range(2 * PAIRS):
        flat[off + u] = DUMMY
    return off


def interact(total, flat, fs, ft, vals, add):
    zero = jnp.zeros((FEAT, 128), BF16)

    def step(start, size):
        for u in range(size // 2):
            ca = flat[start + 2 * u]
            cb = flat[start + 2 * u + 1]
            ta, sa = ca >> 7, ca & 127
            tb, sb = cb >> 7, cb & 127
            fa = ft[ta]
            fb = ft[tb]
            tgt = jnp.concatenate([jnp.concatenate([fa, zero], 1), jnp.concatenate([zero, fb], 1)], 0)
            ra, rb = fs[sa], fs[sb]
            src = jnp.concatenate([ra, ra, rb, rb], 0).T.astype(BF16)
            r = product(src, tgt, jnp.concatenate([vals[sa], vals[sb]], 0))
            add(ta, r[0:8, 0:128] + r[8:16, 0:128])
            add(tb, r[16:24, 128:256] + r[24:32, 128:256])

    in_chunks(total, 2 * PAIRS, step)


def clear_dummy(fs, vals):
    fs[DUMMY] = jnp.zeros((16, 128), F32)
    vals[DUMMY] = jnp.zeros((16, 128), BF16)


def far_prep_kernel(req, tgt, ft, ftop, leaf_flat, top_flat, counts, tmp):
    for d in range(8):
        prepare_targets(d, [tgt[40 * d + 8 * c : 40 * d + 8 * c + 8, :] for c in range(3)], tmp.at[d], ft)
    prepare_targets(0, [tgt[pl.ds(24 + c, 8, stride=40), :] for c in range(3)], tmp.at[8], ftop)
    counts[0] = flatten(req, leaf_flat, 0, 0, 0)
    counts[1] = flatten(req, top_flat, 1, 16, 1)


def far_prep(req, tgt):
    sd = jax.ShapeDtypeStruct
    return pl.pallas_call(
        far_prep_kernel,
        in_specs=[SMEM, VMEM],
        out_specs=[VMEM, VMEM, SMEM, SMEM, SMEM],
        out_shape=[
            sd((64, FEAT, 128), BF16),
            sd((8, FEAT, 128), BF16),
            sd((1024 + 64,), jnp.int32),
            sd((256,), jnp.int32),
            sd((2,), jnp.int32),
        ],
        scratch_shapes=[pltpu.VMEM((9, 3, 1, 64, 128), F32)],
        cost_estimate=pl.CostEstimate(flops=100000000, bytes_accessed=900000, transcendentals=0),
        compiler_params=PARAMS,
        name="far_prep",
    )(req, tgt.reshape(320, 128))


def far_leaf_kernel(counts, flat, src, ft, out, fs, vals, t0, t1):
    for y in range(8):
        prepare_sources(y, [src[y, 64 + 8 * c : 72 + 8 * c, :] for c in range(3)], t0.at[y], t1.at[y], fs)
        for l in range(OWN):
            vals[8 * y + l] = two_halves(src[y, 8 * l : 8 * l + 8, :])
    clear_dummy(fs, vals)
    out[...] = jnp.zeros_like(out)

    def add(t, v):
        out[t >> 3, t & 7] += v

    interact(counts[0], flat, fs, ft, vals, add)


FAR_SCRATCH = [
    pltpu.VMEM((65, 16, 128), F32),
    pltpu.VMEM((65, 16, 128), BF16),
    pltpu.VMEM((8, 1, 64, 128), F32),
    pltpu.VMEM((8, 1, 64, 128), F32),
]


def far_leaf(counts, flat, src, ft):
    return pl.pallas_call(
        far_leaf_kernel,
        in_specs=[SMEM, SMEM, VMEM, VMEM],
        out_specs=VMEM,
        out_shape=jax.ShapeDtypeStruct((8, 9, 8, 128), F32),
        scratch_shapes=FAR_SCRATCH,
        cost_estimate=pl.CostEstimate(flops=2097152000, bytes_accessed=900000, transcendentals=4194304),
        compiler_params=PARAMS,
        name="far_leaf",
    )(counts, flat, src, ft)


def cells_kernel(along_u, along_v, out, slab):
    for y in range(8):
        slab[0, 8 * y : 8 * y + 8, :] = along_u[y, 88:96, :]
        slab[1, 8 * y : 8 * y + 8, :] = along_v[y, 32:40, :]
        for c in range(3):
            slab[0, 64 + 8 * c + y : 65 + 8 * c + y, :] = along_u[y, 96 + c : 97 + c, :]
            slab[1, 64 + 8 * c + y : 65 + 8 * c + y, :] = along_v[y, 24 + c : 25 + c, :]
    odd = odd_group()
    for d in range(8):
        out[d] = slab[(d % 2) ^ odd]


def cells_message(along_u, along_v):
    return pl.pallas_call(
        cells_kernel,
        in_specs=[VMEM] * 2,
        out_specs=VMEM,
        out_shape=jax.ShapeDtypeStruct((8, 88, 128), F32),
        scratch_shapes=[pltpu.VMEM((2, 88, 128), F32)],
        compiler_params=PARAMS,
        name="cells",
    )(along_u, along_v)


def far_top_kernel(counts, flat, src, ft, part, out, fs, vals, t0, t1):
    for g in range(8):
        xyz = [src[g, 64 + 8 * c : 72 + 8 * c, :] for c in range(3)]
        prepare_sources(g, xyz, t0.at[g], t1.at[g], fs)
        for y in range(8):
            vals[8 * g + y] = two_halves(src[g, 8 * y : 8 * y + 8, :])
    clear_dummy(fs, vals)
    out[...] = part[...]

    def add(t, v):
        out[t, 8] += v

    interact(counts[1], flat, fs, ft, vals, add)


def far_top(counts, flat, src, ft, part):
    return pl.pallas_call(
        far_top_kernel,
        in_specs=[SMEM, SMEM, VMEM, VMEM, VMEM],
        out_specs=VMEM,
        out_shape=jax.ShapeDtypeStruct((8, 9, 8, 128), F32),
        scratch_shapes=FAR_SCRATCH,
        compiler_params=PARAMS,
        name="far_top",
    )(counts, flat, src, ft, part)


def final_kernel(got, utm, up, near1, near2, out):
    tot = got[0]
    for d in range(1, 8):
        tot = tot + got[d]
    cell = tot[8]
    for l in range(OWN):
        incoming = tot[l] + dot3(cell, utm[l])
        out[l] = near1[l] + near2[l] + dot3(incoming, up[l])


def final(got, utm, up, near1, near2):
    return pl.pallas_call(
        final_kernel,
        in_specs=[VMEM] * 5,
        out_specs=VMEM,
        out_shape=jax.ShapeDtypeStruct((8, 8, 256), F32),
        compiler_params=PARAMS,
        name="final",
    )(got, utm, up, near1, near2)


def device(g, u, v):
    return g * 64 + (v * 8 + u if g % 2 else u * 8 + v)


def body(points, charges, up_op, skel_pts, utm, cell_pts, near_list, leaf_list, top_list):
    r = range(8)
    along_u = [[device(g, u, v) for u in r] for g in r for v in r]
    along_v = [[device(g, u, v) for v in r] for g in r for u in r]
    along_g = [[g * 64 + i for g in r] for i in range(64)]

    def exchange(x, groups):
        return lax.all_to_all(x, "d", 0, 0, axis_index_groups=groups, tiled=True)

    pts = jnp.transpose(points, (1, 0, 2))
    skel = jnp.transpose(skel_pts, (1, 0, 2))
    cpts = jnp.transpose(cell_pts, (1, 0, 2))
    count = lax.axis_size("d")
    up = [(i, i + 1) for i in range(count - 1)]
    down = [(i + 1, i) for i in range(count - 1)]
    m0, m1, first, last = pack(pts, charges, skel, cpts, leaf_list, top_list, up_op, utm)
    got0 = exchange(m0, along_v)
    before = lax.ppermute(last, "d", up)
    m1, got0, before = lax.optimization_barrier((m1, got0, before))
    got1 = exchange(m1, along_u)
    req = got0[:, 27:29, :].astype(jnp.int32)
    ft, ftop, leaf_flat, top_flat, counts = far_prep(req, got0)
    near1 = near_part(True, near_list, pts, charges, before)
    got1, near1, ft, counts = lax.optimization_barrier((got1, near1, ft, counts))
    gotg = exchange(cells_message(got1, got0), along_g)
    part = far_leaf(counts, leaf_flat, got1, ft)
    part = far_top(counts, top_flat, gotg, ftop, part)
    part, first = lax.optimization_barrier((part, first))
    gotr = exchange(part, along_v)
    after = lax.ppermute(first, "d", down)
    near2 = near_part(False, near_list, pts, after)
    return final(gotr, utm, up_op, near1, near2)


def solution(mesh):
    line = Mesh(mesh.devices.reshape(-1), ("d",))
    specs = tuple(P("d", *([None] * k)) for k in (2, 2, 2, 2, 2, 2, 1, 1, 1))
    return jax.shard_map(body, mesh=line, in_specs=specs, out_specs=P("d", None, None), check_vma=False)
```

```python
import functools
import math

import jax
import jax.numpy as jnp
from jax import lax
from jax.experimental import pallas as pl
from jax.experimental.pallas import tpu as pltpu
from jax.sharding import Mesh, PartitionSpec as P

F32 = jnp.float32
BF16 = jnp.bfloat16
KAPPA = math.sqrt(3.0) * math.log2(math.e)
LN2 = math.log(2.0)
CENTER = 1.5
FEAT = 32
REACH = 4
OWN = 8
NBR = 9
PAIRS = 16
DUMMY = 64
CHUNK = 16
NEAR_DUMMY = 16
FIRST_OWN = 16

SMEM = pl.BlockSpec(memory_space=pltpu.SMEM)
HBM = pl.BlockSpec(memory_space=pltpu.HBM)
VMEM = pl.BlockSpec(memory_space=pltpu.VMEM)
PARAMS = pltpu.CompilerParams(vmem_limit_bytes=40 << 20)
WIDE = pltpu.CompilerParams(vmem_limit_bytes=60 << 20)


def split2(x):
    a = x.astype(BF16).astype(F32)
    return a, (x - a).astype(BF16).astype(F32)


def split3(x):
    a = x.astype(BF16).astype(F32)
    b, c = split2(x - a)
    return a, b, c


def dense_features(xyz):
    parts = [split2((x - CENTER) * KAPPA) for x in xyz]
    n = None
    for a, b in parts:
        r = a + b
        n = r * r if n is None else n + r * r
    n1, n2, n3 = split3(n)
    one = jnp.ones_like(n)
    zero = jnp.zeros_like(n)
    high = [a for a, _ in parts]
    low = [b for _, b in parts]
    high2 = [-2.0 * a for a in high]
    low2 = [-2.0 * b for b in low]
    s0 = high + [n1, n2, n3, one, one]
    s1 = low + [one, zero, zero, zero, zero]
    t0 = high2 + [one, one, one, n1, n2]
    t1 = low2 + [zero] * 5
    t2 = high2 + [n3] + [zero] * 4
    return s0, s1, t0, t1, t2


def spread(rows, tmp):
    n, width = rows[0].shape
    halves = width // 128
    for r, v in enumerate(rows):
        for h in range(halves):
            tmp[h, n * r : n * r + n, :] = v[:, 128 * h : 128 * h + 128]

    def load(leaf):
        return jnp.concatenate([tmp[h, pl.ds(leaf, 8, stride=n), :] for h in range(halves)], 1)

    return load


def two_halves(vals):
    v = vals * LN2
    high = v.astype(BF16).astype(F32)
    return jnp.concatenate([high, v - high], 0).astype(BF16)


def matern_over_ln2(t):
    m = jnp.maximum(t, 1e-12)
    s = m * lax.rsqrt(m)
    return (s + 1.0 / LN2) * jnp.exp2(-s)


def product(src_feat, tgt_feat, vals):
    t = jnp.dot(src_feat, tgt_feat, preferred_element_type=F32)
    k = matern_over_ln2(t)
    high = k.astype(BF16)
    low = (k - high.astype(F32)).astype(BF16)
    return jnp.dot(vals, high, preferred_element_type=F32) + jnp.dot(vals, low, preferred_element_type=F32)


def in_chunks(n, size, step):
    half = size // 2
    big = (n + half - 1) // size

    def full(i, carry):
        step(i * size, size)
        return carry

    def rest(i, carry):
        step(big * size, half)
        return carry

    lax.fori_loop(0, big, full, 0)
    lax.fori_loop(0, (n > big * size).astype(jnp.int32), rest, 0)


def dot3(a, b, transposed=False):
    ah = a.astype(BF16).astype(F32)
    both = jnp.concatenate([ah, a - ah], 0).astype(BF16)
    bh = b.astype(BF16)
    bl = (b - bh.astype(F32)).astype(BF16)
    dims = (((1,), (1 if transposed else 0,)), ((), ()))
    r = lax.dot_general(both, bh, dims, preferred_element_type=F32)
    r = r + lax.dot_general(both, bl, dims, preferred_element_type=F32)
    return r[0:8] + r[8:16]


def odd_group():
    return (lax.axis_index("d") >> 6) & 1


def fetch(pairs, sems, at):
    copies = [pltpu.make_async_copy(a, b, sems.at[at + i]) for i, (a, b) in enumerate(pairs)]
    for c in copies:
        c.start()
    return copies


def pack_kernel(
    pts_h, chg_h, skel_h, cpts_h, llist_h, tlist_h, up_h, utm_h,
    m0_h, m1_h, first_h, last_h,
    pts, chg, skel, cpts, llist, tlist, up, utm, m0, m1, first, last, row16, sems,
):
    ins = ((llist_h, llist), (tlist_h, tlist), (skel_h, skel), (cpts_h, cpts), (chg_h, chg), (pts_h, pts), (up_h, up), (utm_h, utm))
    copies = fetch(ins, sems, 0)
    for c in copies[0:2]:
        c.wait()
    lane = lax.broadcasted_iota(jnp.int32, (1, 128), 1)
    sub8 = lax.broadcasted_iota(jnp.int32, (8, 128), 0)
    lane8 = lax.broadcasted_iota(jnp.int32, (8, 128), 1)
    row = lax.broadcasted_iota(jnp.int32, (128, 128), 0)
    col = lax.broadcasted_iota(jnp.int32, (128, 128), 1)
    before = (row < col).astype(F32).astype(BF16)
    pick = (lax.broadcasted_iota(jnp.int32, (16, 128), 0) == (lax.broadcasted_iota(jnp.int32, (16, 128), 1) & 15))
    pick = pick.astype(F32).astype(BF16)
    ll = llist[...]
    mine = sub8 == (lane8 >> 4)

    def flat(v):
        w = jnp.dot(v.astype(F32).astype(BF16), pick, preferred_element_type=F32)
        return jnp.sum(jnp.where(mine, w, 0.0), axis=0, keepdims=True).astype(jnp.int32)

    upper = flat(ll >> 6) & 7
    lower = flat(ll & 63)
    row16[...] = jnp.zeros((8, 128), jnp.int32)
    row16[0:1, 0:16] = tlist[...]
    tl = row16[0:1, :]
    odd = odd_group() == 1
    leaf_u = jnp.where(odd, lower >> 3, upper)
    leaf_v = jnp.where(odd, upper, lower >> 3)
    top_u = jnp.where(odd, tl & 7, (tl >> 3) & 7)
    top_v = jnp.where(odd, (tl >> 3) & 7, tl & 7)
    leaf_hit = leaf_v == sub8
    top_hit = (top_v == sub8) & (lane < 16)
    leaf_one = leaf_hit.astype(F32)
    top_one = top_hit.astype(F32)
    leaf_pos = jnp.dot(leaf_one.astype(BF16), before, preferred_element_type=F32)
    top_pos = jnp.dot(top_one.astype(BF16), before, preferred_element_type=F32) + 16.0
    leaf_n = jnp.sum(leaf_one, axis=1, keepdims=True)
    top_n = jnp.sum(top_one, axis=1, keepdims=True)
    leaf_pos = jnp.where(leaf_hit, leaf_pos, -1.0)
    top_pos = jnp.where(top_hit, top_pos, -1.0)
    local = (lower & 7) + leaf_u * 8
    codes = jnp.where(sub8 == 0, lane >> 4, jnp.where(sub8 == 1, local, 0)).astype(F32).astype(BF16)
    tcodes = jnp.where(sub8 == 0, (tl >> 6) * 8 + top_u, 0).astype(F32).astype(BF16)
    rowf = row.astype(F32)
    for c in copies[2:6]:
        c.wait()
    for d in range(8):
        for c in range(3):
            m0[d, 8 * c : 8 * c + 8, :] = skel[c]
            m0[d, 24 + c : 25 + c, :] = cpts[c]
        m0[d, 29:32, :] = jnp.zeros((3, 128), F32)
        oh = (leaf_pos[d : d + 1] == rowf).astype(F32).astype(BF16)
        got = lax.dot_general(codes, oh, (((1,), (1,)), ((), ())), preferred_element_type=F32)
        m0[d, 27:28, :] = got[0:1] * 128.0 + got[1:2]
        oh = (top_pos[d : d + 1] == rowf).astype(F32).astype(BF16)
        got = lax.dot_general(tcodes, oh, (((1,), (1,)), ((), ())), preferred_element_type=F32)[0:1]
        got = got + jnp.where(lane == 0, leaf_n[d : d + 1], 0.0) + jnp.where(lane == 1, top_n[d : d + 1], 0.0)
        m0[d, 28:29, :] = got
    for slab, start in ((first, 0), (last, OWN - REACH)):
        for i in range(REACH):
            slab[8 * i : 8 * i + 8, :] = chg[start + i]
        for c in range(3):
            slab[32 + 4 * c : 36 + 4 * c, :] = pts[c, start : start + REACH, :]
        slab[44:48, :] = jnp.zeros((4, 256), F32)
    outs = fetch(((first, first_h), (last, last_h)), sems, 8)
    m1[96:104, :] = jnp.zeros((8, 128), F32)
    for c in range(3):
        m1[64 + 8 * c : 72 + 8 * c, :] = skel[c]
        m1[96 + c : 97 + c, :] = cpts[c]
    copies[6].wait()
    own = [dot3(chg[l], up[l], True) for l in range(OWN)]
    for l in range(OWN):
        m1[8 * l : 8 * l + 8, :] = own[l]
    copies[7].wait()
    total = dot3(own[0], utm[0], True)
    for l in range(1, OWN):
        total = total + dot3(own[l], utm[l], True)
    m1[88:96, :] = total
    for d in range(8):
        m0[d, 32:40, :] = total
    outs += fetch([(m0, m0_h)] + [(m1, m1_h.at[d]) for d in range(8)], sems, 10)
    for c in outs:
        c.wait()


def pack(*args):
    sd = jax.ShapeDtypeStruct
    shapes = [(8, 40, 128), (104, 128), (48, 256), (48, 256)]
    return pl.pallas_call(
        pack_kernel,
        in_specs=[HBM] * 8,
        out_specs=[HBM] * 4,
        out_shape=[sd((8, 40, 128), F32), sd((8, 104, 128), F32), sd((48, 256), F32), sd((48, 256), F32)],
        scratch_shapes=[pltpu.VMEM(a.shape, a.dtype) for a in args]
        + [pltpu.VMEM(s, F32) for s in shapes]
        + [pltpu.VMEM((8, 128), jnp.int32), pltpu.SemaphoreType.DMA((19,))],
        compiler_params=WIDE,
        name="pack",
    )(*args)


FIRST, MIDDLE, LAST = range(3)


def near_blocks(ids, flat, base, first_leaf, stage):
    pos = jnp.int32(0)
    seen = jnp.int32(0)
    for l in range(first_leaf, OWN):
        for n in range(NBR):
            ident = ids[l, n]
            e = ident - base
            flat[pos] = l * 32 + e
            if stage == LAST:
                take = e >= REACH + OWN
            else:
                own = (e >= REACH) & (e < REACH + OWN)
                take = own & (seen < FIRST_OWN)
                if stage == MIDDLE:
                    take = (ident >= 0) & (e < REACH + OWN) & jnp.logical_not(take)
                seen = seen + own.astype(jnp.int32)
            pos = pos + take.astype(jnp.int32)
    for u in range(CHUNK):
        flat[pos + u] = (OWN - 1) * 32 + NEAR_DUMMY
    return pos


def near_setup(sources, leaves, xyz, vals_of, fs, ft, vals, ts, tl):
    s0, s1, t0, t1, t2 = dense_features(xyz)
    load0, load1 = spread(s0, ts.at[0]), spread(s1, tl)
    for e in sources:
        a, b = load0(e), load1(e)
        fs[e] = jnp.concatenate([a, b, a, b], 0).T.astype(BF16)
        vals[e] = two_halves(vals_of(e))
    vals[NEAR_DUMMY] = jnp.zeros((16, 256), BF16)
    fs[NEAR_DUMMY] = jnp.zeros((256, FEAT), BF16)
    load0, load1, load2 = spread(t0, ts.at[1]), spread(t1, ts.at[2]), spread(t2, ts.at[3])
    for l in leaves:
        e = l + REACH
        one = load1(e)
        ft[l, 0:16, :] = jnp.concatenate([load0(e), load2(e)], 0).astype(BF16)
        ft[l, 16:32, :] = jnp.concatenate([one, one], 0).astype(BF16)


def near_run(count, flat, start, out, fs, ft, vals):
    out[...] = jnp.zeros_like(out) if start is None else start[...]

    def step(start, size):
        for u in range(size):
            code = flat[start + u]
            l, e = code >> 5, code & 31
            r = product(fs[e], ft[l], vals[e])
            out[l] += r[0:8] + r[8:16]

    in_chunks(count, CHUNK, step)


def near_base():
    return lax.axis_index("d") * OWN - REACH


def near_first_kernel(ids, pts, chg, out, flat, fs, ft, vals, xyz, ts, tl):
    count = near_blocks(ids, flat, near_base(), 0, FIRST)
    for c in range(3):
        xyz[c] = jnp.zeros((16, 256), F32)
        xyz[c, 4:12, :] = pts[c]
    own = range(REACH, REACH + OWN)
    near_setup(own, range(OWN), [xyz[0], xyz[1], xyz[2]], lambda e: chg[e - REACH], fs, ft, vals, ts, tl)
    near_run(count, flat, None, out, fs, ft, vals)


def near_middle_kernel(ids, pts, chg, before, start, out, flat, fs, ft, vals, xyz, ts, tl):
    count = near_blocks(ids, flat, near_base(), 0, MIDDLE)
    for c in range(3):
        xyz[c, 0:4, :] = before[32 + 4 * c : 36 + 4 * c, :]
        xyz[c, 4:12, :] = pts[c]
        xyz[c, 12:16, :] = jnp.zeros((4, 256), F32)

    def vals_of(e):
        return before[8 * e : 8 * e + 8, :] if e < REACH else chg[e - REACH]

    near_setup(range(REACH + OWN), range(OWN), [xyz[0], xyz[1], xyz[2]], vals_of, fs, ft, vals, ts, tl)
    near_run(count, flat, start, out, fs, ft, vals)


def near_last_kernel(ids, pts, after, out, flat, fs, ft, vals, xyz, ts, tl):
    count = near_blocks(ids, flat, near_base(), OWN - REACH, LAST)
    for c in range(3):
        xyz[c, 0:4, :] = jnp.zeros((4, 256), F32)
        xyz[c, 4:12, :] = pts[c]
        xyz[c, 12:16, :] = after[32 + 4 * c : 36 + 4 * c, :]

    def vals_of(e):
        return after[8 * (e - REACH - OWN) : 8 * (e - REACH - OWN) + 8, :]

    halo = range(REACH + OWN, 2 * REACH + OWN)
    near_setup(halo, range(OWN - REACH, OWN), [xyz[0], xyz[1], xyz[2]], vals_of, fs, ft, vals, ts, tl)
    near_run(count, flat, None, out, fs, ft, vals)


def near_part(stage, *args):
    return pl.pallas_call(
        (near_first_kernel, near_middle_kernel, near_last_kernel)[stage],
        in_specs=[SMEM] + [VMEM] * (len(args) - 1),
        out_specs=VMEM,
        out_shape=jax.ShapeDtypeStruct((OWN, 8, 256), F32),
        scratch_shapes=[
            pltpu.SMEM((OWN * NBR + CHUNK + 8,), jnp.int32),
            pltpu.VMEM((17, 256, FEAT), BF16),
            pltpu.VMEM((OWN, FEAT, 256), BF16),
            pltpu.VMEM((17, 16, 256), BF16),
            pltpu.VMEM((3, 16, 256), F32),
            pltpu.VMEM((4, 2, 128, 128), F32),
            pltpu.VMEM((2, 128, 128), F32),
        ],
        cost_estimate=pl.CostEstimate(flops=2000000000, bytes_accessed=300000, transcendentals=4194304),
        compiler_params=PARAMS,
        name="near",
    )(*args)


def prepare_sources(i, xyz, t0, t1, feat):
    s0, s1, _, _, _ = dense_features(xyz)
    s0 = spread(s0, t0)
    s1 = spread(s1, t1)
    for l in range(8):
        feat[8 * i + l, 0:8, :] = s0(l)
        feat[8 * i + l, 8:16, :] = s1(l)


def prepare_targets(i, xyz, tmp, ft):
    _, _, t0, t1, t2 = dense_features(xyz)
    load0, load1, load2 = spread(t0, tmp.at[0]), spread(t1, tmp.at[1]), spread(t2, tmp.at[2])
    for l in range(8):
        one = load1(l)
        ft[8 * i + l, 0:16, :] = jnp.concatenate([load0(l), load2(l)], 0).astype(BF16)
        ft[8 * i + l, 16:32, :] = jnp.concatenate([one, one], 0).astype(BF16)


def flatten(req, flat, row, start, slot):
    off = 0
    for d in range(8):
        n = req[d, 1, slot]

        def copy(j, carry, d=d, off=off):
            for u in range(8):
                flat[off + j * 8 + u] = req[d, row, start + j * 8 + u] + d * (1024 if row == 0 else 128)
            return carry

        lax.fori_loop(0, (n + 7) // 8, copy, 0)
        off = off + n
    for u in range(2 * PAIRS):
        flat[off + u] = DUMMY
    return off


def interact(total, flat, fs, ft, vals, add):
    zero = jnp.zeros((FEAT, 128), BF16)

    def step(start, size):
        for u in range(size // 2):
            ca = flat[start + 2 * u]
            cb = flat[start + 2 * u + 1]
            ta, sa = ca >> 7, ca & 127
            tb, sb = cb >> 7, cb & 127
            fa = ft[ta]
            fb = ft[tb]
            tgt = jnp.concatenate([jnp.concatenate([fa, zero], 1), jnp.concatenate([zero, fb], 1)], 0)
            ra, rb = fs[sa], fs[sb]
            src = jnp.concatenate([ra, ra, rb, rb], 0).T.astype(BF16)
            r = product(src, tgt, jnp.concatenate([vals[sa], vals[sb]], 0))
            add(ta, r[0:8, 0:128] + r[8:16, 0:128])
            add(tb, r[16:24, 128:256] + r[24:32, 128:256])

    in_chunks(total, 2 * PAIRS, step)


def clear_dummy(fs, vals):
    fs[DUMMY] = jnp.zeros((16, 128), F32)
    vals[DUMMY] = jnp.zeros((16, 128), BF16)


def far_prep_kernel(req, tgt, ft, ftop, leaf_flat, top_flat, counts, tmp):
    for d in range(8):
        prepare_targets(d, [tgt[40 * d + 8 * c : 40 * d + 8 * c + 8, :] for c in range(3)], tmp.at[d], ft)
    prepare_targets(0, [tgt[pl.ds(24 + c, 8, stride=40), :] for c in range(3)], tmp.at[8], ftop)
    counts[0] = flatten(req, leaf_flat, 0, 0, 0)
    counts[1] = flatten(req, top_flat, 1, 16, 1)


def far_prep(req, tgt):
    sd = jax.ShapeDtypeStruct
    return pl.pallas_call(
        far_prep_kernel,
        in_specs=[SMEM, VMEM],
        out_specs=[VMEM, VMEM, SMEM, SMEM, SMEM],
        out_shape=[
            sd((64, FEAT, 128), BF16),
            sd((8, FEAT, 128), BF16),
            sd((1024 + 64,), jnp.int32),
            sd((256,), jnp.int32),
            sd((2,), jnp.int32),
        ],
        scratch_shapes=[pltpu.VMEM((9, 3, 1, 64, 128), F32)],
        cost_estimate=pl.CostEstimate(flops=100000000, bytes_accessed=900000, transcendentals=0),
        compiler_params=PARAMS,
        name="far_prep",
    )(req, tgt.reshape(320, 128))


def far_leaf_kernel(counts, flat, src, ft, out, fs, vals, t0, t1):
    for y in range(8):
        prepare_sources(y, [src[y, 64 + 8 * c : 72 + 8 * c, :] for c in range(3)], t0.at[y], t1.at[y], fs)
        for l in range(OWN):
            vals[8 * y + l] = two_halves(src[y, 8 * l : 8 * l + 8, :])
    clear_dummy(fs, vals)
    out[...] = jnp.zeros_like(out)

    def add(t, v):
        out[t >> 3, t & 7] += v

    interact(counts[0], flat, fs, ft, vals, add)


FAR_SCRATCH = [
    pltpu.VMEM((65, 16, 128), F32),
    pltpu.VMEM((65, 16, 128), BF16),
    pltpu.VMEM((8, 1, 64, 128), F32),
    pltpu.VMEM((8, 1, 64, 128), F32),
]


def far_leaf(counts, flat, src, ft):
    return pl.pallas_call(
        far_leaf_kernel,
        in_specs=[SMEM, SMEM, VMEM, VMEM],
        out_specs=VMEM,
        out_shape=jax.ShapeDtypeStruct((8, 9, 8, 128), F32),
        scratch_shapes=FAR_SCRATCH,
        cost_estimate=pl.CostEstimate(flops=2097152000, bytes_accessed=900000, transcendentals=4194304),
        compiler_params=PARAMS,
        name="far_leaf",
    )(counts, flat, src, ft)


def cells_kernel(along_u, along_v, out, slab):
    for y in range(8):
        slab[0, 8 * y : 8 * y + 8, :] = along_u[y, 88:96, :]
        slab[1, 8 * y : 8 * y + 8, :] = along_v[y, 32:40, :]
        for c in range(3):
            slab[0, 64 + 8 * c + y : 65 + 8 * c + y, :] = along_u[y, 96 + c : 97 + c, :]
            slab[1, 64 + 8 * c + y : 65 + 8 * c + y, :] = along_v[y, 24 + c : 25 + c, :]
    odd = odd_group()
    for d in range(8):
        out[d] = slab[(d % 2) ^ odd]


def cells_message(along_u, along_v):
    return pl.pallas_call(
        cells_kernel,
        in_specs=[VMEM] * 2,
        out_specs=VMEM,
        out_shape=jax.ShapeDtypeStruct((8, 88, 128), F32),
        scratch_shapes=[pltpu.VMEM((2, 88, 128), F32)],
        compiler_params=PARAMS,
        name="cells",
    )(along_u, along_v)


def far_top_kernel(counts, flat, src, ft, part, out, fs, vals, t0, t1):
    for g in range(8):
        xyz = [src[g, 64 + 8 * c : 72 + 8 * c, :] for c in range(3)]
        prepare_sources(g, xyz, t0.at[g], t1.at[g], fs)
        for y in range(8):
            vals[8 * g + y] = two_halves(src[g, 8 * y : 8 * y + 8, :])
    clear_dummy(fs, vals)
    out[...] = part[...]

    def add(t, v):
        out[t, 8] += v

    interact(counts[1], flat, fs, ft, vals, add)


def far_top(counts, flat, src, ft, part):
    return pl.pallas_call(
        far_top_kernel,
        in_specs=[SMEM, SMEM, VMEM, VMEM, VMEM],
        out_specs=VMEM,
        out_shape=jax.ShapeDtypeStruct((8, 9, 8, 128), F32),
        scratch_shapes=FAR_SCRATCH,
        compiler_params=PARAMS,
        name="far_top",
    )(counts, flat, src, ft, part)


def final_kernel(got, utm, up, near1, near2, out):
    tot = got[0]
    for d in range(1, 8):
        tot = tot + got[d]
    cell = tot[8]
    for l in range(OWN):
        incoming = tot[l] + dot3(cell, utm[l])
        out[l] = near1[l] + near2[l] + dot3(incoming, up[l])


def final(got, utm, up, near1, near2):
    return pl.pallas_call(
        final_kernel,
        in_specs=[VMEM] * 5,
        out_specs=VMEM,
        out_shape=jax.ShapeDtypeStruct((8, 8, 256), F32),
        compiler_params=PARAMS,
        name="final",
    )(got, utm, up, near1, near2)


def device(g, u, v):
    return g * 64 + (v * 8 + u if g % 2 else u * 8 + v)


def body(points, charges, up_op, skel_pts, utm, cell_pts, near_list, leaf_list, top_list):
    r = range(8)
    along_u = [[device(g, u, v) for u in r] for g in r for v in r]
    along_v = [[device(g, u, v) for v in r] for g in r for u in r]
    along_g = [[g * 64 + i for g in r] for i in range(64)]

    def exchange(x, groups):
        return lax.all_to_all(x, "d", 0, 0, axis_index_groups=groups, tiled=True)

    pts = jnp.transpose(points, (1, 0, 2))
    skel = jnp.transpose(skel_pts, (1, 0, 2))
    cpts = jnp.transpose(cell_pts, (1, 0, 2))
    count = lax.axis_size("d")
    up = [(i, i + 1) for i in range(count - 1)]
    down = [(i + 1, i) for i in range(count - 1)]
    m0, m1, first, last = pack(pts, charges, skel, cpts, leaf_list, top_list, up_op, utm)
    m0, charges1 = lax.optimization_barrier((m0, charges))
    got0 = exchange(m0, along_v)
    before = lax.ppermute(last, "d", up)
    near0 = near_part(FIRST, near_list, pts, charges1)
    m1, got0, before, near0 = lax.optimization_barrier((m1, got0, before, near0))
    got1 = exchange(m1, along_u)
    req = got0[:, 27:29, :].astype(jnp.int32)
    ft, ftop, leaf_flat, top_flat, counts = far_prep(req, got0)
    near1 = near_part(MIDDLE, near_list, pts, charges, before, near0)
    got1, near1, ft, counts = lax.optimization_barrier((got1, near1, ft, counts))
    gotg = exchange(cells_message(got1, got0), along_g)
    part = far_leaf(counts, leaf_flat, got1, ft)
    part = far_top(counts, top_flat, gotg, ftop, part)
    part, first = lax.optimization_barrier((part, first))
    gotr = exchange(part, along_v)
    after = lax.ppermute(first, "d", down)
    near2 = near_part(LAST, near_list, pts, after)
    return final(gotr, utm, up_op, near1, near2)


def solution(mesh):
    line = Mesh(mesh.devices.reshape(-1), ("d",))
    specs = tuple(P("d", *([None] * k)) for k in (2, 2, 2, 2, 2, 2, 1, 1, 1))
    return jax.shard_map(body, mesh=line, in_specs=specs, out_specs=P("d", None, None), check_vma=False)
```

```python
import functools
import math

import jax
import jax.numpy as jnp
from jax import lax
from jax.experimental import pallas as pl
from jax.experimental.pallas import tpu as pltpu
from jax.sharding import Mesh, PartitionSpec as P

F32 = jnp.float32
BF16 = jnp.bfloat16
KAPPA = math.sqrt(3.0) * math.log2(math.e)
LN2 = math.log(2.0)
CENTER = 1.5
FEAT = 32
REACH = 4
OWN = 8
NBR = 9
PAIRS = 16
DUMMY = 64
CHUNK = 16
NEAR_DUMMY = 16
FIRST_OWN = 24

SMEM = pl.BlockSpec(memory_space=pltpu.SMEM)
HBM = pl.BlockSpec(memory_space=pltpu.HBM)
VMEM = pl.BlockSpec(memory_space=pltpu.VMEM)
PARAMS = pltpu.CompilerParams(vmem_limit_bytes=40 << 20)
WIDE = pltpu.CompilerParams(vmem_limit_bytes=60 << 20)


def split2(x):
    a = x.astype(BF16).astype(F32)
    return a, (x - a).astype(BF16).astype(F32)


def split3(x):
    a = x.astype(BF16).astype(F32)
    b, c = split2(x - a)
    return a, b, c


def dense_features(xyz):
    parts = [split2((x - CENTER) * KAPPA) for x in xyz]
    n = None
    for a, b in parts:
        r = a + b
        n = r * r if n is None else n + r * r
    n1, n2, n3 = split3(n)
    one = jnp.ones_like(n)
    zero = jnp.zeros_like(n)
    high = [a for a, _ in parts]
    low = [b for _, b in parts]
    high2 = [-2.0 * a for a in high]
    low2 = [-2.0 * b for b in low]
    s0 = high + [n1, n2, n3, one, one]
    s1 = low + [one, zero, zero, zero, zero]
    t0 = high2 + [one, one, one, n1, n2]
    t1 = low2 + [zero] * 5
    t2 = high2 + [n3] + [zero] * 4
    return s0, s1, t0, t1, t2


def spread(rows, tmp):
    n, width = rows[0].shape
    halves = width // 128
    for r, v in enumerate(rows):
        for h in range(halves):
            tmp[h, n * r : n * r + n, :] = v[:, 128 * h : 128 * h + 128]

    def load(leaf):
        return jnp.concatenate([tmp[h, pl.ds(leaf, 8, stride=n), :] for h in range(halves)], 1)

    return load


def two_halves(vals):
    v = vals * LN2
    high = v.astype(BF16).astype(F32)
    return jnp.concatenate([high, v - high], 0).astype(BF16)


def matern_over_ln2(t):
    m = jnp.maximum(t, 1e-12)
    s = m * lax.rsqrt(m)
    return (s + 1.0 / LN2) * jnp.exp2(-s)


def product(src_feat, tgt_feat, vals):
    t = jnp.dot(src_feat, tgt_feat, preferred_element_type=F32)
    k = matern_over_ln2(t)
    high = k.astype(BF16)
    low = (k - high.astype(F32)).astype(BF16)
    return jnp.dot(vals, high, preferred_element_type=F32) + jnp.dot(vals, low, preferred_element_type=F32)


def in_chunks(n, size, step):
    half = size // 2
    big = (n + half - 1) // size

    def full(i, carry):
        step(i * size, size)
        return carry

    def rest(i, carry):
        step(big * size, half)
        return carry

    lax.fori_loop(0, big, full, 0)
    lax.fori_loop(0, (n > big * size).astype(jnp.int32), rest, 0)


def dot3(a, b, transposed=False):
    ah = a.astype(BF16).astype(F32)
    both = jnp.concatenate([ah, a - ah], 0).astype(BF16)
    bh = b.astype(BF16)
    bl = (b - bh.astype(F32)).astype(BF16)
    dims = (((1,), (1 if transposed else 0,)), ((), ()))
    r = lax.dot_general(both, bh, dims, preferred_element_type=F32)
    r = r + lax.dot_general(both, bl, dims, preferred_element_type=F32)
    return r[0:8] + r[8:16]


def odd_group():
    return (lax.axis_index("d") >> 6) & 1


def fetch(pairs, sems, at):
    copies = [pltpu.make_async_copy(a, b, sems.at[at + i]) for i, (a, b) in enumerate(pairs)]
    for c in copies:
        c.start()
    return copies


def pack_kernel(
    pts_h, chg_h, skel_h, cpts_h, llist_h, tlist_h, up_h, utm_h,
    m0_h, m1_h, first_h, last_h,
    pts, chg, skel, cpts, llist, tlist, up, utm, m0, m1, first, last, row16, sems,
):
    ins = ((llist_h, llist), (tlist_h, tlist), (skel_h, skel), (cpts_h, cpts), (chg_h, chg), (pts_h, pts), (up_h, up), (utm_h, utm))
    copies = fetch(ins, sems, 0)
    for c in copies[0:2]:
        c.wait()
    lane = lax.broadcasted_iota(jnp.int32, (1, 128), 1)
    sub8 = lax.broadcasted_iota(jnp.int32, (8, 128), 0)
    lane8 = lax.broadcasted_iota(jnp.int32, (8, 128), 1)
    row = lax.broadcasted_iota(jnp.int32, (128, 128), 0)
    col = lax.broadcasted_iota(jnp.int32, (128, 128), 1)
    before = (row < col).astype(F32).astype(BF16)
    pick = (lax.broadcasted_iota(jnp.int32, (16, 128), 0) == (lax.broadcasted_iota(jnp.int32, (16, 128), 1) & 15))
    pick = pick.astype(F32).astype(BF16)
    ll = llist[...]
    mine = sub8 == (lane8 >> 4)

    def flat(v):
        w = jnp.dot(v.astype(F32).astype(BF16), pick, preferred_element_type=F32)
        return jnp.sum(jnp.where(mine, w, 0.0), axis=0, keepdims=True).astype(jnp.int32)

    upper = flat(ll >> 6) & 7
    lower = flat(ll & 63)
    row16[...] = jnp.zeros((8, 128), jnp.int32)
    row16[0:1, 0:16] = tlist[...]
    tl = row16[0:1, :]
    odd = odd_group() == 1
    leaf_u = jnp.where(odd, lower >> 3, upper)
    leaf_v = jnp.where(odd, upper, lower >> 3)
    top_u = jnp.where(odd, tl & 7, (tl >> 3) & 7)
    top_v = jnp.where(odd, (tl >> 3) & 7, tl & 7)
    leaf_hit = leaf_v == sub8
    top_hit = (top_v == sub8) & (lane < 16)
    leaf_one = leaf_hit.astype(F32)
    top_one = top_hit.astype(F32)
    leaf_pos = jnp.dot(leaf_one.astype(BF16), before, preferred_element_type=F32)
    top_pos = jnp.dot(top_one.astype(BF16), before, preferred_element_type=F32) + 16.0
    leaf_n = jnp.sum(leaf_one, axis=1, keepdims=True)
    top_n = jnp.sum(top_one, axis=1, keepdims=True)
    leaf_pos = jnp.where(leaf_hit, leaf_pos, -1.0)
    top_pos = jnp.where(top_hit, top_pos, -1.0)
    local = (lower & 7) + leaf_u * 8
    codes = jnp.where(sub8 == 0, lane >> 4, jnp.where(sub8 == 1, local, 0)).astype(F32).astype(BF16)
    tcodes = jnp.where(sub8 == 0, (tl >> 6) * 8 + top_u, 0).astype(F32).astype(BF16)
    rowf = row.astype(F32)
    for c in copies[2:6]:
        c.wait()
    for d in range(8):
        for c in range(3):
            m0[d, 8 * c : 8 * c + 8, :] = skel[c]
            m0[d, 24 + c : 25 + c, :] = cpts[c]
        m0[d, 29:32, :] = jnp.zeros((3, 128), F32)
        oh = (leaf_pos[d : d + 1] == rowf).astype(F32).astype(BF16)
        got = lax.dot_general(codes, oh, (((1,), (1,)), ((), ())), preferred_element_type=F32)
        m0[d, 27:28, :] = got[0:1] * 128.0 + got[1:2]
        oh = (top_pos[d : d + 1] == rowf).astype(F32).astype(BF16)
        got = lax.dot_general(tcodes, oh, (((1,), (1,)), ((), ())), preferred_element_type=F32)[0:1]
        got = got + jnp.where(lane == 0, leaf_n[d : d + 1], 0.0) + jnp.where(lane == 1, top_n[d : d + 1], 0.0)
        m0[d, 28:29, :] = got
    for slab, start in ((first, 0), (last, OWN - REACH)):
        for i in range(REACH):
            slab[8 * i : 8 * i + 8, :] = chg[start + i]
        for c in range(3):
            slab[32 + 4 * c : 36 + 4 * c, :] = pts[c, start : start + REACH, :]
        slab[44:48, :] = jnp.zeros((4, 256), F32)
    outs = fetch(((first, first_h), (last, last_h)), sems, 8)
    m1[96:104, :] = jnp.zeros((8, 128), F32)
    for c in range(3):
        m1[64 + 8 * c : 72 + 8 * c, :] = skel[c]
        m1[96 + c : 97 + c, :] = cpts[c]
    copies[6].wait()
    own = [dot3(chg[l], up[l], True) for l in range(OWN)]
    for l in range(OWN):
        m1[8 * l : 8 * l + 8, :] = own[l]
    copies[7].wait()
    total = dot3(own[0], utm[0], True)
    for l in range(1, OWN):
        total = total + dot3(own[l], utm[l], True)
    m1[88:96, :] = total
    for d in range(8):
        m0[d, 32:40, :] = total
    outs += fetch([(m0, m0_h)] + [(m1, m1_h.at[d]) for d in range(8)], sems, 10)
    for c in outs:
        c.wait()


def pack(*args):
    sd = jax.ShapeDtypeStruct
    shapes = [(8, 40, 128), (104, 128), (48, 256), (48, 256)]
    return pl.pallas_call(
        pack_kernel,
        in_specs=[HBM] * 8,
        out_specs=[HBM] * 4,
        out_shape=[sd((8, 40, 128), F32), sd((8, 104, 128), F32), sd((48, 256), F32), sd((48, 256), F32)],
        scratch_shapes=[pltpu.VMEM(a.shape, a.dtype) for a in args]
        + [pltpu.VMEM(s, F32) for s in shapes]
        + [pltpu.VMEM((8, 128), jnp.int32), pltpu.SemaphoreType.DMA((19,))],
        compiler_params=WIDE,
        name="pack",
    )(*args)


FIRST, MIDDLE, LAST = range(3)


def near_blocks(ids, flat, base, first_leaf, stage):
    pos = jnp.int32(0)
    seen = jnp.int32(0)
    for l in range(first_leaf, OWN):
        for n in range(NBR):
            ident = ids[l, n]
            e = ident - base
            flat[pos] = l * 32 + e
            if stage == LAST:
                take = e >= REACH + OWN
            else:
                own = (e >= REACH) & (e < REACH + OWN)
                take = own & (seen < FIRST_OWN)
                if stage == MIDDLE:
                    take = (ident >= 0) & (e < REACH + OWN) & jnp.logical_not(take)
                seen = seen + own.astype(jnp.int32)
            pos = pos + take.astype(jnp.int32)
    for u in range(CHUNK):
        flat[pos + u] = (OWN - 1) * 32 + NEAR_DUMMY
    return pos


def near_setup(sources, leaves, xyz, vals_of, fs, ft, vals, ts, tl):
    s0, s1, t0, t1, t2 = dense_features(xyz)
    load0, load1 = spread(s0, ts.at[0]), spread(s1, tl)
    for e in sources:
        a, b = load0(e), load1(e)
        fs[e] = jnp.concatenate([a, b, a, b], 0).T.astype(BF16)
        vals[e] = two_halves(vals_of(e))
    vals[NEAR_DUMMY] = jnp.zeros((16, 256), BF16)
    fs[NEAR_DUMMY] = jnp.zeros((256, FEAT), BF16)
    load0, load1, load2 = spread(t0, ts.at[1]), spread(t1, ts.at[2]), spread(t2, ts.at[3])
    for l in leaves:
        e = l + REACH
        one = load1(e)
        ft[l, 0:16, :] = jnp.concatenate([load0(e), load2(e)], 0).astype(BF16)
        ft[l, 16:32, :] = jnp.concatenate([one, one], 0).astype(BF16)


def near_run(count, flat, start, out, fs, ft, vals):
    out[...] = jnp.zeros_like(out) if start is None else start[...]

    def step(start, size):
        for u in range(size):
            code = flat[start + u]
            l, e = code >> 5, code & 31
            r = product(fs[e], ft[l], vals[e])
            out[l] += r[0:8] + r[8:16]

    in_chunks(count, CHUNK, step)


def near_base():
    return lax.axis_index("d") * OWN - REACH


def near_first_kernel(ids, pts, chg, out, flat, fs, ft, vals, xyz, ts, tl):
    count = near_blocks(ids, flat, near_base(), 0, FIRST)
    for c in range(3):
        xyz[c] = jnp.zeros((16, 256), F32)
        xyz[c, 4:12, :] = pts[c]
    own = range(REACH, REACH + OWN)
    near_setup(own, range(OWN), [xyz[0], xyz[1], xyz[2]], lambda e: chg[e - REACH], fs, ft, vals, ts, tl)
    near_run(count, flat, None, out, fs, ft, vals)


def near_middle_kernel(ids, pts, chg, before, start, out, flat, fs, ft, vals, xyz, ts, tl):
    count = near_blocks(ids, flat, near_base(), 0, MIDDLE)
    for c in range(3):
        xyz[c, 0:4, :] = before[32 + 4 * c : 36 + 4 * c, :]
        xyz[c, 4:12, :] = pts[c]
        xyz[c, 12:16, :] = jnp.zeros((4, 256), F32)

    def vals_of(e):
        return before[8 * e : 8 * e + 8, :] if e < REACH else chg[e - REACH]

    near_setup(range(REACH + OWN), range(OWN), [xyz[0], xyz[1], xyz[2]], vals_of, fs, ft, vals, ts, tl)
    near_run(count, flat, start, out, fs, ft, vals)


def near_last_kernel(ids, pts, after, out, flat, fs, ft, vals, xyz, ts, tl):
    count = near_blocks(ids, flat, near_base(), OWN - REACH, LAST)
    for c in range(3):
        xyz[c, 0:4, :] = jnp.zeros((4, 256), F32)
        xyz[c, 4:12, :] = pts[c]
        xyz[c, 12:16, :] = after[32 + 4 * c : 36 + 4 * c, :]

    def vals_of(e):
        return after[8 * (e - REACH - OWN) : 8 * (e - REACH - OWN) + 8, :]

    halo = range(REACH + OWN, 2 * REACH + OWN)
    near_setup(halo, range(OWN - REACH, OWN), [xyz[0], xyz[1], xyz[2]], vals_of, fs, ft, vals, ts, tl)
    near_run(count, flat, None, out, fs, ft, vals)


def near_part(stage, *args):
    return pl.pallas_call(
        (near_first_kernel, near_middle_kernel, near_last_kernel)[stage],
        in_specs=[SMEM] + [VMEM] * (len(args) - 1),
        out_specs=VMEM,
        out_shape=jax.ShapeDtypeStruct((OWN, 8, 256), F32),
        scratch_shapes=[
            pltpu.SMEM((OWN * NBR + CHUNK + 8,), jnp.int32),
            pltpu.VMEM((17, 256, FEAT), BF16),
            pltpu.VMEM((OWN, FEAT, 256), BF16),
            pltpu.VMEM((17, 16, 256), BF16),
            pltpu.VMEM((3, 16, 256), F32),
            pltpu.VMEM((4, 2, 128, 128), F32),
            pltpu.VMEM((2, 128, 128), F32),
        ],
        cost_estimate=pl.CostEstimate(flops=2000000000, bytes_accessed=300000, transcendentals=4194304),
        compiler_params=PARAMS,
        name="near",
    )(*args)


def prepare_sources(i, xyz, t0, t1, feat):
    s0, s1, _, _, _ = dense_features(xyz)
    s0 = spread(s0, t0)
    s1 = spread(s1, t1)
    for l in range(8):
        feat[8 * i + l, 0:8, :] = s0(l)
        feat[8 * i + l, 8:16, :] = s1(l)


def prepare_targets(i, xyz, tmp, ft):
    _, _, t0, t1, t2 = dense_features(xyz)
    load0, load1, load2 = spread(t0, tmp.at[0]), spread(t1, tmp.at[1]), spread(t2, tmp.at[2])
    for l in range(8):
        one = load1(l)
        ft[8 * i + l, 0:16, :] = jnp.concatenate([load0(l), load2(l)], 0).astype(BF16)
        ft[8 * i + l, 16:32, :] = jnp.concatenate([one, one], 0).astype(BF16)


def flatten(req, flat, row, start, slot):
    off = 0
    for d in range(8):
        n = req[d, 1, slot]

        def copy(j, carry, d=d, off=off):
            for u in range(8):
                flat[off + j * 8 + u] = req[d, row, start + j * 8 + u] + d * (1024 if row == 0 else 128)
            return carry

        lax.fori_loop(0, (n + 7) // 8, copy, 0)
        off = off + n
    for u in range(2 * PAIRS):
        flat[off + u] = DUMMY
    return off


def interact(total, flat, fs, ft, vals, add):
    zero = jnp.zeros((FEAT, 128), BF16)

    def step(start, size):
        for u in range(size // 2):
            ca = flat[start + 2 * u]
            cb = flat[start + 2 * u + 1]
            ta, sa = ca >> 7, ca & 127
            tb, sb = cb >> 7, cb & 127
            fa = ft[ta]
            fb = ft[tb]
            tgt = jnp.concatenate([jnp.concatenate([fa, zero], 1), jnp.concatenate([zero, fb], 1)], 0)
            ra, rb = fs[sa], fs[sb]
            src = jnp.concatenate([ra, ra, rb, rb], 0).T.astype(BF16)
            r = product(src, tgt, jnp.concatenate([vals[sa], vals[sb]], 0))
            add(ta, r[0:8, 0:128] + r[8:16, 0:128])
            add(tb, r[16:24, 128:256] + r[24:32, 128:256])

    in_chunks(total, 2 * PAIRS, step)


def clear_dummy(fs, vals):
    fs[DUMMY] = jnp.zeros((16, 128), F32)
    vals[DUMMY] = jnp.zeros((16, 128), BF16)


def far_prep_kernel(req, tgt, ft, ftop, leaf_flat, top_flat, counts, tmp):
    for d in range(8):
        prepare_targets(d, [tgt[40 * d + 8 * c : 40 * d + 8 * c + 8, :] for c in range(3)], tmp.at[d], ft)
    prepare_targets(0, [tgt[pl.ds(24 + c, 8, stride=40), :] for c in range(3)], tmp.at[8], ftop)
    counts[0] = flatten(req, leaf_flat, 0, 0, 0)
    counts[1] = flatten(req, top_flat, 1, 16, 1)


def far_prep(req, tgt):
    sd = jax.ShapeDtypeStruct
    return pl.pallas_call(
        far_prep_kernel,
        in_specs=[SMEM, VMEM],
        out_specs=[VMEM, VMEM, SMEM, SMEM, SMEM],
        out_shape=[
            sd((64, FEAT, 128), BF16),
            sd((8, FEAT, 128), BF16),
            sd((1024 + 64,), jnp.int32),
            sd((256,), jnp.int32),
            sd((2,), jnp.int32),
        ],
        scratch_shapes=[pltpu.VMEM((9, 3, 1, 64, 128), F32)],
        cost_estimate=pl.CostEstimate(flops=100000000, bytes_accessed=900000, transcendentals=0),
        compiler_params=PARAMS,
        name="far_prep",
    )(req, tgt.reshape(320, 128))


def far_leaf_kernel(counts, flat, src, ft, out, fs, vals, t0, t1):
    for y in range(8):
        prepare_sources(y, [src[y, 64 + 8 * c : 72 + 8 * c, :] for c in range(3)], t0.at[y], t1.at[y], fs)
        for l in range(OWN):
            vals[8 * y + l] = two_halves(src[y, 8 * l : 8 * l + 8, :])
    clear_dummy(fs, vals)
    out[...] = jnp.zeros_like(out)

    def add(t, v):
        out[t >> 3, t & 7] += v

    interact(counts[0], flat, fs, ft, vals, add)


FAR_SCRATCH = [
    pltpu.VMEM((65, 16, 128), F32),
    pltpu.VMEM((65, 16, 128), BF16),
    pltpu.VMEM((8, 1, 64, 128), F32),
    pltpu.VMEM((8, 1, 64, 128), F32),
]


def far_leaf(counts, flat, src, ft):
    return pl.pallas_call(
        far_leaf_kernel,
        in_specs=[SMEM, SMEM, VMEM, VMEM],
        out_specs=VMEM,
        out_shape=jax.ShapeDtypeStruct((8, 9, 8, 128), F32),
        scratch_shapes=FAR_SCRATCH,
        cost_estimate=pl.CostEstimate(flops=2097152000, bytes_accessed=900000, transcendentals=4194304),
        compiler_params=PARAMS,
        name="far_leaf",
    )(counts, flat, src, ft)


def cells_kernel(along_u, along_v, out, slab):
    for y in range(8):
        slab[0, 8 * y : 8 * y + 8, :] = along_u[y, 88:96, :]
        slab[1, 8 * y : 8 * y + 8, :] = along_v[y, 32:40, :]
        for c in range(3):
            slab[0, 64 + 8 * c + y : 65 + 8 * c + y, :] = along_u[y, 96 + c : 97 + c, :]
            slab[1, 64 + 8 * c + y : 65 + 8 * c + y, :] = along_v[y, 24 + c : 25 + c, :]
    odd = odd_group()
    for d in range(8):
        out[d] = slab[(d % 2) ^ odd]


def cells_message(along_u, along_v):
    return pl.pallas_call(
        cells_kernel,
        in_specs=[VMEM] * 2,
        out_specs=VMEM,
        out_shape=jax.ShapeDtypeStruct((8, 88, 128), F32),
        scratch_shapes=[pltpu.VMEM((2, 88, 128), F32)],
        compiler_params=PARAMS,
        name="cells",
    )(along_u, along_v)


def far_top_kernel(counts, flat, src, ft, part, out, fs, vals, t0, t1):
    for g in range(8):
        xyz = [src[g, 64 + 8 * c : 72 + 8 * c, :] for c in range(3)]
        prepare_sources(g, xyz, t0.at[g], t1.at[g], fs)
        for y in range(8):
            vals[8 * g + y] = two_halves(src[g, 8 * y : 8 * y + 8, :])
    clear_dummy(fs, vals)
    out[...] = part[...]

    def add(t, v):
        out[t, 8] += v

    interact(counts[1], flat, fs, ft, vals, add)


def far_top(counts, flat, src, ft, part):
    return pl.pallas_call(
        far_top_kernel,
        in_specs=[SMEM, SMEM, VMEM, VMEM, VMEM],
        out_specs=VMEM,
        out_shape=jax.ShapeDtypeStruct((8, 9, 8, 128), F32),
        scratch_shapes=FAR_SCRATCH,
        compiler_params=PARAMS,
        name="far_top",
    )(counts, flat, src, ft, part)


def final_kernel(got, utm, up, near1, near2, out):
    tot = got[0]
    for d in range(1, 8):
        tot = tot + got[d]
    cell = tot[8]
    for l in range(OWN):
        incoming = tot[l] + dot3(cell, utm[l])
        out[l] = near1[l] + near2[l] + dot3(incoming, up[l])


def final(got, utm, up, near1, near2):
    return pl.pallas_call(
        final_kernel,
        in_specs=[VMEM] * 5,
        out_specs=VMEM,
        out_shape=jax.ShapeDtypeStruct((8, 8, 256), F32),
        compiler_params=PARAMS,
        name="final",
    )(got, utm, up, near1, near2)


def device(g, u, v):
    return g * 64 + (v * 8 + u if g % 2 else u * 8 + v)


def body(points, charges, up_op, skel_pts, utm, cell_pts, near_list, leaf_list, top_list):
    r = range(8)
    along_u = [[device(g, u, v) for u in r] for g in r for v in r]
    along_v = [[device(g, u, v) for v in r] for g in r for u in r]
    along_g = [[g * 64 + i for g in r] for i in range(64)]

    def exchange(x, groups):
        return lax.all_to_all(x, "d", 0, 0, axis_index_groups=groups, tiled=True)

    pts = jnp.transpose(points, (1, 0, 2))
    skel = jnp.transpose(skel_pts, (1, 0, 2))
    cpts = jnp.transpose(cell_pts, (1, 0, 2))
    count = lax.axis_size("d")
    up = [(i, i + 1) for i in range(count - 1)]
    down = [(i + 1, i) for i in range(count - 1)]
    m0, m1, first, last = pack(pts, charges, skel, cpts, leaf_list, top_list, up_op, utm)
    m0, charges1 = lax.optimization_barrier((m0, charges))
    got0 = exchange(m0, along_v)
    near0 = near_part(FIRST, near_list, pts, charges1)
    m1, got0, near0, last = lax.optimization_barrier((m1, got0, near0, last))
    got1 = exchange(m1, along_u)
    before = lax.ppermute(last, "d", up)
    req = got0[:, 27:29, :].astype(jnp.int32)
    ft, ftop, leaf_flat, top_flat, counts = far_prep(req, got0)
    ft, near0 = lax.optimization_barrier((ft, near0))
    near1 = near_part(MIDDLE, near_list, pts, charges, before, near0)
    got1, near1, ft, counts = lax.optimization_barrier((got1, near1, ft, counts))
    gotg = exchange(cells_message(got1, got0), along_g)
    part = far_leaf(counts, leaf_flat, got1, ft)
    part = far_top(counts, top_flat, gotg, ftop, part)
    part, first = lax.optimization_barrier((part, first))
    gotr = exchange(part, along_v)
    after = lax.ppermute(first, "d", down)
    near2 = near_part(LAST, near_list, pts, after)
    return final(gotr, utm, up_op, near1, near2)


def solution(mesh):
    line = Mesh(mesh.devices.reshape(-1), ("d",))
    specs = tuple(P("d", *([None] * k)) for k in (2, 2, 2, 2, 2, 2, 1, 1, 1))
    return jax.shard_map(body, mesh=line, in_specs=specs, out_specs=P("d", None, None), check_vma=False)
```

```python
import functools
import math

import jax
import jax.numpy as jnp
from jax import lax
from jax.experimental import pallas as pl
from jax.experimental.pallas import tpu as pltpu
from jax.sharding import Mesh, PartitionSpec as P

F32 = jnp.float32
BF16 = jnp.bfloat16
KAPPA = math.sqrt(3.0) * math.log2(math.e)
LN2 = math.log(2.0)
CENTER = 1.5
FEAT = 32
REACH = 4
OWN = 8
NBR = 9
PAIRS = 16
DUMMY = 64
CHUNK = 16
NEAR_DUMMY = 16
FIRST_OWN = 32

SMEM = pl.BlockSpec(memory_space=pltpu.SMEM)
HBM = pl.BlockSpec(memory_space=pltpu.HBM)
VMEM = pl.BlockSpec(memory_space=pltpu.VMEM)
PARAMS = pltpu.CompilerParams(vmem_limit_bytes=40 << 20)
WIDE = pltpu.CompilerParams(vmem_limit_bytes=60 << 20)


def split2(x):
    a = x.astype(BF16).astype(F32)
    return a, (x - a).astype(BF16).astype(F32)


def split3(x):
    a = x.astype(BF16).astype(F32)
    b, c = split2(x - a)
    return a, b, c


def dense_features(xyz):
    parts = [split2((x - CENTER) * KAPPA) for x in xyz]
    n = None
    for a, b in parts:
        r = a + b
        n = r * r if n is None else n + r * r
    n1, n2, n3 = split3(n)
    one = jnp.ones_like(n)
    zero = jnp.zeros_like(n)
    high = [a for a, _ in parts]
    low = [b for _, b in parts]
    high2 = [-2.0 * a for a in high]
    low2 = [-2.0 * b for b in low]
    s0 = high + [n1, n2, n3, one, one]
    s1 = low + [one, zero, zero, zero, zero]
    t0 = high2 + [one, one, one, n1, n2]
    t1 = low2 + [zero] * 5
    t2 = high2 + [n3] + [zero] * 4
    return s0, s1, t0, t1, t2


def spread(rows, tmp):
    n, width = rows[0].shape
    halves = width // 128
    for r, v in enumerate(rows):
        for h in range(halves):
            tmp[h, n * r : n * r + n, :] = v[:, 128 * h : 128 * h + 128]

    def load(leaf):
        return jnp.concatenate([tmp[h, pl.ds(leaf, 8, stride=n), :] for h in range(halves)], 1)

    return load


def two_halves(vals):
    v = vals * LN2
    high = v.astype(BF16).astype(F32)
    return jnp.concatenate([high, v - high], 0).astype(BF16)


def matern_over_ln2(t):
    m = jnp.maximum(t, 1e-12)
    s = m * lax.rsqrt(m)
    return (s + 1.0 / LN2) * jnp.exp2(-s)


def product(src_feat, tgt_feat, vals):
    t = jnp.dot(src_feat, tgt_feat, preferred_element_type=F32)
    k = matern_over_ln2(t)
    high = k.astype(BF16)
    low = (k - high.astype(F32)).astype(BF16)
    return jnp.dot(vals, high, preferred_element_type=F32) + jnp.dot(vals, low, preferred_element_type=F32)


def in_chunks(n, size, step):
    half = size // 2
    big = (n + half - 1) // size

    def full(i, carry):
        step(i * size, size)
        return carry

    def rest(i, carry):
        step(big * size, half)
        return carry

    lax.fori_loop(0, big, full, 0)
    lax.fori_loop(0, (n > big * size).astype(jnp.int32), rest, 0)


def dot3(a, b, transposed=False):
    ah = a.astype(BF16).astype(F32)
    both = jnp.concatenate([ah, a - ah], 0).astype(BF16)
    bh = b.astype(BF16)
    bl = (b - bh.astype(F32)).astype(BF16)
    dims = (((1,), (1 if transposed else 0,)), ((), ()))
    r = lax.dot_general(both, bh, dims, preferred_element_type=F32)
    r = r + lax.dot_general(both, bl, dims, preferred_element_type=F32)
    return r[0:8] + r[8:16]


def odd_group():
    return (lax.axis_index("d") >> 6) & 1


def fetch(pairs, sems, at):
    copies = [pltpu.make_async_copy(a, b, sems.at[at + i]) for i, (a, b) in enumerate(pairs)]
    for c in copies:
        c.start()
    return copies


def pack_kernel(
    pts_h, chg_h, skel_h, cpts_h, llist_h, tlist_h, up_h, utm_h,
    m0_h, m1_h, first_h, last_h,
    pts, chg, skel, cpts, llist, tlist, up, utm, m0, m1, first, last, row16, sems,
):
    ins = ((llist_h, llist), (tlist_h, tlist), (skel_h, skel), (cpts_h, cpts), (chg_h, chg), (pts_h, pts), (up_h, up), (utm_h, utm))
    copies = fetch(ins, sems, 0)
    for c in copies[0:2]:
        c.wait()
    lane = lax.broadcasted_iota(jnp.int32, (1, 128), 1)
    sub8 = lax.broadcasted_iota(jnp.int32, (8, 128), 0)
    lane8 = lax.broadcasted_iota(jnp.int32, (8, 128), 1)
    row = lax.broadcasted_iota(jnp.int32, (128, 128), 0)
    col = lax.broadcasted_iota(jnp.int32, (128, 128), 1)
    before = (row < col).astype(F32).astype(BF16)
    pick = (lax.broadcasted_iota(jnp.int32, (16, 128), 0) == (lax.broadcasted_iota(jnp.int32, (16, 128), 1) & 15))
    pick = pick.astype(F32).astype(BF16)
    ll = llist[...]
    mine = sub8 == (lane8 >> 4)

    def flat(v):
        w = jnp.dot(v.astype(F32).astype(BF16), pick, preferred_element_type=F32)
        return jnp.sum(jnp.where(mine, w, 0.0), axis=0, keepdims=True).astype(jnp.int32)

    upper = flat(ll >> 6) & 7
    lower = flat(ll & 63)
    row16[...] = jnp.zeros((8, 128), jnp.int32)
    row16[0:1, 0:16] = tlist[...]
    tl = row16[0:1, :]
    odd = odd_group() == 1
    leaf_u = jnp.where(odd, lower >> 3, upper)
    leaf_v = jnp.where(odd, upper, lower >> 3)
    top_u = jnp.where(odd, tl & 7, (tl >> 3) & 7)
    top_v = jnp.where(odd, (tl >> 3) & 7, tl & 7)
    leaf_hit = leaf_v == sub8
    top_hit = (top_v == sub8) & (lane < 16)
    leaf_one = leaf_hit.astype(F32)
    top_one = top_hit.astype(F32)
    leaf_pos = jnp.dot(leaf_one.astype(BF16), before, preferred_element_type=F32)
    top_pos = jnp.dot(top_one.astype(BF16), before, preferred_element_type=F32) + 16.0
    leaf_n = jnp.sum(leaf_one, axis=1, keepdims=True)
    top_n = jnp.sum(top_one, axis=1, keepdims=True)
    leaf_pos = jnp.where(leaf_hit, leaf_pos, -1.0)
    top_pos = jnp.where(top_hit, top_pos, -1.0)
    local = (lower & 7) + leaf_u * 8
    codes = jnp.where(sub8 == 0, lane >> 4, jnp.where(sub8 == 1, local, 0)).astype(F32).astype(BF16)
    tcodes = jnp.where(sub8 == 0, (tl >> 6) * 8 + top_u, 0).astype(F32).astype(BF16)
    rowf = row.astype(F32)
    for c in copies[2:6]:
        c.wait()
    for d in range(8):
        for c in range(3):
            m0[d, 8 * c : 8 * c + 8, :] = skel[c]
            m0[d, 24 + c : 25 + c, :] = cpts[c]
        m0[d, 29:32, :] = jnp.zeros((3, 128), F32)
        oh = (leaf_pos[d : d + 1] == rowf).astype(F32).astype(BF16)
        got = lax.dot_general(codes, oh, (((1,), (1,)), ((), ())), preferred_element_type=F32)
        m0[d, 27:28, :] = got[0:1] * 128.0 + got[1:2]
        oh = (top_pos[d : d + 1] == rowf).astype(F32).astype(BF16)
        got = lax.dot_general(tcodes, oh, (((1,), (1,)), ((), ())), preferred_element_type=F32)[0:1]
        got = got + jnp.where(lane == 0, leaf_n[d : d + 1], 0.0) + jnp.where(lane == 1, top_n[d : d + 1], 0.0)
        m0[d, 28:29, :] = got
    for slab, start in ((first, 0), (last, OWN - REACH)):
        for i in range(REACH):
            slab[8 * i : 8 * i + 8, :] = chg[start + i]
        for c in range(3):
            slab[32 + 4 * c : 36 + 4 * c, :] = pts[c, start : start + REACH, :]
        slab[44:48, :] = jnp.zeros((4, 256), F32)
    outs = fetch(((first, first_h), (last, last_h)), sems, 8)
    m1[96:104, :] = jnp.zeros((8, 128), F32)
    for c in range(3):
        m1[64 + 8 * c : 72 + 8 * c, :] = skel[c]
        m1[96 + c : 97 + c, :] = cpts[c]
    copies[6].wait()
    own = [dot3(chg[l], up[l], True) for l in range(OWN)]
    for l in range(OWN):
        m1[8 * l : 8 * l + 8, :] = own[l]
    copies[7].wait()
    total = dot3(own[0], utm[0], True)
    for l in range(1, OWN):
        total = total + dot3(own[l], utm[l], True)
    m1[88:96, :] = total
    for d in range(8):
        m0[d, 32:40, :] = total
    outs += fetch([(m0, m0_h)] + [(m1, m1_h.at[d]) for d in range(8)], sems, 10)
    for c in outs:
        c.wait()


def pack(*args):
    sd = jax.ShapeDtypeStruct
    shapes = [(8, 40, 128), (104, 128), (48, 256), (48, 256)]
    return pl.pallas_call(
        pack_kernel,
        in_specs=[HBM] * 8,
        out_specs=[HBM] * 4,
        out_shape=[sd((8, 40, 128), F32), sd((8, 104, 128), F32), sd((48, 256), F32), sd((48, 256), F32)],
        scratch_shapes=[pltpu.VMEM(a.shape, a.dtype) for a in args]
        + [pltpu.VMEM(s, F32) for s in shapes]
        + [pltpu.VMEM((8, 128), jnp.int32), pltpu.SemaphoreType.DMA((19,))],
        compiler_params=WIDE,
        name="pack",
    )(*args)


FIRST, MIDDLE, LAST = range(3)


def near_blocks(ids, flat, base, first_leaf, stage):
    pos = jnp.int32(0)
    seen = jnp.int32(0)
    for l in range(first_leaf, OWN):
        for n in range(NBR):
            ident = ids[l, n]
            e = ident - base
            flat[pos] = l * 32 + e
            if stage == LAST:
                take = e >= REACH + OWN
            else:
                own = (e >= REACH) & (e < REACH + OWN)
                take = own & (seen < FIRST_OWN)
                if stage == MIDDLE:
                    take = (ident >= 0) & (e < REACH + OWN) & jnp.logical_not(take)
                seen = seen + own.astype(jnp.int32)
            pos = pos + take.astype(jnp.int32)
    for u in range(CHUNK):
        flat[pos + u] = (OWN - 1) * 32 + NEAR_DUMMY
    return pos


def near_setup(sources, leaves, xyz, vals_of, fs, ft, vals, ts, tl):
    s0, s1, t0, t1, t2 = dense_features(xyz)
    load0, load1 = spread(s0, ts.at[0]), spread(s1, tl)
    for e in sources:
        a, b = load0(e), load1(e)
        fs[e] = jnp.concatenate([a, b, a, b], 0).T.astype(BF16)
        vals[e] = two_halves(vals_of(e))
    vals[NEAR_DUMMY] = jnp.zeros((16, 256), BF16)
    fs[NEAR_DUMMY] = jnp.zeros((256, FEAT), BF16)
    load0, load1, load2 = spread(t0, ts.at[1]), spread(t1, ts.at[2]), spread(t2, ts.at[3])
    for l in leaves:
        e = l + REACH
        one = load1(e)
        ft[l, 0:16, :] = jnp.concatenate([load0(e), load2(e)], 0).astype(BF16)
        ft[l, 16:32, :] = jnp.concatenate([one, one], 0).astype(BF16)


def near_run(count, flat, start, out, fs, ft, vals):
    out[...] = jnp.zeros_like(out) if start is None else start[...]

    def step(start, size):
        for u in range(size):
            code = flat[start + u]
            l, e = code >> 5, code & 31
            r = product(fs[e], ft[l], vals[e])
            out[l] += r[0:8] + r[8:16]

    in_chunks(count, CHUNK, step)


def near_base():
    return lax.axis_index("d") * OWN - REACH


def near_first_kernel(ids, pts, chg, out, flat, fs, ft, vals, xyz, ts, tl):
    count = near_blocks(ids, flat, near_base(), 0, FIRST)
    for c in range(3):
        xyz[c] = jnp.zeros((16, 256), F32)
        xyz[c, 4:12, :] = pts[c]
    own = range(REACH, REACH + OWN)
    near_setup(own, range(OWN), [xyz[0], xyz[1], xyz[2]], lambda e: chg[e - REACH], fs, ft, vals, ts, tl)
    near_run(count, flat, None, out, fs, ft, vals)


def near_middle_kernel(ids, pts, chg, before, start, out, flat, fs, ft, vals, xyz, ts, tl):
    count = near_blocks(ids, flat, near_base(), 0, MIDDLE)
    for c in range(3):
        xyz[c, 0:4, :] = before[32 + 4 * c : 36 + 4 * c, :]
        xyz[c, 4:12, :] = pts[c]
        xyz[c, 12:16, :] = jnp.zeros((4, 256), F32)

    def vals_of(e):
        return before[8 * e : 8 * e + 8, :] if e < REACH else chg[e - REACH]

    near_setup(range(REACH + OWN), range(OWN), [xyz[0], xyz[1], xyz[2]], vals_of, fs, ft, vals, ts, tl)
    near_run(count, flat, start, out, fs, ft, vals)


def near_last_kernel(ids, pts, after, out, flat, fs, ft, vals, xyz, ts, tl):
    count = near_blocks(ids, flat, near_base(), OWN - REACH, LAST)
    for c in range(3):
        xyz[c, 0:4, :] = jnp.zeros((4, 256), F32)
        xyz[c, 4:12, :] = pts[c]
        xyz[c, 12:16, :] = after[32 + 4 * c : 36 + 4 * c, :]

    def vals_of(e):
        return after[8 * (e - REACH - OWN) : 8 * (e - REACH - OWN) + 8, :]

    halo = range(REACH + OWN, 2 * REACH + OWN)
    near_setup(halo, range(OWN - REACH, OWN), [xyz[0], xyz[1], xyz[2]], vals_of, fs, ft, vals, ts, tl)
    near_run(count, flat, None, out, fs, ft, vals)


def near_part(stage, *args):
    return pl.pallas_call(
        (near_first_kernel, near_middle_kernel, near_last_kernel)[stage],
        in_specs=[SMEM] + [VMEM] * (len(args) - 1),
        out_specs=VMEM,
        out_shape=jax.ShapeDtypeStruct((OWN, 8, 256), F32),
        scratch_shapes=[
            pltpu.SMEM((OWN * NBR + CHUNK + 8,), jnp.int32),
            pltpu.VMEM((17, 256, FEAT), BF16),
            pltpu.VMEM((OWN, FEAT, 256), BF16),
            pltpu.VMEM((17, 16, 256), BF16),
            pltpu.VMEM((3, 16, 256), F32),
            pltpu.VMEM((4, 2, 128, 128), F32),
            pltpu.VMEM((2, 128, 128), F32),
        ],
        cost_estimate=pl.CostEstimate(flops=2000000000, bytes_accessed=300000, transcendentals=4194304),
        compiler_params=PARAMS,
        name="near",
    )(*args)


def prepare_sources(i, xyz, t0, t1, feat):
    s0, s1, _, _, _ = dense_features(xyz)
    s0 = spread(s0, t0)
    s1 = spread(s1, t1)
    for l in range(8):
        feat[8 * i + l, 0:8, :] = s0(l)
        feat[8 * i + l, 8:16, :] = s1(l)


def prepare_targets(i, xyz, tmp, ft):
    _, _, t0, t1, t2 = dense_features(xyz)
    load0, load1, load2 = spread(t0, tmp.at[0]), spread(t1, tmp.at[1]), spread(t2, tmp.at[2])
    for l in range(8):
        one = load1(l)
        ft[8 * i + l, 0:16, :] = jnp.concatenate([load0(l), load2(l)], 0).astype(BF16)
        ft[8 * i + l, 16:32, :] = jnp.concatenate([one, one], 0).astype(BF16)


def flatten(req, flat, row, start, slot):
    off = 0
    for d in range(8):
        n = req[d, 1, slot]

        def copy(j, carry, d=d, off=off):
            for u in range(8):
                flat[off + j * 8 + u] = req[d, row, start + j * 8 + u] + d * (1024 if row == 0 else 128)
            return carry

        lax.fori_loop(0, (n + 7) // 8, copy, 0)
        off = off + n
    for u in range(2 * PAIRS):
        flat[off + u] = DUMMY
    return off


def interact(total, flat, fs, ft, vals, add):
    zero = jnp.zeros((FEAT, 128), BF16)

    def step(start, size):
        for u in range(size // 2):
            ca = flat[start + 2 * u]
            cb = flat[start + 2 * u + 1]
            ta, sa = ca >> 7, ca & 127
            tb, sb = cb >> 7, cb & 127
            fa = ft[ta]
            fb = ft[tb]
            tgt = jnp.concatenate([jnp.concatenate([fa, zero], 1), jnp.concatenate([zero, fb], 1)], 0)
            ra, rb = fs[sa], fs[sb]
            src = jnp.concatenate([ra, ra, rb, rb], 0).T.astype(BF16)
            r = product(src, tgt, jnp.concatenate([vals[sa], vals[sb]], 0))
            add(ta, r[0:8, 0:128] + r[8:16, 0:128])
            add(tb, r[16:24, 128:256] + r[24:32, 128:256])

    in_chunks(total, 2 * PAIRS, step)


def clear_dummy(fs, vals):
    fs[DUMMY] = jnp.zeros((16, 128), F32)
    vals[DUMMY] = jnp.zeros((16, 128), BF16)


def far_prep_kernel(req, tgt, ft, ftop, leaf_flat, top_flat, counts, tmp):
    for d in range(8):
        prepare_targets(d, [tgt[40 * d + 8 * c : 40 * d + 8 * c + 8, :] for c in range(3)], tmp.at[d], ft)
    prepare_targets(0, [tgt[pl.ds(24 + c, 8, stride=40), :] for c in range(3)], tmp.at[8], ftop)
    counts[0] = flatten(req, leaf_flat, 0, 0, 0)
    counts[1] = flatten(req, top_flat, 1, 16, 1)


def far_prep(req, tgt):
    sd = jax.ShapeDtypeStruct
    return pl.pallas_call(
        far_prep_kernel,
        in_specs=[SMEM, VMEM],
        out_specs=[VMEM, VMEM, SMEM, SMEM, SMEM],
        out_shape=[
            sd((64, FEAT, 128), BF16),
            sd((8, FEAT, 128), BF16),
            sd((1024 + 64,), jnp.int32),
            sd((256,), jnp.int32),
            sd((2,), jnp.int32),
        ],
        scratch_shapes=[pltpu.VMEM((9, 3, 1, 64, 128), F32)],
        cost_estimate=pl.CostEstimate(flops=100000000, bytes_accessed=900000, transcendentals=0),
        compiler_params=PARAMS,
        name="far_prep",
    )(req, tgt.reshape(320, 128))


def far_leaf_kernel(counts, flat, src, ft, out, fs, vals, t0, t1):
    for y in range(8):
        prepare_sources(y, [src[y, 64 + 8 * c : 72 + 8 * c, :] for c in range(3)], t0.at[y], t1.at[y], fs)
        for l in range(OWN):
            vals[8 * y + l] = two_halves(src[y, 8 * l : 8 * l + 8, :])
    clear_dummy(fs, vals)
    out[...] = jnp.zeros_like(out)

    def add(t, v):
        out[t >> 3, t & 7] += v

    interact(counts[0], flat, fs, ft, vals, add)


FAR_SCRATCH = [
    pltpu.VMEM((65, 16, 128), F32),
    pltpu.VMEM((65, 16, 128), BF16),
    pltpu.VMEM((8, 1, 64, 128), F32),
    pltpu.VMEM((8, 1, 64, 128), F32),
]


def far_leaf(counts, flat, src, ft):
    return pl.pallas_call(
        far_leaf_kernel,
        in_specs=[SMEM, SMEM, VMEM, VMEM],
        out_specs=VMEM,
        out_shape=jax.ShapeDtypeStruct((8, 9, 8, 128), F32),
        scratch_shapes=FAR_SCRATCH,
        cost_estimate=pl.CostEstimate(flops=2097152000, bytes_accessed=900000, transcendentals=4194304),
        compiler_params=PARAMS,
        name="far_leaf",
    )(counts, flat, src, ft)


def cells_kernel(along_u, along_v, out, slab):
    for y in range(8):
        slab[0, 8 * y : 8 * y + 8, :] = along_u[y, 88:96, :]
        slab[1, 8 * y : 8 * y + 8, :] = along_v[y, 32:40, :]
        for c in range(3):
            slab[0, 64 + 8 * c + y : 65 + 8 * c + y, :] = along_u[y, 96 + c : 97 + c, :]
            slab[1, 64 + 8 * c + y : 65 + 8 * c + y, :] = along_v[y, 24 + c : 25 + c, :]
    odd = odd_group()
    for d in range(8):
        out[d] = slab[(d % 2) ^ odd]


def cells_message(along_u, along_v):
    return pl.pallas_call(
        cells_kernel,
        in_specs=[VMEM] * 2,
        out_specs=VMEM,
        out_shape=jax.ShapeDtypeStruct((8, 88, 128), F32),
        scratch_shapes=[pltpu.VMEM((2, 88, 128), F32)],
        compiler_params=PARAMS,
        name="cells",
    )(along_u, along_v)


def far_top_kernel(counts, flat, src, ft, part, out, fs, vals, t0, t1):
    for g in range(8):
        xyz = [src[g, 64 + 8 * c : 72 + 8 * c, :] for c in range(3)]
        prepare_sources(g, xyz, t0.at[g], t1.at[g], fs)
        for y in range(8):
            vals[8 * g + y] = two_halves(src[g, 8 * y : 8 * y + 8, :])
    clear_dummy(fs, vals)
    out[...] = part[...]

    def add(t, v):
        out[t, 8] += v

    interact(counts[1], flat, fs, ft, vals, add)


def far_top(counts, flat, src, ft, part):
    return pl.pallas_call(
        far_top_kernel,
        in_specs=[SMEM, SMEM, VMEM, VMEM, VMEM],
        out_specs=VMEM,
        out_shape=jax.ShapeDtypeStruct((8, 9, 8, 128), F32),
        scratch_shapes=FAR_SCRATCH,
        compiler_params=PARAMS,
        name="far_top",
    )(counts, flat, src, ft, part)


def final_kernel(got, utm, up, near1, near2, out):
    tot = got[0]
    for d in range(1, 8):
        tot = tot + got[d]
    cell = tot[8]
    for l in range(OWN):
        incoming = tot[l] + dot3(cell, utm[l])
        out[l] = near1[l] + near2[l] + dot3(incoming, up[l])


def final(got, utm, up, near1, near2):
    return pl.pallas_call(
        final_kernel,
        in_specs=[VMEM] * 5,
        out_specs=VMEM,
        out_shape=jax.ShapeDtypeStruct((8, 8, 256), F32),
        compiler_params=PARAMS,
        name="final",
    )(got, utm, up, near1, near2)


def device(g, u, v):
    return g * 64 + (v * 8 + u if g % 2 else u * 8 + v)


def body(points, charges, up_op, skel_pts, utm, cell_pts, near_list, leaf_list, top_list):
    r = range(8)
    along_u = [[device(g, u, v) for u in r] for g in r for v in r]
    along_v = [[device(g, u, v) for v in r] for g in r for u in r]
    along_g = [[g * 64 + i for g in r] for i in range(64)]

    def exchange(x, groups):
        return lax.all_to_all(x, "d", 0, 0, axis_index_groups=groups, tiled=True)

    pts = jnp.transpose(points, (1, 0, 2))
    skel = jnp.transpose(skel_pts, (1, 0, 2))
    cpts = jnp.transpose(cell_pts, (1, 0, 2))
    count = lax.axis_size("d")
    up = [(i, i + 1) for i in range(count - 1)]
    down = [(i + 1, i) for i in range(count - 1)]
    m0, m1, first, last = pack(pts, charges, skel, cpts, leaf_list, top_list, up_op, utm)
    m1, charges1 = lax.optimization_barrier((m1, charges))
    got1 = exchange(m1, along_u)
    before = lax.ppermute(last, "d", up)
    near0 = near_part(FIRST, near_list, pts, charges1)
    got1, before, near0, m0, first = lax.optimization_barrier((got1, before, near0, m0, first))
    got0 = exchange(m0, along_v)
    after = lax.ppermute(first, "d", down)
    near1 = near_part(MIDDLE, near_list, pts, charges, before, near0)
    got0, after, near1 = lax.optimization_barrier((got0, after, near1))
    cells, got0 = lax.optimization_barrier((cells_message(got1, got0), got0))
    gotg = exchange(cells, along_g)
    req = got0[:, 27:29, :].astype(jnp.int32)
    ft, ftop, leaf_flat, top_flat, counts = far_prep(req, got0)
    part = far_leaf(counts, leaf_flat, got1, ft)
    part = far_top(counts, top_flat, gotg, ftop, part)
    part, after = lax.optimization_barrier((part, after))
    gotr = exchange(part, along_v)
    near2 = near_part(LAST, near_list, pts, after)
    return final(gotr, utm, up_op, near1, near2)


def solution(mesh):
    line = Mesh(mesh.devices.reshape(-1), ("d",))
    specs = tuple(P("d", *([None] * k)) for k in (2, 2, 2, 2, 2, 2, 1, 1, 1))
    return jax.shard_map(body, mesh=line, in_specs=specs, out_specs=P("d", None, None), check_vma=False)
```

```python
import functools
import math

import jax
import jax.numpy as jnp
from jax import lax
from jax.experimental import pallas as pl
from jax.experimental.pallas import tpu as pltpu
from jax.sharding import Mesh, PartitionSpec as P

F32 = jnp.float32
BF16 = jnp.bfloat16
KAPPA = math.sqrt(3.0) * math.log2(math.e)
LN2 = math.log(2.0)
CENTER = 1.5
FEAT = 32
REACH = 4
OWN = 8
NBR = 9
PAIRS = 16
DUMMY = 64
CHUNK = 16
NEAR_DUMMY = 16
FIRST_OWN = 24

SMEM = pl.BlockSpec(memory_space=pltpu.SMEM)
HBM = pl.BlockSpec(memory_space=pltpu.HBM)
VMEM = pl.BlockSpec(memory_space=pltpu.VMEM)
PARAMS = pltpu.CompilerParams(vmem_limit_bytes=40 << 20)
WIDE = pltpu.CompilerParams(vmem_limit_bytes=60 << 20)


def split2(x):
    a = x.astype(BF16).astype(F32)
    return a, (x - a).astype(BF16).astype(F32)


def split3(x):
    a = x.astype(BF16).astype(F32)
    b, c = split2(x - a)
    return a, b, c


def dense_features(xyz):
    parts = [split2((x - CENTER) * KAPPA) for x in xyz]
    n = None
    for a, b in parts:
        r = a + b
        n = r * r if n is None else n + r * r
    n1, n2, n3 = split3(n)
    one = jnp.ones_like(n)
    zero = jnp.zeros_like(n)
    high = [a for a, _ in parts]
    low = [b for _, b in parts]
    high2 = [-2.0 * a for a in high]
    low2 = [-2.0 * b for b in low]
    s0 = high + [n1, n2, n3, one, one]
    s1 = low + [one, zero, zero, zero, zero]
    t0 = high2 + [one, one, one, n1, n2]
    t1 = low2 + [zero] * 5
    t2 = high2 + [n3] + [zero] * 4
    return s0, s1, t0, t1, t2


def spread(rows, tmp):
    n, width = rows[0].shape
    halves = width // 128
    for r, v in enumerate(rows):
        for h in range(halves):
            tmp[h, n * r : n * r + n, :] = v[:, 128 * h : 128 * h + 128]

    def load(leaf):
        return jnp.concatenate([tmp[h, pl.ds(leaf, 8, stride=n), :] for h in range(halves)], 1)

    return load


def two_halves(vals):
    v = vals * LN2
    high = v.astype(BF16).astype(F32)
    return jnp.concatenate([high, v - high], 0).astype(BF16)


def matern_over_ln2(t):
    m = jnp.maximum(t, 1e-12)
    s = m * lax.rsqrt(m)
    return (s + 1.0 / LN2) * jnp.exp2(-s)


def product(src_feat, tgt_feat, vals):
    t = jnp.dot(src_feat, tgt_feat, preferred_element_type=F32)
    k = matern_over_ln2(t)
    high = k.astype(BF16)
    low = (k - high.astype(F32)).astype(BF16)
    return jnp.dot(vals, high, preferred_element_type=F32) + jnp.dot(vals, low, preferred_element_type=F32)


def in_chunks(n, size, step):
    half = size // 2
    big = (n + half - 1) // size

    def full(i, carry):
        step(i * size, size)
        return carry

    def rest(i, carry):
        step(big * size, half)
        return carry

    lax.fori_loop(0, big, full, 0)
    lax.fori_loop(0, (n > big * size).astype(jnp.int32), rest, 0)


def dot3(a, b, transposed=False):
    ah = a.astype(BF16).astype(F32)
    both = jnp.concatenate([ah, a - ah], 0).astype(BF16)
    bh = b.astype(BF16)
    bl = (b - bh.astype(F32)).astype(BF16)
    dims = (((1,), (1 if transposed else 0,)), ((), ()))
    r = lax.dot_general(both, bh, dims, preferred_element_type=F32)
    r = r + lax.dot_general(both, bl, dims, preferred_element_type=F32)
    return r[0:8] + r[8:16]


def odd_group():
    return (lax.axis_index("d") >> 6) & 1


def fetch(pairs, sems, at):
    copies = [pltpu.make_async_copy(a, b, sems.at[at + i]) for i, (a, b) in enumerate(pairs)]
    for c in copies:
        c.start()
    return copies


def pack_kernel(
    pts_h, chg_h, skel_h, cpts_h, llist_h, tlist_h, up_h, utm_h,
    m0_h, m1_h, first_h, last_h,
    pts, chg, skel, cpts, llist, tlist, up, utm, m0, m1, first, last, row16, sems,
):
    ins = ((llist_h, llist), (tlist_h, tlist), (skel_h, skel), (cpts_h, cpts), (chg_h, chg), (pts_h, pts), (up_h, up), (utm_h, utm))
    copies = fetch(ins, sems, 0)
    for c in copies[0:2]:
        c.wait()
    lane = lax.broadcasted_iota(jnp.int32, (1, 128), 1)
    sub8 = lax.broadcasted_iota(jnp.int32, (8, 128), 0)
    lane8 = lax.broadcasted_iota(jnp.int32, (8, 128), 1)
    row = lax.broadcasted_iota(jnp.int32, (128, 128), 0)
    col = lax.broadcasted_iota(jnp.int32, (128, 128), 1)
    before = (row < col).astype(F32).astype(BF16)
    pick = (lax.broadcasted_iota(jnp.int32, (16, 128), 0) == (lax.broadcasted_iota(jnp.int32, (16, 128), 1) & 15))
    pick = pick.astype(F32).astype(BF16)
    ll = llist[...]
    mine = sub8 == (lane8 >> 4)

    def flat(v):
        w = jnp.dot(v.astype(F32).astype(BF16), pick, preferred_element_type=F32)
        return jnp.sum(jnp.where(mine, w, 0.0), axis=0, keepdims=True).astype(jnp.int32)

    upper = flat(ll >> 6) & 7
    lower = flat(ll & 63)
    row16[...] = jnp.zeros((8, 128), jnp.int32)
    row16[0:1, 0:16] = tlist[...]
    tl = row16[0:1, :]
    odd = odd_group() == 1
    leaf_u = jnp.where(odd, lower >> 3, upper)
    leaf_v = jnp.where(odd, upper, lower >> 3)
    top_u = jnp.where(odd, tl & 7, (tl >> 3) & 7)
    top_v = jnp.where(odd, (tl >> 3) & 7, tl & 7)
    leaf_hit = leaf_v == sub8
    top_hit = (top_v == sub8) & (lane < 16)
    leaf_one = leaf_hit.astype(F32)
    top_one = top_hit.astype(F32)
    leaf_pos = jnp.dot(leaf_one.astype(BF16), before, preferred_element_type=F32)
    top_pos = jnp.dot(top_one.astype(BF16), before, preferred_element_type=F32) + 16.0
    leaf_n = jnp.sum(leaf_one, axis=1, keepdims=True)
    top_n = jnp.sum(top_one, axis=1, keepdims=True)
    leaf_pos = jnp.where(leaf_hit, leaf_pos, -1.0)
    top_pos = jnp.where(top_hit, top_pos, -1.0)
    local = (lower & 7) + leaf_u * 8
    codes = jnp.where(sub8 == 0, lane >> 4, jnp.where(sub8 == 1, local, 0)).astype(F32).astype(BF16)
    tcodes = jnp.where(sub8 == 0, (tl >> 6) * 8 + top_u, 0).astype(F32).astype(BF16)
    rowf = row.astype(F32)
    for c in copies[2:6]:
        c.wait()
    for d in range(8):
        for c in range(3):
            m0[d, 8 * c : 8 * c + 8, :] = skel[c]
            m0[d, 24 + c : 25 + c, :] = cpts[c]
        m0[d, 29:32, :] = jnp.zeros((3, 128), F32)
        oh = (leaf_pos[d : d + 1] == rowf).astype(F32).astype(BF16)
        got = lax.dot_general(codes, oh, (((1,), (1,)), ((), ())), preferred_element_type=F32)
        m0[d, 27:28, :] = got[0:1] * 128.0 + got[1:2]
        oh = (top_pos[d : d + 1] == rowf).astype(F32).astype(BF16)
        got = lax.dot_general(tcodes, oh, (((1,), (1,)), ((), ())), preferred_element_type=F32)[0:1]
        got = got + jnp.where(lane == 0, leaf_n[d : d + 1], 0.0) + jnp.where(lane == 1, top_n[d : d + 1], 0.0)
        m0[d, 28:29, :] = got
    for slab, start in ((first, 0), (last, OWN - REACH)):
        for i in range(REACH):
            slab[8 * i : 8 * i + 8, :] = chg[start + i]
        for c in range(3):
            slab[32 + 4 * c : 36 + 4 * c, :] = pts[c, start : start + REACH, :]
        slab[44:48, :] = jnp.zeros((4, 256), F32)
    outs = fetch(((first, first_h), (last, last_h)), sems, 8)
    m1[96:104, :] = jnp.zeros((8, 128), F32)
    for c in range(3):
        m1[64 + 8 * c : 72 + 8 * c, :] = skel[c]
        m1[96 + c : 97 + c, :] = cpts[c]
    copies[6].wait()
    own = [dot3(chg[l], up[l], True) for l in range(OWN)]
    for l in range(OWN):
        m1[8 * l : 8 * l + 8, :] = own[l]
    copies[7].wait()
    total = dot3(own[0], utm[0], True)
    for l in range(1, OWN):
        total = total + dot3(own[l], utm[l], True)
    m1[88:96, :] = total
    for d in range(8):
        m0[d, 32:40, :] = total
    outs += fetch([(m0, m0_h)] + [(m1, m1_h.at[d]) for d in range(8)], sems, 10)
    for c in outs:
        c.wait()


def pack(*args):
    sd = jax.ShapeDtypeStruct
    shapes = [(8, 40, 128), (104, 128), (48, 256), (48, 256)]
    return pl.pallas_call(
        pack_kernel,
        in_specs=[HBM] * 8,
        out_specs=[HBM] * 4,
        out_shape=[sd((8, 40, 128), F32), sd((8, 104, 128), F32), sd((48, 256), F32), sd((48, 256), F32)],
        scratch_shapes=[pltpu.VMEM(a.shape, a.dtype) for a in args]
        + [pltpu.VMEM(s, F32) for s in shapes]
        + [pltpu.VMEM((8, 128), jnp.int32), pltpu.SemaphoreType.DMA((19,))],
        compiler_params=WIDE,
        name="pack",
    )(*args)


def near_blocks(ids, flat, base, first):
    pos = jnp.int32(0)
    seen = jnp.int32(0)
    for l in range(OWN):
        for n in range(NBR):
            ident = ids[l, n]
            e = ident - base
            flat[pos] = l * 32 + e
            own = (e >= REACH) & (e < REACH + OWN)
            take = own & (seen < FIRST_OWN)
            if not first:
                take = (ident >= 0) & jnp.logical_not(take)
            seen = seen + own.astype(jnp.int32)
            pos = pos + take.astype(jnp.int32)
    for u in range(CHUNK):
        flat[pos + u] = (OWN - 1) * 32 + NEAR_DUMMY
    return pos


def near_setup(sources, leaves, xyz, vals_of, fs, ft, vals, ts, tl):
    s0, s1, t0, t1, t2 = dense_features(xyz)
    load0, load1 = spread(s0, ts.at[0]), spread(s1, tl)
    for e in sources:
        a, b = load0(e), load1(e)
        fs[e] = jnp.concatenate([a, b, a, b], 0).T.astype(BF16)
        vals[e] = two_halves(vals_of(e))
    vals[NEAR_DUMMY] = jnp.zeros((16, 256), BF16)
    fs[NEAR_DUMMY] = jnp.zeros((256, FEAT), BF16)
    load0, load1, load2 = spread(t0, ts.at[1]), spread(t1, ts.at[2]), spread(t2, ts.at[3])
    for l in leaves:
        e = l + REACH
        one = load1(e)
        ft[l, 0:16, :] = jnp.concatenate([load0(e), load2(e)], 0).astype(BF16)
        ft[l, 16:32, :] = jnp.concatenate([one, one], 0).astype(BF16)


def near_run(count, flat, start, out, fs, ft, vals):
    out[...] = jnp.zeros_like(out) if start is None else start[...]

    def step(start, size):
        for u in range(size):
            code = flat[start + u]
            l, e = code >> 5, code & 31
            r = product(fs[e], ft[l], vals[e])
            out[l] += r[0:8] + r[8:16]

    in_chunks(count, CHUNK, step)


def near_base():
    return lax.axis_index("d") * OWN - REACH


def near_first_kernel(ids, pts, chg, out, flat, fs, ft, vals, xyz, ts, tl):
    count = near_blocks(ids, flat, near_base(), True)
    for c in range(3):
        xyz[c] = jnp.zeros((16, 256), F32)
        xyz[c, 4:12, :] = pts[c]
    own = range(REACH, REACH + OWN)
    near_setup(own, range(OWN), [xyz[0], xyz[1], xyz[2]], lambda e: chg[e - REACH], fs, ft, vals, ts, tl)
    near_run(count, flat, None, out, fs, ft, vals)


def near_rest_kernel(ids, pts, chg, before, after, start, out, flat, fs, ft, vals, xyz, ts, tl):
    count = near_blocks(ids, flat, near_base(), False)
    for c in range(3):
        xyz[c, 0:4, :] = before[32 + 4 * c : 36 + 4 * c, :]
        xyz[c, 4:12, :] = pts[c]
        xyz[c, 12:16, :] = after[32 + 4 * c : 36 + 4 * c, :]

    def vals_of(e):
        if e < REACH:
            return before[8 * e : 8 * e + 8, :]
        if e < REACH + OWN:
            return chg[e - REACH]
        return after[8 * (e - REACH - OWN) : 8 * (e - REACH - OWN) + 8, :]

    near_setup(range(OWN + 2 * REACH), range(OWN), [xyz[0], xyz[1], xyz[2]], vals_of, fs, ft, vals, ts, tl)
    near_run(count, flat, start, out, fs, ft, vals)


def near_part(kernel, *args):
    return pl.pallas_call(
        kernel,
        in_specs=[SMEM] + [VMEM] * (len(args) - 1),
        out_specs=VMEM,
        out_shape=jax.ShapeDtypeStruct((OWN, 8, 256), F32),
        scratch_shapes=[
            pltpu.SMEM((OWN * NBR + CHUNK + 8,), jnp.int32),
            pltpu.VMEM((17, 256, FEAT), BF16),
            pltpu.VMEM((OWN, FEAT, 256), BF16),
            pltpu.VMEM((17, 16, 256), BF16),
            pltpu.VMEM((3, 16, 256), F32),
            pltpu.VMEM((4, 2, 128, 128), F32),
            pltpu.VMEM((2, 128, 128), F32),
        ],
        cost_estimate=pl.CostEstimate(flops=2000000000, bytes_accessed=300000, transcendentals=4194304),
        compiler_params=PARAMS,
        name="near",
    )(*args)


def prepare_sources(i, xyz, t0, t1, feat):
    s0, s1, _, _, _ = dense_features(xyz)
    s0 = spread(s0, t0)
    s1 = spread(s1, t1)
    for l in range(8):
        feat[8 * i + l, 0:8, :] = s0(l)
        feat[8 * i + l, 8:16, :] = s1(l)


def prepare_targets(i, xyz, tmp, ft):
    _, _, t0, t1, t2 = dense_features(xyz)
    load0, load1, load2 = spread(t0, tmp.at[0]), spread(t1, tmp.at[1]), spread(t2, tmp.at[2])
    for l in range(8):
        one = load1(l)
        ft[8 * i + l, 0:16, :] = jnp.concatenate([load0(l), load2(l)], 0).astype(BF16)
        ft[8 * i + l, 16:32, :] = jnp.concatenate([one, one], 0).astype(BF16)


def flatten(req, flat, row, start, slot):
    off = 0
    for d in range(8):
        n = req[d, 1, slot]

        def copy(j, carry, d=d, off=off):
            for u in range(8):
                flat[off + j * 8 + u] = req[d, row, start + j * 8 + u] + d * (1024 if row == 0 else 128)
            return carry

        lax.fori_loop(0, (n + 7) // 8, copy, 0)
        off = off + n
    for u in range(2 * PAIRS):
        flat[off + u] = DUMMY
    return off


def interact(total, flat, fs, ft, vals, add):
    zero = jnp.zeros((FEAT, 128), BF16)

    def step(start, size):
        for u in range(size // 2):
            ca = flat[start + 2 * u]
            cb = flat[start + 2 * u + 1]
            ta, sa = ca >> 7, ca & 127
            tb, sb = cb >> 7, cb & 127
            fa = ft[ta]
            fb = ft[tb]
            tgt = jnp.concatenate([jnp.concatenate([fa, zero], 1), jnp.concatenate([zero, fb], 1)], 0)
            ra, rb = fs[sa], fs[sb]
            src = jnp.concatenate([ra, ra, rb, rb], 0).T.astype(BF16)
            r = product(src, tgt, jnp.concatenate([vals[sa], vals[sb]], 0))
            add(ta, r[0:8, 0:128] + r[8:16, 0:128])
            add(tb, r[16:24, 128:256] + r[24:32, 128:256])

    in_chunks(total, 2 * PAIRS, step)


def clear_dummy(fs, vals):
    fs[DUMMY] = jnp.zeros((16, 128), F32)
    vals[DUMMY] = jnp.zeros((16, 128), BF16)


def far_prep_kernel(req, tgt, ft, ftop, leaf_flat, top_flat, counts, tmp):
    for d in range(8):
        prepare_targets(d, [tgt[40 * d + 8 * c : 40 * d + 8 * c + 8, :] for c in range(3)], tmp.at[d], ft)
    prepare_targets(0, [tgt[pl.ds(24 + c, 8, stride=40), :] for c in range(3)], tmp.at[8], ftop)
    counts[0] = flatten(req, leaf_flat, 0, 0, 0)
    counts[1] = flatten(req, top_flat, 1, 16, 1)


def far_prep(req, tgt):
    sd = jax.ShapeDtypeStruct
    return pl.pallas_call(
        far_prep_kernel,
        in_specs=[SMEM, VMEM],
        out_specs=[VMEM, VMEM, SMEM, SMEM, SMEM],
        out_shape=[
            sd((64, FEAT, 128), BF16),
            sd((8, FEAT, 128), BF16),
            sd((1024 + 64,), jnp.int32),
            sd((256,), jnp.int32),
            sd((2,), jnp.int32),
        ],
        scratch_shapes=[pltpu.VMEM((9, 3, 1, 64, 128), F32)],
        cost_estimate=pl.CostEstimate(flops=100000000, bytes_accessed=900000, transcendentals=0),
        compiler_params=PARAMS,
        name="far_prep",
    )(req, tgt.reshape(320, 128))


def far_leaf_kernel(counts, flat, src, ft, out, fs, vals, t0, t1):
    for y in range(8):
        prepare_sources(y, [src[y, 64 + 8 * c : 72 + 8 * c, :] for c in range(3)], t0.at[y], t1.at[y], fs)
        for l in range(OWN):
            vals[8 * y + l] = two_halves(src[y, 8 * l : 8 * l + 8, :])
    clear_dummy(fs, vals)
    out[...] = jnp.zeros_like(out)

    def add(t, v):
        out[t >> 3, t & 7] += v

    interact(counts[0], flat, fs, ft, vals, add)


FAR_SCRATCH = [
    pltpu.VMEM((65, 16, 128), F32),
    pltpu.VMEM((65, 16, 128), BF16),
    pltpu.VMEM((8, 1, 64, 128), F32),
    pltpu.VMEM((8, 1, 64, 128), F32),
]


def far_leaf(counts, flat, src, ft):
    return pl.pallas_call(
        far_leaf_kernel,
        in_specs=[SMEM, SMEM, VMEM, VMEM],
        out_specs=VMEM,
        out_shape=jax.ShapeDtypeStruct((8, 9, 8, 128), F32),
        scratch_shapes=FAR_SCRATCH,
        cost_estimate=pl.CostEstimate(flops=2097152000, bytes_accessed=900000, transcendentals=4194304),
        compiler_params=PARAMS,
        name="far_leaf",
    )(counts, flat, src, ft)


def cells_kernel(along_u, along_v, out, slab):
    for y in range(8):
        slab[0, 8 * y : 8 * y + 8, :] = along_u[y, 88:96, :]
        slab[1, 8 * y : 8 * y + 8, :] = along_v[y, 32:40, :]
        for c in range(3):
            slab[0, 64 + 8 * c + y : 65 + 8 * c + y, :] = along_u[y, 96 + c : 97 + c, :]
            slab[1, 64 + 8 * c + y : 65 + 8 * c + y, :] = along_v[y, 24 + c : 25 + c, :]
    odd = odd_group()
    for d in range(8):
        out[d] = slab[(d % 2) ^ odd]


def cells_message(along_u, along_v):
    return pl.pallas_call(
        cells_kernel,
        in_specs=[VMEM] * 2,
        out_specs=VMEM,
        out_shape=jax.ShapeDtypeStruct((8, 88, 128), F32),
        scratch_shapes=[pltpu.VMEM((2, 88, 128), F32)],
        compiler_params=PARAMS,
        name="cells",
    )(along_u, along_v)


def far_top_kernel(counts, flat, src, ft, part, out, fs, vals, t0, t1):
    for g in range(8):
        xyz = [src[g, 64 + 8 * c : 72 + 8 * c, :] for c in range(3)]
        prepare_sources(g, xyz, t0.at[g], t1.at[g], fs)
        for y in range(8):
            vals[8 * g + y] = two_halves(src[g, 8 * y : 8 * y + 8, :])
    clear_dummy(fs, vals)
    out[...] = part[...]

    def add(t, v):
        out[t, 8] += v

    interact(counts[1], flat, fs, ft, vals, add)


def far_top(counts, flat, src, ft, part):
    return pl.pallas_call(
        far_top_kernel,
        in_specs=[SMEM, SMEM, VMEM, VMEM, VMEM],
        out_specs=VMEM,
        out_shape=jax.ShapeDtypeStruct((8, 9, 8, 128), F32),
        scratch_shapes=FAR_SCRATCH,
        compiler_params=PARAMS,
        name="far_top",
    )(counts, flat, src, ft, part)


def final_kernel(got, utm, up, near, out):
    tot = got[0]
    for d in range(1, 8):
        tot = tot + got[d]
    cell = tot[8]
    for l in range(OWN):
        incoming = tot[l] + dot3(cell, utm[l])
        out[l] = near[l] + dot3(incoming, up[l])


def final(got, utm, up, near):
    return pl.pallas_call(
        final_kernel,
        in_specs=[VMEM] * 4,
        out_specs=VMEM,
        out_shape=jax.ShapeDtypeStruct((8, 8, 256), F32),
        compiler_params=PARAMS,
        name="final",
    )(got, utm, up, near)


def device(g, u, v):
    return g * 64 + (v * 8 + u if g % 2 else u * 8 + v)


def body(points, charges, up_op, skel_pts, utm, cell_pts, near_list, leaf_list, top_list):
    r = range(8)
    along_u = [[device(g, u, v) for u in r] for g in r for v in r]
    along_v = [[device(g, u, v) for v in r] for g in r for u in r]
    along_g = [[g * 64 + i for g in r] for i in range(64)]

    def exchange(x, groups):
        return lax.all_to_all(x, "d", 0, 0, axis_index_groups=groups, tiled=True)

    pts = jnp.transpose(points, (1, 0, 2))
    skel = jnp.transpose(skel_pts, (1, 0, 2))
    cpts = jnp.transpose(cell_pts, (1, 0, 2))
    count = lax.axis_size("d")
    up = [(i, i + 1) for i in range(count - 1)]
    down = [(i + 1, i) for i in range(count - 1)]
    m0, m1, first, last = pack(pts, charges, skel, cpts, leaf_list, top_list, up_op, utm)
    m1, charges1 = lax.optimization_barrier((m1, charges))
    got1 = exchange(m1, along_u)
    before = lax.ppermute(last, "d", up)
    near0 = near_part(near_first_kernel, near_list, pts, charges1)
    got1, before, near0, m0, first = lax.optimization_barrier((got1, before, near0, m0, first))
    got0 = exchange(m0, along_v)
    after = lax.ppermute(first, "d", down)
    got0, after = lax.optimization_barrier((got0, after))
    cells, got0 = lax.optimization_barrier((cells_message(got1, got0), got0))
    gotg = exchange(cells, along_g)
    req = got0[:, 27:29, :].astype(jnp.int32)
    ft, ftop, leaf_flat, top_flat, counts = far_prep(req, got0)
    part = far_leaf(counts, leaf_flat, got1, ft)
    part = far_top(counts, top_flat, gotg, ftop, part)
    part, after = lax.optimization_barrier((part, after))
    gotr = exchange(part, along_v)
    near = near_part(near_rest_kernel, near_list, pts, charges, before, after, near0)
    return final(gotr, utm, up_op, near)


def solution(mesh):
    line = Mesh(mesh.devices.reshape(-1), ("d",))
    specs = tuple(P("d", *([None] * k)) for k in (2, 2, 2, 2, 2, 2, 1, 1, 1))
    return jax.shard_map(body, mesh=line, in_specs=specs, out_specs=P("d", None, None), check_vma=False)
```

```python
import functools
import math

import jax
import jax.numpy as jnp
from jax import lax
from jax.experimental import pallas as pl
from jax.experimental.pallas import tpu as pltpu
from jax.sharding import Mesh, PartitionSpec as P

F32 = jnp.float32
BF16 = jnp.bfloat16
KAPPA = math.sqrt(3.0) * math.log2(math.e)
LN2 = math.log(2.0)
CENTER = 1.5
FEAT = 32
REACH = 4
OWN = 8
NBR = 9
PAIRS = 16
DUMMY = 64
CHUNK = 16
NEAR_DUMMY = 16
FIRST_OWN = 16

SMEM = pl.BlockSpec(memory_space=pltpu.SMEM)
HBM = pl.BlockSpec(memory_space=pltpu.HBM)
VMEM = pl.BlockSpec(memory_space=pltpu.VMEM)
PARAMS = pltpu.CompilerParams(vmem_limit_bytes=40 << 20)
WIDE = pltpu.CompilerParams(vmem_limit_bytes=60 << 20)


def split2(x):
    a = x.astype(BF16).astype(F32)
    return a, (x - a).astype(BF16).astype(F32)


def split3(x):
    a = x.astype(BF16).astype(F32)
    b, c = split2(x - a)
    return a, b, c


def dense_features(xyz):
    parts = [split2((x - CENTER) * KAPPA) for x in xyz]
    n = None
    for a, b in parts:
        r = a + b
        n = r * r if n is None else n + r * r
    n1, n2, n3 = split3(n)
    one = jnp.ones_like(n)
    zero = jnp.zeros_like(n)
    high = [a for a, _ in parts]
    low = [b for _, b in parts]
    high2 = [-2.0 * a for a in high]
    low2 = [-2.0 * b for b in low]
    s0 = high + [n1, n2, n3, one, one]
    s1 = low + [one, zero, zero, zero, zero]
    t0 = high2 + [one, one, one, n1, n2]
    t1 = low2 + [zero] * 5
    t2 = high2 + [n3] + [zero] * 4
    return s0, s1, t0, t1, t2


def spread(rows, tmp):
    n, width = rows[0].shape
    halves = width // 128
    for r, v in enumerate(rows):
        for h in range(halves):
            tmp[h, n * r : n * r + n, :] = v[:, 128 * h : 128 * h + 128]

    def load(leaf):
        return jnp.concatenate([tmp[h, pl.ds(leaf, 8, stride=n), :] for h in range(halves)], 1)

    return load


def two_halves(vals):
    v = vals * LN2
    high = v.astype(BF16).astype(F32)
    return jnp.concatenate([high, v - high], 0).astype(BF16)


def matern_over_ln2(t):
    m = jnp.maximum(t, 1e-12)
    s = m * lax.rsqrt(m)
    return (s + 1.0 / LN2) * jnp.exp2(-s)


def product(src_feat, tgt_feat, vals):
    t = jnp.dot(src_feat, tgt_feat, preferred_element_type=F32)
    k = matern_over_ln2(t)
    high = k.astype(BF16)
    low = (k - high.astype(F32)).astype(BF16)
    return jnp.dot(vals, high, preferred_element_type=F32) + jnp.dot(vals, low, preferred_element_type=F32)


def in_chunks(n, size, step):
    half = size // 2
    big = (n + half - 1) // size

    def full(i, carry):
        step(i * size, size)
        return carry

    def rest(i, carry):
        step(big * size, half)
        return carry

    lax.fori_loop(0, big, full, 0)
    lax.fori_loop(0, (n > big * size).astype(jnp.int32), rest, 0)


def dot3(a, b, transposed=False):
    ah = a.astype(BF16).astype(F32)
    both = jnp.concatenate([ah, a - ah], 0).astype(BF16)
    bh = b.astype(BF16)
    bl = (b - bh.astype(F32)).astype(BF16)
    dims = (((1,), (1 if transposed else 0,)), ((), ()))
    r = lax.dot_general(both, bh, dims, preferred_element_type=F32)
    r = r + lax.dot_general(both, bl, dims, preferred_element_type=F32)
    return r[0:8] + r[8:16]


def odd_group():
    return (lax.axis_index("d") >> 6) & 1


def fetch(pairs, sems, at):
    copies = [pltpu.make_async_copy(a, b, sems.at[at + i]) for i, (a, b) in enumerate(pairs)]
    for c in copies:
        c.start()
    return copies


def pack_kernel(
    pts_h, chg_h, skel_h, cpts_h, llist_h, tlist_h, up_h, utm_h,
    m0_h, m1_h, first_h, last_h,
    pts, chg, skel, cpts, llist, tlist, up, utm, m0, m1, first, last, row16, sems,
):
    ins = ((llist_h, llist), (tlist_h, tlist), (skel_h, skel), (cpts_h, cpts), (chg_h, chg), (pts_h, pts), (up_h, up), (utm_h, utm))
    copies = fetch(ins, sems, 0)
    for c in copies[0:2]:
        c.wait()
    lane = lax.broadcasted_iota(jnp.int32, (1, 128), 1)
    sub8 = lax.broadcasted_iota(jnp.int32, (8, 128), 0)
    lane8 = lax.broadcasted_iota(jnp.int32, (8, 128), 1)
    row = lax.broadcasted_iota(jnp.int32, (128, 128), 0)
    col = lax.broadcasted_iota(jnp.int32, (128, 128), 1)
    before = (row < col).astype(F32).astype(BF16)
    pick = (lax.broadcasted_iota(jnp.int32, (16, 128), 0) == (lax.broadcasted_iota(jnp.int32, (16, 128), 1) & 15))
    pick = pick.astype(F32).astype(BF16)
    ll = llist[...]
    mine = sub8 == (lane8 >> 4)

    def flat(v):
        w = jnp.dot(v.astype(F32).astype(BF16), pick, preferred_element_type=F32)
        return jnp.sum(jnp.where(mine, w, 0.0), axis=0, keepdims=True).astype(jnp.int32)

    upper = flat(ll >> 6) & 7
    lower = flat(ll & 63)
    row16[...] = jnp.zeros((8, 128), jnp.int32)
    row16[0:1, 0:16] = tlist[...]
    tl = row16[0:1, :]
    odd = odd_group() == 1
    leaf_u = jnp.where(odd, lower >> 3, upper)
    leaf_v = jnp.where(odd, upper, lower >> 3)
    top_u = jnp.where(odd, tl & 7, (tl >> 3) & 7)
    top_v = jnp.where(odd, (tl >> 3) & 7, tl & 7)
    leaf_hit = leaf_v == sub8
    top_hit = (top_v == sub8) & (lane < 16)
    leaf_one = leaf_hit.astype(F32)
    top_one = top_hit.astype(F32)
    leaf_pos = jnp.dot(leaf_one.astype(BF16), before, preferred_element_type=F32)
    top_pos = jnp.dot(top_one.astype(BF16), before, preferred_element_type=F32) + 16.0
    leaf_n = jnp.sum(leaf_one, axis=1, keepdims=True)
    top_n = jnp.sum(top_one, axis=1, keepdims=True)
    leaf_pos = jnp.where(leaf_hit, leaf_pos, -1.0)
    top_pos = jnp.where(top_hit, top_pos, -1.0)
    local = (lower & 7) + leaf_u * 8
    codes = jnp.where(sub8 == 0, lane >> 4, jnp.where(sub8 == 1, local, 0)).astype(F32).astype(BF16)
    tcodes = jnp.where(sub8 == 0, (tl >> 6) * 8 + top_u, 0).astype(F32).astype(BF16)
    rowf = row.astype(F32)
    for c in copies[2:6]:
        c.wait()
    for d in range(8):
        for c in range(3):
            m0[d, 8 * c : 8 * c + 8, :] = skel[c]
            m0[d, 24 + c : 25 + c, :] = cpts[c]
        m0[d, 29:32, :] = jnp.zeros((3, 128), F32)
        oh = (leaf_pos[d : d + 1] == rowf).astype(F32).astype(BF16)
        got = lax.dot_general(codes, oh, (((1,), (1,)), ((), ())), preferred_element_type=F32)
        m0[d, 27:28, :] = got[0:1] * 128.0 + got[1:2]
        oh = (top_pos[d : d + 1] == rowf).astype(F32).astype(BF16)
        got = lax.dot_general(tcodes, oh, (((1,), (1,)), ((), ())), preferred_element_type=F32)[0:1]
        got = got + jnp.where(lane == 0, leaf_n[d : d + 1], 0.0) + jnp.where(lane == 1, top_n[d : d + 1], 0.0)
        m0[d, 28:29, :] = got
    for slab, start in ((first, 0), (last, OWN - REACH)):
        for i in range(REACH):
            slab[8 * i : 8 * i + 8, :] = chg[start + i]
        for c in range(3):
            slab[32 + 4 * c : 36 + 4 * c, :] = pts[c, start : start + REACH, :]
        slab[44:48, :] = jnp.zeros((4, 256), F32)
    outs = fetch(((first, first_h), (last, last_h)), sems, 8)
    m1[96:104, :] = jnp.zeros((8, 128), F32)
    for c in range(3):
        m1[64 + 8 * c : 72 + 8 * c, :] = skel[c]
        m1[96 + c : 97 + c, :] = cpts[c]
    copies[6].wait()
    own = [dot3(chg[l], up[l], True) for l in range(OWN)]
    for l in range(OWN):
        m1[8 * l : 8 * l + 8, :] = own[l]
    copies[7].wait()
    total = dot3(own[0], utm[0], True)
    for l in range(1, OWN):
        total = total + dot3(own[l], utm[l], True)
    m1[88:96, :] = total
    for d in range(8):
        m0[d, 32:40, :] = total
    outs += fetch([(m0, m0_h)] + [(m1, m1_h.at[d]) for d in range(8)], sems, 10)
    for c in outs:
        c.wait()


def pack(*args):
    sd = jax.ShapeDtypeStruct
    shapes = [(8, 40, 128), (104, 128), (48, 256), (48, 256)]
    return pl.pallas_call(
        pack_kernel,
        in_specs=[HBM] * 8,
        out_specs=[HBM] * 4,
        out_shape=[sd((8, 40, 128), F32), sd((8, 104, 128), F32), sd((48, 256), F32), sd((48, 256), F32)],
        scratch_shapes=[pltpu.VMEM(a.shape, a.dtype) for a in args]
        + [pltpu.VMEM(s, F32) for s in shapes]
        + [pltpu.VMEM((8, 128), jnp.int32), pltpu.SemaphoreType.DMA((19,))],
        compiler_params=WIDE,
        name="pack",
    )(*args)


def near_blocks(ids, flat, base, first):
    pos = jnp.int32(0)
    seen = jnp.int32(0)
    for l in range(OWN):
        for n in range(NBR):
            ident = ids[l, n]
            e = ident - base
            flat[pos] = l * 32 + e
            own = (e >= REACH) & (e < REACH + OWN)
            take = own & (seen < FIRST_OWN)
            if not first:
                take = (ident >= 0) & jnp.logical_not(take)
            seen = seen + own.astype(jnp.int32)
            pos = pos + take.astype(jnp.int32)
    for u in range(CHUNK):
        flat[pos + u] = (OWN - 1) * 32 + NEAR_DUMMY
    return pos


def near_setup(sources, leaves, xyz, vals_of, fs, ft, vals, ts, tl):
    s0, s1, t0, t1, t2 = dense_features(xyz)
    load0, load1 = spread(s0, ts.at[0]), spread(s1, tl)
    for e in sources:
        a, b = load0(e), load1(e)
        fs[e] = jnp.concatenate([a, b, a, b], 0).T.astype(BF16)
        vals[e] = two_halves(vals_of(e))
    vals[NEAR_DUMMY] = jnp.zeros((16, 256), BF16)
    fs[NEAR_DUMMY] = jnp.zeros((256, FEAT), BF16)
    load0, load1, load2 = spread(t0, ts.at[1]), spread(t1, ts.at[2]), spread(t2, ts.at[3])
    for l in leaves:
        e = l + REACH
        one = load1(e)
        ft[l, 0:16, :] = jnp.concatenate([load0(e), load2(e)], 0).astype(BF16)
        ft[l, 16:32, :] = jnp.concatenate([one, one], 0).astype(BF16)


def near_run(count, flat, start, out, fs, ft, vals):
    out[...] = jnp.zeros_like(out) if start is None else start[...]

    def step(start, size):
        for u in range(size):
            code = flat[start + u]
            l, e = code >> 5, code & 31
            r = product(fs[e], ft[l], vals[e])
            out[l] += r[0:8] + r[8:16]

    in_chunks(count, CHUNK, step)


def near_base():
    return lax.axis_index("d") * OWN - REACH


def near_first_kernel(ids, pts, chg, out, flat, fs, ft, vals, xyz, ts, tl):
    count = near_blocks(ids, flat, near_base(), True)
    for c in range(3):
        xyz[c] = jnp.zeros((16, 256), F32)
        xyz[c, 4:12, :] = pts[c]
    own = range(REACH, REACH + OWN)
    near_setup(own, range(OWN), [xyz[0], xyz[1], xyz[2]], lambda e: chg[e - REACH], fs, ft, vals, ts, tl)
    near_run(count, flat, None, out, fs, ft, vals)


def near_rest_kernel(ids, pts, chg, before, after, start, out, flat, fs, ft, vals, xyz, ts, tl):
    count = near_blocks(ids, flat, near_base(), False)
    for c in range(3):
        xyz[c, 0:4, :] = before[32 + 4 * c : 36 + 4 * c, :]
        xyz[c, 4:12, :] = pts[c]
        xyz[c, 12:16, :] = after[32 + 4 * c : 36 + 4 * c, :]

    def vals_of(e):
        if e < REACH:
            return before[8 * e : 8 * e + 8, :]
        if e < REACH + OWN:
            return chg[e - REACH]
        return after[8 * (e - REACH - OWN) : 8 * (e - REACH - OWN) + 8, :]

    near_setup(range(OWN + 2 * REACH), range(OWN), [xyz[0], xyz[1], xyz[2]], vals_of, fs, ft, vals, ts, tl)
    near_run(count, flat, start, out, fs, ft, vals)


def near_part(kernel, *args):
    return pl.pallas_call(
        kernel,
        in_specs=[SMEM] + [VMEM] * (len(args) - 1),
        out_specs=VMEM,
        out_shape=jax.ShapeDtypeStruct((OWN, 8, 256), F32),
        scratch_shapes=[
            pltpu.SMEM((OWN * NBR + CHUNK + 8,), jnp.int32),
            pltpu.VMEM((17, 256, FEAT), BF16),
            pltpu.VMEM((OWN, FEAT, 256), BF16),
            pltpu.VMEM((17, 16, 256), BF16),
            pltpu.VMEM((3, 16, 256), F32),
            pltpu.VMEM((4, 2, 128, 128), F32),
            pltpu.VMEM((2, 128, 128), F32),
        ],
        cost_estimate=pl.CostEstimate(flops=2000000000, bytes_accessed=300000, transcendentals=4194304),
        compiler_params=PARAMS,
        name="near",
    )(*args)


def prepare_sources(i, xyz, t0, t1, feat):
    s0, s1, _, _, _ = dense_features(xyz)
    s0 = spread(s0, t0)
    s1 = spread(s1, t1)
    for l in range(8):
        feat[8 * i + l, 0:8, :] = s0(l)
        feat[8 * i + l, 8:16, :] = s1(l)


def prepare_targets(i, xyz, tmp, ft):
    _, _, t0, t1, t2 = dense_features(xyz)
    load0, load1, load2 = spread(t0, tmp.at[0]), spread(t1, tmp.at[1]), spread(t2, tmp.at[2])
    for l in range(8):
        one = load1(l)
        ft[8 * i + l, 0:16, :] = jnp.concatenate([load0(l), load2(l)], 0).astype(BF16)
        ft[8 * i + l, 16:32, :] = jnp.concatenate([one, one], 0).astype(BF16)


def flatten(req, flat, row, start, slot):
    off = 0
    for d in range(8):
        n = req[d, 1, slot]

        def copy(j, carry, d=d, off=off):
            for u in range(8):
                flat[off + j * 8 + u] = req[d, row, start + j * 8 + u] + d * (1024 if row == 0 else 128)
            return carry

        lax.fori_loop(0, (n + 7) // 8, copy, 0)
        off = off + n
    for u in range(2 * PAIRS):
        flat[off + u] = DUMMY
    return off


def interact(total, flat, fs, ft, vals, add):
    zero = jnp.zeros((FEAT, 128), BF16)

    def step(start, size):
        for u in range(size // 2):
            ca = flat[start + 2 * u]
            cb = flat[start + 2 * u + 1]
            ta, sa = ca >> 7, ca & 127
            tb, sb = cb >> 7, cb & 127
            fa = ft[ta]
            fb = ft[tb]
            tgt = jnp.concatenate([jnp.concatenate([fa, zero], 1), jnp.concatenate([zero, fb], 1)], 0)
            ra, rb = fs[sa], fs[sb]
            src = jnp.concatenate([ra, ra, rb, rb], 0).T.astype(BF16)
            r = product(src, tgt, jnp.concatenate([vals[sa], vals[sb]], 0))
            add(ta, r[0:8, 0:128] + r[8:16, 0:128])
            add(tb, r[16:24, 128:256] + r[24:32, 128:256])

    in_chunks(total, 2 * PAIRS, step)


def clear_dummy(fs, vals):
    fs[DUMMY] = jnp.zeros((16, 128), F32)
    vals[DUMMY] = jnp.zeros((16, 128), BF16)


def far_prep_kernel(req, tgt, ft, ftop, leaf_flat, top_flat, counts, tmp):
    for d in range(8):
        prepare_targets(d, [tgt[40 * d + 8 * c : 40 * d + 8 * c + 8, :] for c in range(3)], tmp.at[d], ft)
    prepare_targets(0, [tgt[pl.ds(24 + c, 8, stride=40), :] for c in range(3)], tmp.at[8], ftop)
    counts[0] = flatten(req, leaf_flat, 0, 0, 0)
    counts[1] = flatten(req, top_flat, 1, 16, 1)


def far_prep(req, tgt):
    sd = jax.ShapeDtypeStruct
    return pl.pallas_call(
        far_prep_kernel,
        in_specs=[SMEM, VMEM],
        out_specs=[VMEM, VMEM, SMEM, SMEM, SMEM],
        out_shape=[
            sd((64, FEAT, 128), BF16),
            sd((8, FEAT, 128), BF16),
            sd((1024 + 64,), jnp.int32),
            sd((256,), jnp.int32),
            sd((2,), jnp.int32),
        ],
        scratch_shapes=[pltpu.VMEM((9, 3, 1, 64, 128), F32)],
        cost_estimate=pl.CostEstimate(flops=100000000, bytes_accessed=900000, transcendentals=0),
        compiler_params=PARAMS,
        name="far_prep",
    )(req, tgt.reshape(320, 128))


def far_leaf_kernel(counts, flat, src, ft, out, fs, vals, t0, t1):
    for y in range(8):
        prepare_sources(y, [src[y, 64 + 8 * c : 72 + 8 * c, :] for c in range(3)], t0.at[y], t1.at[y], fs)
        for l in range(OWN):
            vals[8 * y + l] = two_halves(src[y, 8 * l : 8 * l + 8, :])
    clear_dummy(fs, vals)
    out[...] = jnp.zeros_like(out)

    def add(t, v):
        out[t >> 3, t & 7] += v

    interact(counts[0], flat, fs, ft, vals, add)


FAR_SCRATCH = [
    pltpu.VMEM((65, 16, 128), F32),
    pltpu.VMEM((65, 16, 128), BF16),
    pltpu.VMEM((8, 1, 64, 128), F32),
    pltpu.VMEM((8, 1, 64, 128), F32),
]


def far_leaf(counts, flat, src, ft):
    return pl.pallas_call(
        far_leaf_kernel,
        in_specs=[SMEM, SMEM, VMEM, VMEM],
        out_specs=VMEM,
        out_shape=jax.ShapeDtypeStruct((8, 9, 8, 128), F32),
        scratch_shapes=FAR_SCRATCH,
        cost_estimate=pl.CostEstimate(flops=2097152000, bytes_accessed=900000, transcendentals=4194304),
        compiler_params=PARAMS,
        name="far_leaf",
    )(counts, flat, src, ft)


def cells_kernel(along_u, along_v, out, slab):
    for y in range(8):
        slab[0, 8 * y : 8 * y + 8, :] = along_u[y, 88:96, :]
        slab[1, 8 * y : 8 * y + 8, :] = along_v[y, 32:40, :]
        for c in range(3):
            slab[0, 64 + 8 * c + y : 65 + 8 * c + y, :] = along_u[y, 96 + c : 97 + c, :]
            slab[1, 64 + 8 * c + y : 65 + 8 * c + y, :] = along_v[y, 24 + c : 25 + c, :]
    odd = odd_group()
    for d in range(8):
        out[d] = slab[(d % 2) ^ odd]


def cells_message(along_u, along_v):
    return pl.pallas_call(
        cells_kernel,
        in_specs=[VMEM] * 2,
        out_specs=VMEM,
        out_shape=jax.ShapeDtypeStruct((8, 88, 128), F32),
        scratch_shapes=[pltpu.VMEM((2, 88, 128), F32)],
        compiler_params=PARAMS,
        name="cells",
    )(along_u, along_v)


def far_top_kernel(counts, flat, src, ft, part, out, fs, vals, t0, t1):
    for g in range(8):
        xyz = [src[g, 64 + 8 * c : 72 + 8 * c, :] for c in range(3)]
        prepare_sources(g, xyz, t0.at[g], t1.at[g], fs)
        for y in range(8):
            vals[8 * g + y] = two_halves(src[g, 8 * y : 8 * y + 8, :])
    clear_dummy(fs, vals)
    out[...] = part[...]

    def add(t, v):
        out[t, 8] += v

    interact(counts[1], flat, fs, ft, vals, add)


def far_top(counts, flat, src, ft, part):
    return pl.pallas_call(
        far_top_kernel,
        in_specs=[SMEM, SMEM, VMEM, VMEM, VMEM],
        out_specs=VMEM,
        out_shape=jax.ShapeDtypeStruct((8, 9, 8, 128), F32),
        scratch_shapes=FAR_SCRATCH,
        compiler_params=PARAMS,
        name="far_top",
    )(counts, flat, src, ft, part)


def final_kernel(got, utm, up, near, out):
    tot = got[0]
    for d in range(1, 8):
        tot = tot + got[d]
    cell = tot[8]
    for l in range(OWN):
        incoming = tot[l] + dot3(cell, utm[l])
        out[l] = near[l] + dot3(incoming, up[l])


def final(got, utm, up, near):
    return pl.pallas_call(
        final_kernel,
        in_specs=[VMEM] * 4,
        out_specs=VMEM,
        out_shape=jax.ShapeDtypeStruct((8, 8, 256), F32),
        compiler_params=PARAMS,
        name="final",
    )(got, utm, up, near)


def device(g, u, v):
    return g * 64 + (v * 8 + u if g % 2 else u * 8 + v)


def body(points, charges, up_op, skel_pts, utm, cell_pts, near_list, leaf_list, top_list):
    r = range(8)
    along_u = [[device(g, u, v) for u in r] for g in r for v in r]
    along_v = [[device(g, u, v) for v in r] for g in r for u in r]
    along_g = [[g * 64 + i for g in r] for i in range(64)]

    def exchange(x, groups):
        return lax.all_to_all(x, "d", 0, 0, axis_index_groups=groups, tiled=True)

    pts = jnp.transpose(points, (1, 0, 2))
    skel = jnp.transpose(skel_pts, (1, 0, 2))
    cpts = jnp.transpose(cell_pts, (1, 0, 2))
    count = lax.axis_size("d")
    up = [(i, i + 1) for i in range(count - 1)]
    down = [(i + 1, i) for i in range(count - 1)]
    m0, m1, first, last = pack(pts, charges, skel, cpts, leaf_list, top_list, up_op, utm)
    m1, charges1 = lax.optimization_barrier((m1, charges))
    got1 = exchange(m1, along_u)
    before = lax.ppermute(last, "d", up)
    near0 = near_part(near_first_kernel, near_list, pts, charges1)
    got1, before, near0, m0, first = lax.optimization_barrier((got1, before, near0, m0, first))
    got0 = exchange(m0, along_v)
    after = lax.ppermute(first, "d", down)
    got0, after = lax.optimization_barrier((got0, after))
    cells, got0 = lax.optimization_barrier((cells_message(got1, got0), got0))
    gotg = exchange(cells, along_g)
    req = got0[:, 27:29, :].astype(jnp.int32)
    ft, ftop, leaf_flat, top_flat, counts = far_prep(req, got0)
    part = far_leaf(counts, leaf_flat, got1, ft)
    part = far_top(counts, top_flat, gotg, ftop, part)
    part, after = lax.optimization_barrier((part, after))
    gotr = exchange(part, along_v)
    near = near_part(near_rest_kernel, near_list, pts, charges, before, after, near0)
    return final(gotr, utm, up_op, near)


def solution(mesh):
    line = Mesh(mesh.devices.reshape(-1), ("d",))
    specs = tuple(P("d", *([None] * k)) for k in (2, 2, 2, 2, 2, 2, 1, 1, 1))
    return jax.shard_map(body, mesh=line, in_specs=specs, out_specs=P("d", None, None), check_vma=False)
```
